32 devices in a mesh: dp: 4 (over y, core), seq: 8 (over z, x).
Axes of the slice: x: 2, y: 2, z: 4, core: 2. Of those that a mesh axis runs over, the one named last changes fastest.
Arguments:
- tokens: bfloat16 [2, 4, 4096, 2048], P(None, 'dp', 'seq'), may hold values from -6 to 6
- segment_ids: int32 [2, 4, 4096], P(None, 'dp'), may hold values from 0 to 3, as said below
- w_qkv: bfloat16 [2048, 6144], P(('dp', 'seq')), may hold values from -0.125 to 0.125
- w_out: bfloat16 [2048, 2048], P(('dp', 'seq')), may hold values from -0.5 to 0.5
- w_gate_up: bfloat16 [2048, 11008], P(('dp', 'seq')), may hold values from -0.125 to 0.125
- w_down: bfloat16 [5504, 2048], P(('dp', 'seq')), may hold values from -0.078125 to 0.078125
- gain_attn: bfloat16 [2048], P(('dp', 'seq')), may hold values from 0.5 to 1.5
- gain_mlp: bfloat16 [2048], P(('dp', 'seq')), may hold values from 0.5 to 1.5
- cotangent: bfloat16 [2, 4, 4096, 2048], P(None, 'dp', 'seq'), may hold values from -6 to 6
Outputs:
- layer_out: bfloat16 [2, 4, 4096, 2048], P(None, 'dp', 'seq')
- grad_tokens: float32 [2, 4, 4096, 2048], P(None, 'dp', 'seq')
- grad_w_qkv: float32 [2048, 6144], P(('dp', 'seq'))
- grad_w_out: float32 [2048, 2048], P(('dp', 'seq'))
- grad_w_gate_up: float32 [2048, 11008], P(('dp', 'seq'))
- grad_w_down: float32 [5504, 2048], P(('dp', 'seq'))
- grad_gain_attn: float32 [2048], P(('dp', 'seq'))
- grad_gain_mlp: float32 [2048], P(('dp', 'seq'))
The draws below stay inside these ranges and needn't reach their ends.
Inputs may be any that keep to these rules, and one draw needn't show every extreme that they name: `segment_ids`: along each sequence the ids start at 0 and never fall; every document but the last of a sequence has 16 tokens or more; for each of the 4 sequence slots, one of the 2 micro-batches, drawn from the seed, holds a single document over all 4096 tokens.
All inputs are finite; a program needn't handle non-finite values.
Results may differ from the reference program's by a relative error of at most 0.013.
Values may be sent and summed in bfloat16 or wider, within the bound.
No kernel may reach another device: no remote copies, remote signals or barrier semaphores. Data moves between devices by JAX's collectives and lax.ppermute only.
A program may use at most 832 MiB of HBM per device.

```python
import math
import jax
import jax.numpy as jnp
from jax import lax

D = 2048
H = 16
HD = 128
FF = 5504
WINDOW = 2048
MB = 2
ROWS = 512
SEQLEN = 4096
SEQS = 4
N_SEQ = 8


def draw_segment_ids(key, part):
    key_exp, key_extra, key_pick, key_short = jax.random.split(key, 4)
    doc_count = SEQLEN // 16 + 1
    exponents = jax.random.randint(key_exp, (MB, SEQS, doc_count), 4, 12)
    short_exp = jax.random.randint(key_short, (MB, SEQS, doc_count), 4, 8)
    first_docs = jnp.arange(doc_count, dtype=jnp.int32)[None, None, :] < 3
    exponents = jnp.where(first_docs, short_exp, exponents)
    extras = jax.random.randint(key_extra, (MB, SEQS, doc_count), 0, 16)
    lengths = jnp.left_shift(jnp.ones_like(exponents), exponents) + extras
    doc_ends = jnp.cumsum(lengths, axis=-1)
    positions = jnp.arange(SEQLEN, dtype=jnp.int32)
    segment_vals = jnp.sum((doc_ends[:, :, None, :] <= positions[None, None, :, None]).astype(jnp.int32), axis=-1)
    segment_vals = jnp.minimum(segment_vals, 3)
    whole_pick = jax.random.randint(key_pick, (SEQS,), 0, MB)
    single_doc = jnp.arange(MB, dtype=jnp.int32)[:, None] == whole_pick[None, :]
    return jnp.where(single_doc[:, :, None], 0, segment_vals).astype(jnp.int32)


def level_of(stream_key, shape, cuts, least, top_value):
    def one(dim, blocks):
        draws = jax.random.uniform(jax.random.fold_in(jax.random.fold_in(stream_key, 6), dim), (blocks,), jnp.float32, least / len(cuts), top_value / len(cuts))
        return jnp.repeat(jnp.exp(draws), shape[dim] // blocks).reshape((-1,) + (1,) * (len(shape) - dim - 1))

    level = one(*cuts[0])
    for cut in cuts[1:]:
        level = level * one(*cut)
    return level


def bell_draw(rng, extent, scale, reach, pieces=(), kind=jnp.bfloat16):
    loudness = level_of(rng, extent, pieces, -0.22, 0.18) if pieces else 1.0
    result = jax.random.normal(rng, extent, jnp.float32) * scale * loudness
    return jnp.minimum(jnp.maximum(result, -reach), reach).astype(kind)


def setup_inputs(seed: int = 0) -> dict:
    keys = jax.random.split(jax.random.key(seed), 10)
    return {
        "tokens": bell_draw(keys[0], (MB, SEQS, SEQLEN, D), 1.0, 6.0, ((1, 4), (2, 8))),
        "segment_ids": draw_segment_ids(jax.random.fold_in(keys[9], 71), 0),
        "w_qkv": bell_draw(keys[2], (D, 3 * D), D ** -0.5, 0.125, ((0, 32),)),
        "w_out": bell_draw(keys[3], (D, D), (D // 16) ** -0.5, 0.5, ((0, 32),)),
        "w_gate_up": bell_draw(keys[4], (D, 2 * FF), D ** -0.5, 0.125, ((0, 32),)),
        "w_down": bell_draw(keys[5], (FF, D), FF ** -0.5, 0.078125, ((0, 32),)),
        "gain_attn": jnp.clip(1.0 + 0.1 * jax.random.normal(keys[6], (D,), jnp.float32), 0.5, 1.5).astype(jnp.bfloat16),
        "gain_mlp": jnp.clip(1.0 + 0.1 * jax.random.normal(keys[7], (D,), jnp.float32), 0.5, 1.5).astype(jnp.bfloat16),
        "cotangent": bell_draw(keys[8], (MB, SEQS, SEQLEN, D), 1.0, 6.0, ((1, 4), (2, 8))),
    }


epsilon = 1e-05
masked_score = -1e+30

@jax.custom_vjp
def low(v):
    return lax.optimization_barrier(v.astype(jnp.bfloat16)).astype(jnp.float32)

@jax.custom_vjp
def low_back(v):
    return v

def low_keep(v):
    return (low(v), None)

def low_pass(kept, grad):
    return (grad,)

def back_keep(v):
    return (v, None)

def back_low(kept, grad):
    return (low(grad),)
low.defvjp(low_keep, low_pass)
low_back.defvjp(back_keep, back_low)

def matmul(left, right):
    return jnp.dot(left, right, precision=lax.Precision.HIGHEST, preferred_element_type=jnp.float32)

def rms_norm(values, gain_vector):
    row_scale = lax.rsqrt(lax.optimization_barrier(jnp.mean(values * values, axis=-1, keepdims=True)) + epsilon)
    return values * row_scale * gain_vector

def attend_block(block_no, queries, key_pad, value_pad, segment_row, segment_pad, reach_blocks):
    key_span = (reach_blocks + 1) * ROWS
    start_row = (block_no * ROWS).astype(jnp.int32)
    block_queries = lax.dynamic_slice_in_dim(queries, start_row, ROWS, 0)
    block_keys = lax.dynamic_slice_in_dim(key_pad, start_row, key_span, 0)
    block_values = lax.dynamic_slice_in_dim(value_pad, start_row, key_span, 0)
    query_seg = lax.dynamic_slice_in_dim(segment_row, start_row, ROWS, 0)
    key_seg = lax.dynamic_slice_in_dim(segment_pad, start_row, key_span, 0)
    query_pos = start_row + jnp.arange(ROWS, dtype=jnp.int32)
    key_pos = start_row - reach_blocks * ROWS + jnp.arange(key_span, dtype=jnp.int32)
    live_pairs = (query_seg[:, None] == key_seg[None, :]) & (key_pos[None, :] <= query_pos[:, None])
    live_pairs = live_pairs & (query_pos[:, None] - key_pos[None, :] < WINDOW) & (key_pos[None, :] >= 0)
    scores = jnp.einsum('qhd,khd->hqk', block_queries, block_keys, precision=lax.Precision.HIGHEST) * (1.0 / math.sqrt(HD))
    scores = low_back(scores)
    scores = jnp.where(live_pairs[None], scores, masked_score)
    row_max = lax.optimization_barrier(jnp.max(scores, axis=-1, keepdims=True))
    exp_scores = jnp.exp(scores - row_max)
    attn_probs = low(exp_scores / lax.optimization_barrier(jnp.sum(exp_scores, axis=-1, keepdims=True)))
    return jnp.einsum('hqk,khd->qhd', attn_probs, block_values, precision=lax.Precision.HIGHEST)

def layer_sequence(tokens_row, segment_row, full_qkv, full_out, full_gate_up, full_down, full_gain_attn, full_gain_mlp):
    reach_blocks = min(WINDOW // ROWS, N_SEQ - 1)
    pad_rows = reach_blocks * ROWS
    h_attn = low(rms_norm(tokens_row, full_gain_attn))
    qkv_rows = low(low_back(matmul(h_attn, full_qkv)))
    queries = qkv_rows[:, :D].reshape(SEQLEN, H, HD)
    zeros_pad = jnp.zeros((pad_rows, H, HD), jnp.float32)
    key_pad = jnp.concatenate([zeros_pad, qkv_rows[:, D:2 * D].reshape(SEQLEN, H, HD)], axis=0)
    value_pad = jnp.concatenate([zeros_pad, qkv_rows[:, 2 * D:].reshape(SEQLEN, H, HD)], axis=0)
    segment_pad = jnp.concatenate([jnp.full((pad_rows,), -1, jnp.int32), segment_row.astype(jnp.int32)], axis=0)

    def one_block(block_no):
        return attend_block(block_no, queries, key_pad, value_pad, segment_row.astype(jnp.int32), segment_pad, reach_blocks)
    mixed = lax.map(jax.checkpoint(one_block), jnp.arange(N_SEQ, dtype=jnp.int32))
    attended = low(low_back(mixed.reshape(SEQLEN, D)))
    mid_stream = tokens_row + low_back(matmul(attended, full_out))
    h_mlp = low(rms_norm(mid_stream, full_gain_mlp))
    gate_up = low_back(matmul(h_mlp, full_gate_up))
    activated = low(jax.nn.silu(gate_up[:, :FF]) * gate_up[:, FF:])
    return mid_stream + low_back(matmul(activated, full_down))

def reference(tokens, segment_ids, w_qkv, w_out, w_gate_up, w_down, gain_attn, gain_mlp, cotangent):

    def forward(token_vals, full_qkv, full_out, full_gate_up, full_down, full_gain_attn, full_gain_mlp):
        flat_tokens = token_vals.reshape(MB * SEQS, SEQLEN, D)
        flat_segments = segment_ids.reshape(MB * SEQS, SEQLEN)

        def one_sequence(sequence_pair):
            return layer_sequence(sequence_pair[0], sequence_pair[1], full_qkv, full_out, full_gate_up, full_down, full_gain_attn, full_gain_mlp)
        results = lax.map(jax.checkpoint(one_sequence), (flat_tokens, flat_segments))
        return results.reshape(MB, SEQS, SEQLEN, D)
    floats = tuple((array_in.astype(jnp.float32) for array_in in (tokens, w_qkv, w_out, w_gate_up, w_down, gain_attn, gain_mlp)))
    layer_out, pullback = jax.vjp(forward, *floats)
    grads = pullback(cotangent.astype(jnp.float32))
    return (layer_out.astype(jnp.bfloat16), grads[0], grads[1], grads[2], grads[3], grads[4], grads[5], grads[6])
```

```python
import functools
import math

import jax
import jax.numpy as jnp
from jax import lax
from jax.experimental import pallas as pl
from jax.experimental.pallas import tpu as pltpu
from jax.sharding import PartitionSpec as P

D = 2048
H = 16
HD = 128
FF = 5504
WINDOW = 2048
MB = 2
TILE = 512

EPSILON = 1e-05
MASKED = -1e30
LOG2E = 1.4426950408889634
SCALE = 1.0 / math.sqrt(HD)

bf16 = jnp.bfloat16
f32 = jnp.float32


def digits_of(size):
    if size == 8:
        return [(1, 2), (2, 4)]
    if size == 32:
        return [(1, 4), (4, 2), (8, 4)]
    return [(1, size)] if size > 1 else []


def digit_index(axis, digit):
    stride, size = digit
    return lax.rem(lax.axis_index(axis) // stride, size)


def shift(block, axis, digit, distance):
    stride, size = digit
    total = lax.axis_size(axis)
    route = []
    for i in range(total):
        own = (i // stride) % size
        route.append((i, i + ((own + distance) % size - own) * stride))
    return lax.ppermute(block, axis, route)


def pick(array, index, dim):
    return lax.dynamic_index_in_dim(array, index, dim, keepdims=False)


def scatter_digit(parts, axis, digit, dim, out_type):
    own = digit_index(axis, digit)
    size = digit[1]
    got = []
    for distance in range(1, size):
        piece = pick(parts, lax.rem(own + distance, size), dim)
        got.append(shift(piece, axis, digit, distance))
    total = pick(parts, own, dim).astype(f32)
    for piece in got:
        total = total + piece.astype(f32)
    return total.astype(out_type)


def gather_small(block):
    for axis in ("seq", "dp"):
        for digit in digits_of(lax.axis_size(axis)) if axis == "seq" else [(1, 2), (2, lax.axis_size("dp") // 2)]:
            size = digit[1]
            if size == 1:
                continue
            own = digit_index(axis, digit)
            pieces = [block] + [shift(block, axis, digit, d) for d in range(1, size)]
            stacked = jnp.stack(pieces, axis=0)
            order = lax.rem(own - jnp.arange(size) + size, size)
            block = jnp.concatenate(
                [jnp.sum(jnp.where((order == t).reshape((size,) + (1,) * block.ndim), stacked, 0), axis=0) for t in range(size)],
                axis=-1,
            ).astype(block.dtype)
    return block


def scatter_small(terms):
    k = terms.shape[0]
    dp, seq = lax.axis_size("dp"), lax.axis_size("seq")
    terms = scatter_digit(terms.reshape(k, dp // 2, 2, -1), "dp", (1, 2), 2, f32)
    if dp > 2:
        terms = scatter_digit(terms, "dp", (2, dp // 2), 1, f32)
    else:
        terms = terms[:, 0]
    for digit in reversed(digits_of(seq)):
        terms = scatter_digit(terms.reshape(k, digit[1], -1), "seq", digit, 1, f32)
    return terms


def weight_grad(rows_side, cols_side, seq_first):
    tokens, row_total = rows_side.shape
    dp, seq = lax.axis_size("dp"), lax.axis_size("seq")
    ys = dp // 2
    own = row_total // (dp * seq)
    cols = cols_side.shape[1]
    slow = digits_of(seq)[::-1]
    core, height = (1, 2), (2, ys)
    c = digit_index("dp", core)
    if seq_first:
        fast = digits_of(seq)[0]
        first, first_axis, first_own = fast, "seq", digit_index("seq", fast)
        lhs = rows_side.reshape(tokens, ys, 2, seq // fast[1], fast[1], own)
        lhs = lhs.transpose(2, 4, 1, 3, 5, 0)
    else:
        first, first_axis, first_own = height, "dp", digit_index("dp", height)
        lhs = rows_side.reshape(tokens, ys, 2, seq, own)
        lhs = lhs.transpose(2, 1, 3, 4, 0)
    size = first[1]
    lhs = lhs.reshape(2, size, -1, tokens)

    def term(core_index, first_index):
        side = pick(pick(lhs, core_index, 0), first_index, 0)
        return jnp.dot(side, cols_side, preferred_element_type=f32)

    order = [lax.rem(first_own + d, size) for d in range(1, size)] + [first_own]
    from_core = [shift(term(1 - c, index).astype(bf16), "dp", core, 1) for index in order]
    sums = [term(c, index) + got.astype(f32) for index, got in zip(order, from_core)]
    total = sums[-1]
    for distance in range(1, size):
        total = total + shift(sums[distance - 1].astype(bf16), first_axis, first, distance).astype(f32)
    total = total.astype(bf16)
    if seq_first:
        rest = [(axis, digit) for axis, digit in [("dp", height)] + [("seq", d) for d in slow[:-1]]]
    else:
        rest = [("seq", d) for d in slow[-1:]] + [("seq", d) for d in slow[:-1]]
    if not seq_first:
        fast = slow[-1]
        total = total.reshape(seq // fast[1], fast[1], own, cols)
        total = scatter_digit(total, "seq", fast, 1, bf16 if len(slow) > 1 else f32)
        rest = [("seq", d) for d in slow[:-1]]
    for n, (axis, digit) in enumerate(rest):
        total = total.reshape(digit[1], -1, cols)
        total = scatter_digit(total, axis, digit, 0, f32 if n == len(rest) - 1 else bf16)
    return total.reshape(own, cols).astype(f32)


def dot_nt(a, b):
    return lax.dot_general(a, b, (((1,), (1,)), ((), ())), preferred_element_type=f32)


def dot_tn(a, b):
    return lax.dot_general(a, b, (((0,), (0,)), ((), ())), preferred_element_type=f32)


def dot_nn(a, b):
    return lax.dot_general(a, b, (((1,), (0,)), ((), ())), preferred_element_type=f32)


def forward_kernel(bounds, q_ref, k_ref, v_ref, lo_ref, o_ref, lse_ref, acc):
    i = pl.program_id(1)
    q = q_ref[...]
    lo = lo_ref[...]
    factor = SCALE * LOG2E

    def step(j, carry, masked, first=False):
        m, l = carry
        rows = pl.ds(pl.multiple_of(j * TILE, TILE), TILE)
        s = dot_nt(k_ref[rows, :], q) * factor
        if masked:
            key = j * TILE + lax.broadcasted_iota(jnp.int32, (TILE, TILE), 0)
            query = i * TILE + lax.broadcasted_iota(jnp.int32, (TILE, TILE), 1)
            s = jnp.where((key >= lo) & (key <= query), s, MASKED)
        new = jnp.maximum(m, jnp.max(s, axis=0, keepdims=True))
        p = jnp.exp2(s - new)
        old = jnp.exp2(m - new)
        acc[...] = acc[...] * old + dot_tn(v_ref[rows, :], p.astype(bf16))
        return new, l * old + jnp.sum(p, axis=0, keepdims=True)

    acc[...] = jnp.zeros_like(acc)
    carry = (jnp.full((1, TILE), MASKED, f32), jnp.zeros((1, TILE), f32))
    start = bounds[0, i]
    middle = bounds[1, i]
    carry = lax.fori_loop(start, middle, lambda j, c: step(j, c, True), carry)
    carry = lax.fori_loop(middle, i, lambda j, c: step(j, c, False), carry)
    m, l = step(i, carry, True)
    o_ref[...] = (acc[...] / l).T.astype(bf16)
    lse_ref[0] = m + jnp.log2(l)


def attend(qkv, bounds, low, heads):
    length = qkv.shape[0]
    blocks = length // TILE
    whole = lambda part: pl.BlockSpec((length, HD), lambda h, i, b: (0, part * heads + h))
    return pl.pallas_call(
        forward_kernel,
        grid_spec=pltpu.PrefetchScalarGridSpec(
            num_scalar_prefetch=1,
            grid=(heads, blocks),
            in_specs=[
                pl.BlockSpec((TILE, HD), lambda h, i, b: (i, h)),
                whole(1),
                whole(2),
                pl.BlockSpec((1, TILE), lambda h, i, b: (0, i)),
            ],
            out_specs=[
                pl.BlockSpec((TILE, HD), lambda h, i, b: (i, h)),
                pl.BlockSpec((1, 1, TILE), lambda h, i, b: (h, 0, i)),
            ],
            scratch_shapes=[pltpu.VMEM((HD, TILE), f32)],
        ),
        out_shape=[
            jax.ShapeDtypeStruct((length, heads * HD), bf16),
            jax.ShapeDtypeStruct((heads, 1, length), f32),
        ],
        compiler_params=pltpu.CompilerParams(vmem_limit_bytes=32 * 1024 * 1024),
        cost_estimate=pl.CostEstimate(
            flops=4 * heads * length * 1792 * HD,
            bytes_accessed=8 * heads * length * HD,
            transcendentals=heads * length * 1792,
        ),
        name="attend",
    )(bounds, qkv, qkv, qkv, low)


def backward_kernel(bounds, q_ref, k_ref, v_ref, do_ref, lse_ref, delta_ref, lo_ref, dq_ref, dk_ref, dv_ref, dq, dk, dv):
    j = pl.program_id(1)
    k = k_ref[...]
    v = v_ref[...]
    factor = SCALE * LOG2E

    def step(i, masked):
        rows = pl.ds(pl.multiple_of(i * TILE, TILE), TILE)
        q = q_ref[rows, :]
        do = do_ref[rows, :]
        s = dot_nt(k, q) * factor
        p = jnp.exp2(s - lse_ref[0, :, rows])
        if masked:
            key = j * TILE + lax.broadcasted_iota(jnp.int32, (TILE, TILE), 0)
            query = i * TILE + lax.broadcasted_iota(jnp.int32, (TILE, TILE), 1)
            p = jnp.where((key >= lo_ref[:, rows]) & (key <= query), p, 0.0)
        dp = dot_nt(v, do)
        ds = (p * (dp - delta_ref[0, :, rows])).astype(bf16)
        dv[...] += dot_nn(p.astype(bf16), do)
        dk[...] += dot_nn(ds, q)
        dq[rows, :] += dot_tn(ds, k)

    @pl.when(j == 0)
    def _():
        dq[...] = jnp.zeros_like(dq)

    dk[...] = jnp.zeros_like(dk)
    dv[...] = jnp.zeros_like(dv)
    step(j, True)
    middle = bounds[2, j]
    end = bounds[3, j]

    @pl.loop(j + 1, middle)
    def _(i):
        step(i, False)

    @pl.loop(middle, end)
    def _(i):
        step(i, True)

    own = pl.ds(pl.multiple_of(j * TILE, TILE), TILE)
    dq_ref[...] = (dq[own, :] * SCALE).astype(bf16)
    dk_ref[...] = (dk[...] * SCALE).astype(bf16)
    dv_ref[...] = dv[...].astype(bf16)


def attend_back(qkv, grad, lse, delta, bounds, low, heads):
    length = qkv.shape[0]
    blocks = length // TILE
    whole = pl.BlockSpec((length, HD), lambda h, j, b: (0, h))
    line = pl.BlockSpec((1, 1, length), lambda h, j, b: (h, 0, 0))
    block = lambda part: pl.BlockSpec((TILE, HD), lambda h, j, b: (j, part * heads + h))
    piece = jax.ShapeDtypeStruct((length, heads * HD), bf16)
    return pl.pallas_call(
        backward_kernel,
        grid_spec=pltpu.PrefetchScalarGridSpec(
            num_scalar_prefetch=1,
            grid=(heads, blocks),
            in_specs=[
                whole,
                block(1),
                block(2),
                whole,
                line,
                line,
                pl.BlockSpec((1, length), lambda h, j, b: (0, 0)),
            ],
            out_specs=[block(0)] * 3,
            scratch_shapes=[
                pltpu.VMEM((length, HD), f32),
                pltpu.VMEM((TILE, HD), f32),
                pltpu.VMEM((TILE, HD), f32),
            ],
        ),
        out_shape=[piece] * 3,
        compiler_params=pltpu.CompilerParams(vmem_limit_bytes=40 * 1024 * 1024),
        cost_estimate=pl.CostEstimate(
            flops=10 * heads * length * 1792 * HD,
            bytes_accessed=16 * heads * length * HD,
            transcendentals=heads * length * 1792,
        ),
        name="attend_back",
    )(bounds, qkv, qkv, qkv, grad, lse, delta, low)


def key_bounds(segments):
    length = segments.shape[0]
    blocks = length // TILE
    place = jnp.arange(length, dtype=jnp.int32)
    start = jnp.zeros_like(place)
    for value in range(1, 4):
        earlier = jnp.sum(segments < value, dtype=jnp.int32)
        start = jnp.where(segments == value, earlier, start)
    low = jnp.maximum(start, place - (WINDOW - 1))
    index = jnp.arange(blocks, dtype=jnp.int32)
    first = low[::TILE]
    last = low[TILE - 1 :: TILE]
    begin = first // TILE
    middle = jnp.clip((last + TILE - 1) // TILE, begin, index)
    full = (last[None, :] <= index[:, None] * TILE) & (index[None, :] > index[:, None])
    some = (first[None, :] < (index[:, None] + 1) * TILE) & (index[None, :] > index[:, None])
    back_middle = index + 1 + jnp.sum(full, axis=1, dtype=jnp.int32)
    back_end = index + 1 + jnp.sum(some, axis=1, dtype=jnp.int32)
    return low[None], jnp.stack([begin, middle, back_middle, back_end])


def to_heads(rows, micros, heads):
    parts = rows.shape[1] // D
    count = rows.shape[0] // micros
    split = rows.reshape(micros, count, parts, H // heads, heads * HD).transpose(0, 3, 1, 2, 4)
    split = split.reshape(micros * H // heads, count, parts * heads * HD)
    got = lax.all_to_all(split, "seq", 0, 0, tiled=True)
    return got.reshape(-1, parts * heads * HD)


def to_rows(whole, micros, heads):
    seq = lax.axis_size("seq")
    parts = whole.shape[1] // (heads * HD)
    got = lax.all_to_all(whole.reshape(seq, -1, parts * heads * HD), "seq", 0, 0, tiled=True)
    count = got.shape[1]
    got = got.reshape(micros, H // heads, count, parts, heads * HD).transpose(0, 2, 3, 1, 4)
    return got.reshape(micros * count, parts * D)


def norm_scale(values):
    return lax.rsqrt(jnp.mean(values * values, axis=-1, keepdims=True) + EPSILON)


def norm_backward(grad_in, values, row_scale, gain):
    normed = values * row_scale
    gain_grad = jnp.sum(grad_in * normed, axis=0)
    scaled = grad_in * gain
    inner = jnp.mean(scaled * normed, axis=-1, keepdims=True)
    return row_scale * (scaled - normed * inner), gain_grad


def nt(a, b):
    return jnp.einsum("re,de->rd", a, b, preferred_element_type=f32)


def shards(tokens, segment_ids, w_qkv, w_out, w_gate_up, w_down, gain_attn, gain_mlp, cotangent):
    rows = tokens.shape[2]
    seq = lax.axis_size("seq")
    gather = lambda w: lax.all_gather(w, ("dp", "seq"), axis=0, tiled=True)
    gains = gather_small(jnp.stack([gain_attn, gain_mlp])).astype(f32)
    gain_a, gain_m = gains[0], gains[1]
    full_qkv, full_out, full_gate_up, full_down = (gather(w) for w in (w_qkv, w_out, w_gate_up, w_down))

    micros = 1 if H % seq == 0 else MB
    groups = MB // micros
    heads = micros * H // seq
    x = tokens.reshape(MB * rows, D).astype(f32)
    cot = cotangent.reshape(MB * rows, D)
    scale_a = norm_scale(x)
    h_attn = (x * scale_a * gain_a).astype(bf16)

    saved = []
    attended_parts = []
    for g in range(groups):
        if micros == 1:
            segments = segment_ids[g, 0]
        else:
            segments = pick(segment_ids[:, 0], lax.axis_index("seq") * micros // seq, 0)
        low, bounds = key_bounds(segments)
        part = h_attn[g * micros * rows : (g + 1) * micros * rows]
        qkv_rows = jnp.dot(part, full_qkv, preferred_element_type=f32).astype(bf16)
        qkv = to_heads(qkv_rows, micros, heads)
        mixed, lse = attend(qkv, bounds, low, heads)
        saved.append((qkv, low, bounds, mixed, lse))
        attended_parts.append(to_rows(mixed, micros, heads))
    attended = jnp.concatenate(attended_parts, axis=0)

    mid = x + jnp.dot(attended, full_out, preferred_element_type=f32)
    scale_m = norm_scale(mid)
    h_mlp = (mid * scale_m * gain_m).astype(bf16)
    gate_up = jnp.dot(h_mlp, full_gate_up, preferred_element_type=f32)
    gate, up = gate_up[:, :FF], gate_up[:, FF:]
    sig = jax.nn.sigmoid(gate)
    act = (gate * sig * up).astype(bf16)
    layer_out = (mid + jnp.dot(act, full_down, preferred_element_type=f32)).astype(bf16)

    grad_act = nt(cot, full_down)
    half_d = D // 2
    down_terms = [weight_grad(act, cot[:, :half_d], False), weight_grad(act, cot[:, half_d:], True)]
    grad_gate = (grad_act * up * sig * (1.0 + gate * (1.0 - sig))).astype(bf16)
    grad_up = (grad_act * (gate * sig)).astype(bf16)
    grad_gate_up = jnp.concatenate([grad_gate, grad_up], axis=-1)
    gate_up_terms = [weight_grad(h_mlp, grad_gate, False), weight_grad(h_mlp, grad_up, True)]
    grad_h_mlp = nt(grad_gate_up, full_gate_up)
    grad_mid_norm, gain_m_grad = norm_backward(grad_h_mlp, mid, scale_m, gain_m)
    grad_mid = cot.astype(f32) + grad_mid_norm
    grad_branch = grad_mid.astype(bf16)
    grad_attended = nt(grad_branch, full_out).astype(bf16)
    out_terms = [
        weight_grad(attended, grad_branch[:, :half_d], False),
        weight_grad(attended, grad_branch[:, half_d:], True),
    ]

    grad_qkv_parts = []
    for g in range(groups):
        qkv, low, bounds, mixed, lse = saved[g]
        grad = to_heads(grad_attended[g * micros * rows : (g + 1) * micros * rows], micros, heads)
        product = grad.astype(f32) * mixed.astype(f32)
        delta = jnp.sum(product.reshape(-1, heads, HD), axis=-1).T.reshape(heads, 1, -1)
        pieces = attend_back(qkv, grad, lse, delta, bounds, low, heads)
        grad_qkv_parts.append(to_rows(jnp.concatenate(pieces, axis=-1), micros, heads))
    grad_qkv = jnp.concatenate(grad_qkv_parts, axis=0)
    half_q = 3 * D // 2
    qkv_terms = [weight_grad(h_attn, grad_qkv[:, :half_q], False), weight_grad(h_attn, grad_qkv[:, half_q:], True)]
    grad_h_attn = nt(grad_qkv, full_qkv)
    grad_tok_norm, gain_a_grad = norm_backward(grad_h_attn, x, scale_a, gain_a)
    grad_tokens = grad_mid + grad_tok_norm
    gain_grads = scatter_small(jnp.stack([gain_a_grad, gain_m_grad]))

    return (
        layer_out.reshape(MB, 1, rows, D),
        grad_tokens.reshape(MB, 1, rows, D),
        jnp.concatenate(qkv_terms, axis=-1),
        jnp.concatenate(out_terms, axis=-1),
        jnp.concatenate(gate_up_terms, axis=-1),
        jnp.concatenate(down_terms, axis=-1),
        gain_grads[0],
        gain_grads[1],
    )


def solution(mesh):
    by_rows = P(("dp", "seq"), None)
    by_tokens = P(None, "dp", "seq", None)
    vector = P(("dp", "seq"))
    return jax.shard_map(
        shards,
        mesh=mesh,
        in_specs=(by_tokens, P(None, "dp", None), by_rows, by_rows, by_rows, by_rows, vector, vector, by_tokens),
        out_specs=(by_tokens, by_tokens, by_rows, by_rows, by_rows, by_rows, vector, vector),
        check_vma=False,
    )
```

```python
import functools
import math

import jax
import jax.numpy as jnp
from jax import lax
from jax.experimental import pallas as pl
from jax.experimental.pallas import tpu as pltpu
from jax.sharding import PartitionSpec as P

D = 2048
H = 16
HD = 128
FF = 5504
WINDOW = 2048
MB = 2
TILE = 512

EPSILON = 1e-05
MASKED = -1e30
LOG2E = 1.4426950408889634
SCALE = 1.0 / math.sqrt(HD)

bf16 = jnp.bfloat16
f32 = jnp.float32


def digits_of(axis):
    size = lax.axis_size(axis)
    return [(axis, 1 << bit) for bit in reversed(range(size.bit_length() - 1))]


def digit_index(digit):
    axis, stride = digit
    return lax.rem(lax.axis_index(axis) // stride, 2)


def swap(block, digit):
    axis, stride = digit
    return lax.ppermute(block, axis, [(i, i ^ stride) for i in range(lax.axis_size(axis))])


def pick(array, index, dim):
    return lax.dynamic_index_in_dim(array, index, dim, keepdims=False)


def scatter_digit(parts, digit, dim, out_type):
    own = digit_index(digit)
    got = swap(pick(parts, 1 - own, dim), digit)
    return (pick(parts, own, dim).astype(f32) + got.astype(f32)).astype(out_type)


def gather_small(block):
    for digit in reversed(digits_of("dp") + digits_of("seq")):
        got = swap(block, digit)
        low = digit_index(digit) == 0
        block = jnp.concatenate([jnp.where(low, block, got), jnp.where(low, got, block)], axis=-1)
    return block


def scatter_small(terms):
    k = terms.shape[0]
    for digit in digits_of("dp") + digits_of("seq"):
        terms = scatter_digit(terms.reshape(k, 2, -1), digit, 1, f32)
    return terms


SLOTS = 8


def place_kernel(count, rows, widths, target, *refs):
    sources, outs = refs[: -3 - len(widths)], refs[-3 - len(widths) : -3]
    held, in_sems, out_sems = refs[-3:]
    per = sources[0].shape[0] // rows

    def read(n):
        source = sources[n // per].at[pl.ds((n % per) * rows, rows), :]
        return pltpu.make_async_copy(source, held.at[n % SLOTS], in_sems.at[n % SLOTS])

    def writes(n):
        start, left = pl.multiple_of(target[n], 16), 0
        copies = []
        for k, width in enumerate(widths):
            source = held.at[n % SLOTS, :, pl.ds(left, width)]
            copies.append(pltpu.make_async_copy(source, outs[k].at[pl.ds(start, rows), :], out_sems.at[n % SLOTS, k]))
            left += width
        return copies

    lag = SLOTS // 2
    for n in range(min(lag, count)):
        read(n).start()
    for n in range(count):
        if n >= lag:
            for copy in writes(n - lag):
                copy.wait()
        if n + lag < count:
            read(n + lag).start()
        read(n).wait()
        for copy in writes(n):
            copy.start()
    for n in range(max(count - lag, 0), count):
        for copy in writes(n):
            copy.wait()


class Gather:
    def __init__(self, blocks, seq_first):
        self.rows, self.widths = blocks[0].shape[0], [b.shape[1] for b in blocks]
        fast, height = digits_of("seq")[-1:], digits_of("dp")[:-1]
        self.far = digits_of("seq")[:-1]
        self.near = (fast + height if seq_first else height + fast) + digits_of("dp")[-1:]
        self.buffers = [(jnp.concatenate(blocks, axis=1), ())]

    def values(self):
        return [b for b, _ in self.buffers]

    def wait(self, *others):
        self.buffers = [(after(b, *others), d) for b, d in self.buffers]

    def far_step(self, n):
        (block, digits), digit = self.buffers[0], self.far[n]
        self.buffers = [(jnp.concatenate([block, swap(block, digit)], axis=0), digits + (digit,))]

    def near_step(self, n):
        digit = self.near[n]
        self.buffers = self.buffers + [(swap(b, digit), d + (digit,)) for b, d in self.buffers]

    def finish(self):
        offsets = []
        rows = self.rows
        stride_of = lambda digit: digit[1] * (lax.axis_size("seq") if digit[0] == "dp" else 1)
        for _, digits in self.buffers:
            near = sum(stride_of(d) for d in digits if d not in self.far)
            for n in range(1 << len(self.far)):
                offsets.append(near + sum(stride_of(d) for bit, d in enumerate(self.far) if n >> bit & 1))
        mine = lax.axis_index("dp") * lax.axis_size("seq") + lax.axis_index("seq")
        targets = lax.bitwise_xor(jnp.asarray(offsets, jnp.int32), mine.astype(jnp.int32)) * rows
        count = len(offsets)
        return pl.pallas_call(
            functools.partial(place_kernel, count, rows, self.widths),
            grid_spec=pltpu.PrefetchScalarGridSpec(
                num_scalar_prefetch=1,
                in_specs=[pl.BlockSpec(memory_space=pl.ANY)] * len(self.buffers),
                out_specs=[pl.BlockSpec(memory_space=pl.ANY)] * len(self.widths),
                scratch_shapes=[
                    pltpu.VMEM((SLOTS, rows, sum(self.widths)), bf16),
                    pltpu.SemaphoreType.DMA((SLOTS,)),
                    pltpu.SemaphoreType.DMA((SLOTS, len(self.widths))),
                ],
            ),
            out_shape=[jax.ShapeDtypeStruct((count * rows, width), bf16) for width in self.widths],
            compiler_params=pltpu.CompilerParams(vmem_limit_bytes=16 * 1024 * 1024),
            cost_estimate=pl.CostEstimate(flops=0, bytes_accessed=4 * count * rows * sum(self.widths), transcendentals=0),
            name="place",
        )(targets, *self.values())


def tn(a, b):
    return lax.dot_general(a, b, (((0,), (0,)), ((), ())), preferred_element_type=f32)


def after(value, *others):
    return lax.optimization_barrier((value,) + others)[0]


def pieces_of(side, seq_first):
    dp, seq = lax.axis_size("dp"), lax.axis_size("seq")
    tokens, total = side.shape
    if seq_first:
        pieces = side.reshape(tokens, dp // 2, 2, seq // 2, 2, -1).transpose(2, 0, 4, 1, 3, 5)
    else:
        pieces = side.reshape(tokens, dp // 2, 2, -1).transpose(2, 0, 1, 3)
    return pieces.reshape(2, tokens, total // 2)


class Reduce:
    def __init__(self, pieces, cols_side, seq_first, transposed=False):
        self.pieces, self.cols_side, self.seq_first, self.transposed = pieces, cols_side, seq_first, transposed
        self.half = pieces.shape[1 if transposed else 2] // 2
        self.own = self.half * 4 // (lax.axis_size("dp") * lax.axis_size("seq"))
        self.core, self.height = digits_of("dp")[-1], digits_of("dp")[0]
        self.fast, self.far = digits_of("seq")[-1], digits_of("seq")[:-1]
        self.first = self.fast if seq_first else self.height
        self.c, self.mine = digit_index(self.core), digit_index(self.first)

    def term(self, core_index, index, others):
        side = pick(after(self.pieces, *others), core_index, 0)
        if index is not None:
            side = lax.dynamic_slice_in_dim(side, index * self.half, self.half, 0 if self.transposed else 1)
        if self.transposed:
            return jnp.dot(side, self.cols_side, preferred_element_type=f32)
        return tn(side, self.cols_side)

    def cross(self, *others):
        term = self.term(1 - self.c, None, others).astype(bf16)
        self.got = swap(term, self.core)
        return term

    def got_part(self, index):
        return lax.dynamic_slice_in_dim(self.got, index * self.half, self.half, 0).astype(f32)

    def send(self, *others):
        away = (self.term(self.c, 1 - self.mine, others) + self.got_part(1 - self.mine)).astype(bf16)
        self.away = swap(away, self.first)
        return away

    def keep(self, *others):
        total = self.term(self.c, self.mine, others) + self.got_part(self.mine) + self.away.astype(f32)
        self.total = total.astype(bf16)
        return self.total

    def second(self, *others):
        cols = self.cols_side.shape[1]
        total = after(self.total, *others)
        if self.seq_first:
            self.total = scatter_digit(total.reshape(2, -1, cols), self.height, 0, bf16)
        else:
            self.total = scatter_digit(total.reshape(-1, 2, self.own, cols), self.fast, 1, bf16)
        return self.total


class Finish:
    def __init__(self, reduces, *others):
        self.reduces, self.far = reduces, reduces[0].far
        self.count = 1 << len(self.far)
        self.unit = D // (lax.axis_size("dp") * lax.axis_size("seq"))
        totals = [after(r.total, *others).reshape(self.count, self.unit, -1) for r in reduces]
        self.widths = [t.shape[2] for t in totals]
        self.total = jnp.concatenate(totals, axis=2)

    def step(self, n, *others):
        total = after(self.total, *others).reshape(-1, 2, self.unit, sum(self.widths))
        self.total = scatter_digit(total, self.far[-1 - n], 1, f32 if n == len(self.far) - 1 else bf16)
        return self.total

    def results(self):
        left = 0
        results = []
        for r, width in zip(self.reduces, self.widths):
            results.append(self.total[0, :, left : left + width].reshape(r.own, -1))
            left += width
        return results


def dot_nt(a, b):
    return lax.dot_general(a, b, (((1,), (1,)), ((), ())), preferred_element_type=f32)


def dot_tn(a, b):
    return lax.dot_general(a, b, (((0,), (0,)), ((), ())), preferred_element_type=f32)


def dot_nn(a, b):
    return lax.dot_general(a, b, (((1,), (0,)), ((), ())), preferred_element_type=f32)


def tile_of(ref, index):
    per = TILE // ref.shape[1]
    return ref[pl.ds(index * per, per)].reshape(TILE, HD)


def mask_of(i, j, lo):
    key = j * TILE + lax.broadcasted_iota(jnp.int32, (TILE, TILE), 0)
    query = i * TILE + lax.broadcasted_iota(jnp.int32, (TILE, TILE), 1)
    return (key >= lo) & (key <= query)


def forward_kernel(bounds, q_ref, k_ref, v_ref, lo_ref, o_ref, lse_ref, acc):
    pair, i = pl.program_id(0), pl.program_id(1)
    q = q_ref[...].reshape(TILE, HD)
    lo = lo_ref[...]
    factor = SCALE * LOG2E

    def step(j, carry, masked):
        m, l = carry
        s = dot_nt(tile_of(k_ref, j), q) * factor
        if masked:
            s = jnp.where(mask_of(i, j, lo), s, MASKED)
        new = jnp.maximum(m, jnp.max(s, axis=0, keepdims=True))
        p = jnp.exp2(s - new)
        old = jnp.exp2(m - new)
        acc[...] = acc[...] * old + dot_tn(tile_of(v_ref, j), p.astype(bf16))
        return new, l * old + jnp.sum(p, axis=0, keepdims=True)

    acc[...] = jnp.zeros_like(acc)
    carry = (jnp.full((1, TILE), MASKED, f32), jnp.zeros((1, TILE), f32))
    start = bounds[pair, 0, i]
    middle = bounds[pair, 1, i]
    carry = lax.fori_loop(start, middle, lambda j, c: step(j, c, True), carry)
    carry = lax.fori_loop(middle, i, lambda j, c: step(j, c, False), carry)
    m, l = step(i, carry, True)
    o_ref[...] = (acc[...] / l).T.astype(bf16).reshape(o_ref.shape)
    lse_ref[...] = m + jnp.log2(l)


def attend(qkv, bounds, low):
    seq, pairs, rows, _ = qkv.shape
    length = seq * rows
    blocks, per = length // TILE, TILE // rows
    whole = lambda part: pl.BlockSpec((seq, None, rows, HD), lambda p, i, b: (0, p, 0, part))
    line = pl.BlockSpec((None, 1, TILE), lambda p, i, b: (p, 0, i))
    block = pl.BlockSpec((per, None, rows, HD), lambda p, i, b: (i, p, 0, 0))
    return pl.pallas_call(
        forward_kernel,
        grid_spec=pltpu.PrefetchScalarGridSpec(
            num_scalar_prefetch=1,
            grid=(pairs, blocks),
            in_specs=[block, whole(1), whole(2), line],
            out_specs=[block, line],
            scratch_shapes=[pltpu.VMEM((HD, TILE), f32)],
        ),
        out_shape=[
            jax.ShapeDtypeStruct((seq, pairs, rows, HD), bf16),
            jax.ShapeDtypeStruct((pairs, 1, length), f32),
        ],
        compiler_params=pltpu.CompilerParams(vmem_limit_bytes=32 * 1024 * 1024),
        cost_estimate=pl.CostEstimate(
            flops=8 * pairs * length * 1792 * HD,
            bytes_accessed=8 * pairs * length * HD,
            transcendentals=pairs * length * 1792,
        ),
        name="attend",
    )(bounds, qkv, qkv, qkv, low)


def backward_kernel(bounds, q_ref, k_ref, v_ref, do_ref, o_ref, lse_ref, lo_ref, out_ref, dq, dk, dv, delta):
    pair, j = pl.program_id(0), pl.program_id(1)
    k = k_ref[...].reshape(TILE, HD)
    v = v_ref[...].reshape(TILE, HD)
    factor = SCALE * LOG2E

    def step(i, masked):
        rows = pl.ds(pl.multiple_of(i * TILE, TILE), TILE)
        q = tile_of(q_ref, i)
        do = tile_of(do_ref, i)
        s = dot_nt(k, q) * factor
        p = jnp.exp2(s - lse_ref[:, rows])
        if masked:
            p = jnp.where(mask_of(i, j, lo_ref[:, rows]), p, 0.0)
        dp = dot_nt(v, do)
        ds = (p * (dp - delta[:, rows])).astype(bf16)
        dv[...] += dot_nn(p.astype(bf16), do)
        dk[...] += dot_nn(ds, q)
        dq[rows, :] += dot_tn(ds, k)

    @pl.when(j == 0)
    def _():
        dq[...] = jnp.zeros_like(dq)

        @pl.loop(0, pl.num_programs(1))
        def _(i):
            rows = pl.ds(pl.multiple_of(i * TILE, TILE), TILE)
            product = tile_of(do_ref, i).astype(f32) * tile_of(o_ref, i).astype(f32)
            delta[:, rows] = jnp.sum(product.T, axis=0, keepdims=True)

    dk[...] = jnp.zeros_like(dk)
    dv[...] = jnp.zeros_like(dv)
    step(j, True)
    middle = bounds[pair, 2, j]
    end = bounds[pair, 3, j]

    @pl.loop(j + 1, middle)
    def _(i):
        step(i, False)

    @pl.loop(middle, end)
    def _(i):
        step(i, True)

    own = pl.ds(pl.multiple_of(j * TILE, TILE), TILE)
    shape = out_ref.shape[:-1] + (HD,)
    out_ref[:, :, :HD] = (dq[own, :] * SCALE).astype(bf16).reshape(shape)
    out_ref[:, :, HD : 2 * HD] = (dk[...] * SCALE).astype(bf16).reshape(shape)
    out_ref[:, :, 2 * HD :] = dv[...].astype(bf16).reshape(shape)


def attend_back(qkv, grad, mixed, lse, bounds, low):
    seq, pairs, rows, _ = qkv.shape
    length = seq * rows
    blocks, per = length // TILE, TILE // rows
    whole = pl.BlockSpec((seq, None, rows, HD), lambda p, j, b: (0, p, 0, 0))
    line = pl.BlockSpec((None, 1, length), lambda p, j, b: (p, 0, 0))
    block = lambda part: pl.BlockSpec((per, None, rows, HD), lambda p, j, b: (j, p, 0, part))
    return pl.pallas_call(
        backward_kernel,
        grid_spec=pltpu.PrefetchScalarGridSpec(
            num_scalar_prefetch=1,
            grid=(pairs, blocks),
            in_specs=[whole, block(1), block(2), whole, whole, line, line],
            out_specs=pl.BlockSpec((per, None, rows, 3 * HD), lambda p, j, b: (j, p, 0, 0)),
            scratch_shapes=[
                pltpu.VMEM((length, HD), f32),
                pltpu.VMEM((TILE, HD), f32),
                pltpu.VMEM((TILE, HD), f32),
                pltpu.VMEM((1, length), f32),
            ],
        ),
        out_shape=jax.ShapeDtypeStruct(qkv.shape, bf16),
        compiler_params=pltpu.CompilerParams(vmem_limit_bytes=40 * 1024 * 1024),
        cost_estimate=pl.CostEstimate(
            flops=20 * pairs * length * 1792 * HD,
            bytes_accessed=16 * pairs * length * HD,
            transcendentals=pairs * length * 1792,
        ),
        name="attend_back",
    )(bounds, qkv, qkv, qkv, grad, mixed, lse, low)


def key_bounds(segments):
    length = segments.shape[0]
    blocks = length // TILE
    place = jnp.arange(length, dtype=jnp.int32)
    start = jnp.zeros_like(place)
    for value in range(1, 4):
        earlier = jnp.sum(segments < value, dtype=jnp.int32)
        start = jnp.where(segments == value, earlier, start)
    low = jnp.maximum(start, place - (WINDOW - 1))
    index = jnp.arange(blocks, dtype=jnp.int32)
    first = low[::TILE]
    last = low[TILE - 1 :: TILE]
    begin = first // TILE
    middle = jnp.clip((last + TILE - 1) // TILE, begin, index)
    full = (last[None, :] <= index[:, None] * TILE) & (index[None, :] > index[:, None])
    some = (first[None, :] < (index[:, None] + 1) * TILE) & (index[None, :] > index[:, None])
    back_middle = index + 1 + jnp.sum(full, axis=1, dtype=jnp.int32)
    back_end = index + 1 + jnp.sum(some, axis=1, dtype=jnp.int32)
    return low[None], jnp.stack([begin, middle, back_middle, back_end])


def to_heads(rows, heads):
    seq = lax.axis_size("seq")
    parts = rows.shape[1] // (heads * HD)
    count = rows.shape[0] // MB
    split = rows.reshape(MB, count, parts, heads, HD).transpose(3, 0, 1, 2, 4)
    split = split.reshape(seq, heads * MB // seq, count, parts * HD)
    return lax.all_to_all(split, "seq", 0, 0, tiled=True)


def to_rows(whole, heads):
    got = lax.all_to_all(whole, "seq", 0, 0, tiled=True)
    count, parts = got.shape[2], got.shape[3] // HD
    got = got.reshape(heads, MB, count, parts, HD).transpose(1, 2, 3, 0, 4)
    return got.reshape(MB * count, parts * heads * HD)


def norm_scale(values):
    return lax.rsqrt(jnp.mean(values * values, axis=-1, keepdims=True) + EPSILON)


def norm_backward(grad_in, values, row_scale, gain):
    normed = values * row_scale
    gain_grad = jnp.sum(grad_in * normed, axis=0)
    scaled = grad_in * gain
    inner = jnp.mean(scaled * normed, axis=-1, keepdims=True)
    return row_scale * (scaled - normed * inner), gain_grad


def nt(a, b):
    return jnp.einsum("re,de->rd", a, b, preferred_element_type=f32)


def shards(tokens, segment_ids, w_qkv, w_out, w_gate_up, w_down, gain_attn, gain_mlp, cotangent):
    rows = tokens.shape[2]
    seq = lax.axis_size("seq")
    gather = lambda w: lax.all_gather(w, ("dp", "seq"), axis=0, tiled=True)
    groups = 2 if H * MB % (2 * seq) == 0 else 1
    heads = H // groups
    pairs = heads * MB // seq
    width = heads * HD

    x = tokens.reshape(MB * rows, D).astype(f32)
    cot = cotangent.reshape(MB * rows, D)
    bounds, low = [], []
    for k in range(pairs):
        micro = lax.rem(lax.axis_index("seq") * pairs + k, MB)
        pair_low, pair_bounds = key_bounds(pick(segment_ids[:, 0], micro, 0))
        bounds.append(pair_bounds)
        low.append(pair_low)
    bounds, low = jnp.stack(bounds), jnp.stack(low)

    order_qkv = w_qkv.reshape(-1, 3, groups, width).transpose(0, 2, 1, 3).reshape(w_qkv.shape)
    all_qkv = gather(order_qkv)
    full_qkv = [all_qkv[:, g * 3 * width : (g + 1) * 3 * width] for g in range(groups)]
    gains = gather_small(jnp.stack([gain_attn, gain_mlp])).astype(f32)
    gain_a, gain_m = gains[0], gains[1]
    scale_a = norm_scale(x)
    h_attn = (x * scale_a * gain_a).astype(bf16)
    gathers = [
        Gather([w_gate_up[:, FF:], w_down.reshape(w_qkv.shape[0], -1)], True),
        Gather([w_gate_up[:, :FF], w_out], False),
    ]
    values = lambda: [v for w in gathers for v in w.values()]

    def advance(step, *others):
        ready = values()
        for w in gathers:
            w.wait(*others, *ready)
            step(w)

    for n in range(len(gathers[0].far)):
        advance(lambda w: w.far_step(n))
    h_attn = after(h_attn, *values())
    advance(lambda w: w.near_step(0))
    arrived = []
    step_in = h_attn
    for g in range(groups):
        qkv_rows = jnp.dot(step_in, full_qkv[g], preferred_element_type=f32).astype(bf16)
        arrived.append(to_heads(qkv_rows, heads))
        step_in = after(h_attn, qkv_rows, *values())
    advance(lambda w: w.near_step(1))
    saved, attended = [], []
    last = None
    for g in range(groups):
        qkv = arrived[g] if last is None else after(arrived[g], last)
        last, lse = attend(qkv, bounds, low)
        saved.append((qkv, last, lse))
        attended.append(to_rows(last, heads))
    advance(lambda w: w.near_step(2), last)
    full_up, full_down = gathers[0].finish()
    full_gate, full_out = gathers[1].finish()
    attended = jnp.concatenate(attended, axis=1)

    mid = x + jnp.dot(attended, full_out, preferred_element_type=f32)
    scale_m = norm_scale(mid)
    h_mlp = (mid * scale_m * gain_m).astype(bf16)
    gate = jnp.dot(h_mlp, full_gate, preferred_element_type=f32)
    up = jnp.dot(h_mlp, full_up, preferred_element_type=f32)
    sig = jax.nn.sigmoid(gate)
    act = (gate * sig * up).astype(bf16)
    full_down = after(full_down, act).reshape(FF, D)
    grad_act = nt(cot, full_down)
    grad_gate = (grad_act * up * sig * (1.0 + gate * (1.0 - sig))).astype(bf16)
    grad_up = (grad_act * (gate * sig)).astype(bf16)
    grad_h_mlp = nt(grad_gate, full_gate) + nt(grad_up, full_up)
    grad_mid_norm, gain_m_grad = norm_backward(grad_h_mlp, mid, scale_m, gain_m)
    grad_mid = cot.astype(f32) + grad_mid_norm
    grad_branch = grad_mid.astype(bf16)
    grad_rows = [nt(grad_branch, full_out[g * width : (g + 1) * width]).astype(bf16) for g in range(groups)]
    grads = [to_heads(r, heads) for r in grad_rows]

    act_pieces = act.T.reshape(lax.axis_size("dp") // 2, 2, -1, MB * rows).transpose(1, 0, 2, 3)
    down = Reduce(act_pieces.reshape(2, FF // 2, MB * rows), cot, False, transposed=True)
    gate_r = Reduce(pieces_of(h_mlp, False), grad_gate, False)
    up_r = Reduce(pieces_of(h_mlp, True), grad_up, True)
    out_r = Reduce(pieces_of(attended, False), grad_branch, False)
    early = [gate_r, up_r, down, out_r]
    mark = tuple(grad_rows)
    for r in early:
        mark = (r.cross(*mark),)
    for r in early:
        mark = (r.send(*mark),)
    grad_heads = []
    for g in range(groups):
        qkv, mixed, lse = saved[g]
        back = attend_back(after(qkv, *mark), grads[g], mixed, lse, bounds, low)
        grad_heads.append(back)
        mark = (back,)
    grad_qkv = [to_rows(back, heads) for back in grad_heads]
    for r in early:
        mark = (r.keep(*mark),)
    layer_out = (mid + jnp.dot(after(act, *mark), full_down, preferred_element_type=f32)).astype(bf16)
    mark = (layer_out,)
    for r in early:
        r.second()

    h_sides = [pieces_of(h_attn, False), pieces_of(h_attn, True)]
    half = 3 * width // 2
    late = []
    grad_h_attn = 0.0
    for g in range(groups):
        final = g == groups - 1
        pair = [Reduce(h_sides[0], grad_qkv[g][:, :half], False), Reduce(h_sides[1], grad_qkv[g][:, half:], True)]
        for r in pair:
            mark = (r.cross(*mark),)
        part = nt(after(grad_qkv[g], *mark), full_qkv[g])
        grad_h_attn = grad_h_attn + part
        mark = (part,)
        for r in pair:
            mark = (r.send(*mark),)
        if final:
            first = Finish(early + late, *mark)
            first.step(0)
            grad_tok_norm, gain_a_grad = norm_backward(after(grad_h_attn, *mark), x, scale_a, gain_a)
            grad_tokens = grad_mid + grad_tok_norm
            mark = (grad_tokens,)
        late += pair
        for r in pair:
            mark = (r.keep(*mark),)
        for r in pair:
            r.second(*mark)
        if not final:
            mark = mark + tuple(r.total for r in early + pair)
    gain_grads = scatter_small(jnp.stack([gain_a_grad, gain_m_grad]))
    second = Finish(pair)
    far = len(first.far)
    for n in range(far):
        if n:
            first.step(n, *mark)
        second.step(n)
    results = first.results() + second.results()
    gate_grad, up_grad, down_grad, out_grad = results[:4]
    qkv_grads = [
        jnp.concatenate(results[4 + 2 * g : 6 + 2 * g], axis=1).reshape(-1, 3, 1, width) for g in range(groups)
    ]

    return (
        layer_out.reshape(MB, 1, rows, D),
        grad_tokens.reshape(MB, 1, rows, D),
        jnp.concatenate(qkv_grads, axis=2).reshape(-1, 3 * D),
        out_grad,
        jnp.concatenate([gate_grad, up_grad], axis=1),
        down_grad,
        gain_grads[0],
        gain_grads[1],
    )


def solution(mesh):
    by_rows = P(("dp", "seq"), None)
    by_tokens = P(None, "dp", "seq", None)
    vector = P(("dp", "seq"))
    return jax.shard_map(
        shards,
        mesh=mesh,
        in_specs=(by_tokens, P(None, "dp", None), by_rows, by_rows, by_rows, by_rows, vector, vector, by_tokens),
        out_specs=(by_tokens, by_tokens, by_rows, by_rows, by_rows, by_rows, vector, vector),
        check_vma=False,
    )
```

```python
import functools
import math

import jax
import jax.numpy as jnp
from jax import lax
from jax.experimental import pallas as pl
from jax.experimental.pallas import tpu as pltpu
from jax.sharding import PartitionSpec as P

D = 2048
H = 16
HD = 128
FF = 5504
WINDOW = 2048
MB = 2
TILE = 512

EPSILON = 1e-05
MASKED = -1e30
LOG2E = 1.4426950408889634
SCALE = 1.0 / math.sqrt(HD)

bf16 = jnp.bfloat16
f32 = jnp.float32


def digits_of(axis):
    size = lax.axis_size(axis)
    return [(axis, 1 << bit) for bit in reversed(range(size.bit_length() - 1))]


def digit_index(digit):
    axis, stride = digit
    return lax.rem(lax.axis_index(axis) // stride, 2)


def swap(block, digit):
    axis, stride = digit
    return lax.ppermute(block, axis, [(i, i ^ stride) for i in range(lax.axis_size(axis))])


def pick(array, index, dim):
    return lax.dynamic_index_in_dim(array, index, dim, keepdims=False)


def scatter_digit(parts, digit, dim, out_type):
    own = digit_index(digit)
    got = swap(pick(parts, 1 - own, dim), digit)
    return (pick(parts, own, dim).astype(f32) + got.astype(f32)).astype(out_type)


def gather_small(block):
    for digit in reversed(digits_of("dp") + digits_of("seq")):
        got = swap(block, digit)
        low = digit_index(digit) == 0
        block = jnp.concatenate([jnp.where(low, block, got), jnp.where(low, got, block)], axis=-1)
    return block


def scatter_small(terms):
    k = terms.shape[0]
    for digit in digits_of("dp") + digits_of("seq"):
        terms = scatter_digit(terms.reshape(k, 2, -1), digit, 1, f32)
    return terms


SLOTS = 8


def place_kernel(count, rows, widths, target, *refs):
    sources, outs = refs[: -3 - len(widths)], refs[-3 - len(widths) : -3]
    held, in_sems, out_sems = refs[-3:]
    per = sources[0].shape[0] // rows

    def read(n):
        source = sources[n // per].at[pl.ds((n % per) * rows, rows), :]
        return pltpu.make_async_copy(source, held.at[n % SLOTS], in_sems.at[n % SLOTS])

    def writes(n):
        start, left = pl.multiple_of(target[n], 16), 0
        copies = []
        for k, width in enumerate(widths):
            source = held.at[n % SLOTS, :, pl.ds(left, width)]
            copies.append(pltpu.make_async_copy(source, outs[k].at[pl.ds(start, rows), :], out_sems.at[n % SLOTS, k]))
            left += width
        return copies

    lag = SLOTS // 2
    for n in range(min(lag, count)):
        read(n).start()
    for n in range(count):
        if n >= lag:
            for copy in writes(n - lag):
                copy.wait()
        if n + lag < count:
            read(n + lag).start()
        read(n).wait()
        for copy in writes(n):
            copy.start()
    for n in range(max(count - lag, 0), count):
        for copy in writes(n):
            copy.wait()


class Gather:
    def __init__(self, blocks, seq_first):
        self.rows, self.widths = blocks[0].shape[0], [b.shape[1] for b in blocks]
        fast, height = digits_of("seq")[-1:], digits_of("dp")[:-1]
        self.far = digits_of("seq")[:-1]
        self.near = (fast + height if seq_first else height + fast) + digits_of("dp")[-1:]
        self.buffers = [(jnp.concatenate(blocks, axis=1), ())]

    def values(self):
        return [b for b, _ in self.buffers]

    def wait(self, *others):
        self.buffers = [(after(b, *others), d) for b, d in self.buffers]

    def far_step(self, n):
        (block, digits), digit = self.buffers[0], self.far[n]
        self.buffers = [(jnp.concatenate([block, swap(block, digit)], axis=0), digits + (digit,))]

    def near_step(self, n):
        digit = self.near[n]
        self.buffers = self.buffers + [(swap(b, digit), d + (digit,)) for b, d in self.buffers]

    def finish(self):
        offsets = []
        rows = self.rows
        stride_of = lambda digit: digit[1] * (lax.axis_size("seq") if digit[0] == "dp" else 1)
        for _, digits in self.buffers:
            near = sum(stride_of(d) for d in digits if d not in self.far)
            for n in range(1 << len(self.far)):
                offsets.append(near + sum(stride_of(d) for bit, d in enumerate(self.far) if n >> bit & 1))
        mine = lax.axis_index("dp") * lax.axis_size("seq") + lax.axis_index("seq")
        targets = lax.bitwise_xor(jnp.asarray(offsets, jnp.int32), mine.astype(jnp.int32)) * rows
        count = len(offsets)
        return pl.pallas_call(
            functools.partial(place_kernel, count, rows, self.widths),
            grid_spec=pltpu.PrefetchScalarGridSpec(
                num_scalar_prefetch=1,
                in_specs=[pl.BlockSpec(memory_space=pl.ANY)] * len(self.buffers),
                out_specs=[pl.BlockSpec(memory_space=pl.ANY)] * len(self.widths),
                scratch_shapes=[
                    pltpu.VMEM((SLOTS, rows, sum(self.widths)), bf16),
                    pltpu.SemaphoreType.DMA((SLOTS,)),
                    pltpu.SemaphoreType.DMA((SLOTS, len(self.widths))),
                ],
            ),
            out_shape=[jax.ShapeDtypeStruct((count * rows, width), bf16) for width in self.widths],
            compiler_params=pltpu.CompilerParams(vmem_limit_bytes=16 * 1024 * 1024),
            cost_estimate=pl.CostEstimate(flops=0, bytes_accessed=4 * count * rows * sum(self.widths), transcendentals=0),
            name="place",
        )(targets, *self.values())


def tn(a, b):
    return lax.dot_general(a, b, (((0,), (0,)), ((), ())), preferred_element_type=f32)


def after(value, *others):
    return lax.optimization_barrier((value,) + others)[0]


def pieces_of(side, seq_first):
    dp, seq = lax.axis_size("dp"), lax.axis_size("seq")
    tokens, total = side.shape
    if seq_first:
        pieces = side.reshape(tokens, dp // 2, 2, seq // 2, 2, -1).transpose(2, 0, 4, 1, 3, 5)
    else:
        pieces = side.reshape(tokens, dp // 2, 2, -1).transpose(2, 0, 1, 3)
    return pieces.reshape(2, tokens, total // 2)


class Reduce:
    def __init__(self, pieces, cols_side, seq_first, product=None):
        self.pieces, self.cols_side, self.seq_first, self.product = pieces, cols_side, seq_first, product
        self.half = product.shape[0] // 4 if pieces is None else pieces.shape[2] // 2
        self.own = self.half * 4 // (lax.axis_size("dp") * lax.axis_size("seq"))
        self.core, self.height = digits_of("dp")[-1], digits_of("dp")[0]
        self.fast, self.far = digits_of("seq")[-1], digits_of("seq")[:-1]
        self.first = self.fast if seq_first else self.height
        self.c, self.mine = digit_index(self.core), digit_index(self.first)

    def term(self, core_index, index, others):
        if self.pieces is None:
            parts = pick(after(self.product, *others).reshape(2, 2, self.half, -1), core_index, 1)
            return (parts.reshape(2 * self.half, -1) if index is None else pick(parts, index, 0)).astype(f32)
        side = pick(after(self.pieces, *others), core_index, 0)
        if index is not None:
            side = lax.dynamic_slice_in_dim(side, index * self.half, self.half, 1)
        return tn(side, self.cols_side)

    def cross(self, *others):
        term = self.term(1 - self.c, None, others).astype(bf16)
        self.got = swap(term, self.core)
        return term

    def got_part(self, index):
        return lax.dynamic_slice_in_dim(self.got, index * self.half, self.half, 0).astype(f32)

    def send(self, *others):
        away = (self.term(self.c, 1 - self.mine, others) + self.got_part(1 - self.mine)).astype(bf16)
        self.away = swap(away, self.first)
        return away

    def keep(self, *others):
        total = self.term(self.c, self.mine, others) + self.got_part(self.mine) + self.away.astype(f32)
        self.total = total.astype(bf16)
        return self.total

    def second(self, *others):
        cols = self.cols_side.shape[1]
        total = after(self.total, *others)
        if self.seq_first:
            self.total = scatter_digit(total.reshape(2, -1, cols), self.height, 0, bf16)
        else:
            self.total = scatter_digit(total.reshape(-1, 2, self.own, cols), self.fast, 1, bf16)
        return self.total


class Finish:
    def __init__(self, reduces, *others):
        self.reduces, self.far = reduces, reduces[0].far
        self.count = 1 << len(self.far)
        self.unit = D // (lax.axis_size("dp") * lax.axis_size("seq"))
        totals = [after(r.total, *others).reshape(self.count, self.unit, -1) for r in reduces]
        self.widths = [t.shape[2] for t in totals]
        self.total = jnp.concatenate(totals, axis=2)

    def step(self, n, *others):
        total = after(self.total, *others).reshape(-1, 2, self.unit, sum(self.widths))
        self.total = scatter_digit(total, self.far[-1 - n], 1, f32 if n == len(self.far) - 1 else bf16)
        return self.total

    def results(self):
        left = 0
        results = []
        for r, width in zip(self.reduces, self.widths):
            results.append(self.total[0, :, left : left + width].reshape(r.own, -1))
            left += width
        return results


def dot_nt(a, b):
    return lax.dot_general(a, b, (((1,), (1,)), ((), ())), preferred_element_type=f32)


def dot_tn(a, b):
    return lax.dot_general(a, b, (((0,), (0,)), ((), ())), preferred_element_type=f32)


def dot_nn(a, b):
    return lax.dot_general(a, b, (((1,), (0,)), ((), ())), preferred_element_type=f32)


def tile_of(ref, index):
    per = TILE // ref.shape[1]
    return ref[pl.ds(index * per, per)].reshape(TILE, HD)


def mask_of(i, j, lo):
    key = j * TILE + lax.broadcasted_iota(jnp.int32, (TILE, TILE), 0)
    query = i * TILE + lax.broadcasted_iota(jnp.int32, (TILE, TILE), 1)
    return (key >= lo) & (key <= query)


def forward_kernel(bounds, q_ref, k_ref, v_ref, lo_ref, o_ref, lse_ref, acc):
    pair, i = pl.program_id(0), pl.program_id(1)
    q = q_ref[...].reshape(TILE, HD)
    lo = lo_ref[...]
    factor = SCALE * LOG2E

    def step(j, carry, masked):
        m, l = carry
        s = dot_nt(tile_of(k_ref, j), q) * factor
        if masked:
            s = jnp.where(mask_of(i, j, lo), s, MASKED)
        new = jnp.maximum(m, jnp.max(s, axis=0, keepdims=True))
        p = jnp.exp2(s - new)
        old = jnp.exp2(m - new)
        acc[...] = acc[...] * old + dot_tn(tile_of(v_ref, j), p.astype(bf16))
        return new, l * old + jnp.sum(p, axis=0, keepdims=True)

    acc[...] = jnp.zeros_like(acc)
    carry = (jnp.full((1, TILE), MASKED, f32), jnp.zeros((1, TILE), f32))
    start = bounds[pair, 0, i]
    middle = bounds[pair, 1, i]
    carry = lax.fori_loop(start, middle, lambda j, c: step(j, c, True), carry)
    carry = lax.fori_loop(middle, i, lambda j, c: step(j, c, False), carry)
    m, l = step(i, carry, True)
    o_ref[...] = (acc[...] / l).T.astype(bf16).reshape(o_ref.shape)
    lse_ref[...] = m + jnp.log2(l)


def attend(qkv, bounds, low):
    seq, pairs, rows, _ = qkv.shape
    length = seq * rows
    blocks, per = length // TILE, TILE // rows
    whole = lambda part: pl.BlockSpec((seq, None, rows, HD), lambda p, i, b: (0, p, 0, part))
    line = pl.BlockSpec((None, 1, TILE), lambda p, i, b: (p, 0, i))
    block = pl.BlockSpec((per, None, rows, HD), lambda p, i, b: (i, p, 0, 0))
    return pl.pallas_call(
        forward_kernel,
        grid_spec=pltpu.PrefetchScalarGridSpec(
            num_scalar_prefetch=1,
            grid=(pairs, blocks),
            in_specs=[block, whole(1), whole(2), line],
            out_specs=[block, line],
            scratch_shapes=[pltpu.VMEM((HD, TILE), f32)],
        ),
        out_shape=[
            jax.ShapeDtypeStruct((seq, pairs, rows, HD), bf16),
            jax.ShapeDtypeStruct((pairs, 1, length), f32),
        ],
        compiler_params=pltpu.CompilerParams(vmem_limit_bytes=32 * 1024 * 1024),
        cost_estimate=pl.CostEstimate(
            flops=8 * pairs * length * 1792 * HD,
            bytes_accessed=8 * pairs * length * HD,
            transcendentals=pairs * length * 1792,
        ),
        name="attend",
    )(bounds, qkv, qkv, qkv, low)


def backward_kernel(bounds, q_ref, k_ref, v_ref, do_ref, o_ref, lse_ref, lo_ref, out_ref, dq, dk, dv, delta):
    pair, j = pl.program_id(0), pl.program_id(1)
    k = k_ref[...].reshape(TILE, HD)
    v = v_ref[...].reshape(TILE, HD)
    factor = SCALE * LOG2E

    def step(i, masked):
        rows = pl.ds(pl.multiple_of(i * TILE, TILE), TILE)
        q = tile_of(q_ref, i)
        do = tile_of(do_ref, i)
        s = dot_nt(k, q) * factor
        p = jnp.exp2(s - lse_ref[:, rows])
        if masked:
            p = jnp.where(mask_of(i, j, lo_ref[:, rows]), p, 0.0)
        dp = dot_nt(v, do)
        ds = (p * (dp - delta[:, rows])).astype(bf16)
        dv[...] += dot_nn(p.astype(bf16), do)
        dk[...] += dot_nn(ds, q)
        dq[rows, :] += dot_tn(ds, k)

    @pl.when(j == 0)
    def _():
        dq[...] = jnp.zeros_like(dq)

        @pl.loop(0, pl.num_programs(1))
        def _(i):
            rows = pl.ds(pl.multiple_of(i * TILE, TILE), TILE)
            product = tile_of(do_ref, i).astype(f32) * tile_of(o_ref, i).astype(f32)
            delta[:, rows] = jnp.sum(product.T, axis=0, keepdims=True)

    dk[...] = jnp.zeros_like(dk)
    dv[...] = jnp.zeros_like(dv)
    step(j, True)
    middle = bounds[pair, 2, j]
    end = bounds[pair, 3, j]

    @pl.loop(j + 1, middle)
    def _(i):
        step(i, False)

    @pl.loop(middle, end)
    def _(i):
        step(i, True)

    own = pl.ds(pl.multiple_of(j * TILE, TILE), TILE)
    shape = out_ref.shape[:-1] + (HD,)
    out_ref[:, :, :HD] = (dq[own, :] * SCALE).astype(bf16).reshape(shape)
    out_ref[:, :, HD : 2 * HD] = (dk[...] * SCALE).astype(bf16).reshape(shape)
    out_ref[:, :, 2 * HD :] = dv[...].astype(bf16).reshape(shape)


def attend_back(qkv, grad, mixed, lse, bounds, low):
    seq, pairs, rows, _ = qkv.shape
    length = seq * rows
    blocks, per = length // TILE, TILE // rows
    whole = pl.BlockSpec((seq, None, rows, HD), lambda p, j, b: (0, p, 0, 0))
    line = pl.BlockSpec((None, 1, length), lambda p, j, b: (p, 0, 0))
    block = lambda part: pl.BlockSpec((per, None, rows, HD), lambda p, j, b: (j, p, 0, part))
    return pl.pallas_call(
        backward_kernel,
        grid_spec=pltpu.PrefetchScalarGridSpec(
            num_scalar_prefetch=1,
            grid=(pairs, blocks),
            in_specs=[whole, block(1), block(2), whole, whole, line, line],
            out_specs=pl.BlockSpec((per, None, rows, 3 * HD), lambda p, j, b: (j, p, 0, 0)),
            scratch_shapes=[
                pltpu.VMEM((length, HD), f32),
                pltpu.VMEM((TILE, HD), f32),
                pltpu.VMEM((TILE, HD), f32),
                pltpu.VMEM((1, length), f32),
            ],
        ),
        out_shape=jax.ShapeDtypeStruct(qkv.shape, bf16),
        compiler_params=pltpu.CompilerParams(vmem_limit_bytes=40 * 1024 * 1024),
        cost_estimate=pl.CostEstimate(
            flops=20 * pairs * length * 1792 * HD,
            bytes_accessed=16 * pairs * length * HD,
            transcendentals=pairs * length * 1792,
        ),
        name="attend_back",
    )(bounds, qkv, qkv, qkv, grad, mixed, lse, low)


def key_bounds(segments):
    length = segments.shape[0]
    blocks = length // TILE
    place = jnp.arange(length, dtype=jnp.int32)
    start = jnp.zeros_like(place)
    for value in range(1, 4):
        earlier = jnp.sum(segments < value, dtype=jnp.int32)
        start = jnp.where(segments == value, earlier, start)
    low = jnp.maximum(start, place - (WINDOW - 1))
    index = jnp.arange(blocks, dtype=jnp.int32)
    first = low[::TILE]
    last = low[TILE - 1 :: TILE]
    begin = first // TILE
    middle = jnp.clip((last + TILE - 1) // TILE, begin, index)
    full = (last[None, :] <= index[:, None] * TILE) & (index[None, :] > index[:, None])
    some = (first[None, :] < (index[:, None] + 1) * TILE) & (index[None, :] > index[:, None])
    back_middle = index + 1 + jnp.sum(full, axis=1, dtype=jnp.int32)
    back_end = index + 1 + jnp.sum(some, axis=1, dtype=jnp.int32)
    return low[None], jnp.stack([begin, middle, back_middle, back_end])


def to_heads(rows, heads):
    seq = lax.axis_size("seq")
    count, width = rows.shape[0] // MB, rows.shape[1] // heads
    split = rows.reshape(MB, count, heads, width).transpose(2, 0, 1, 3)
    split = split.reshape(seq, heads * MB // seq, count, width)
    return lax.all_to_all(split, "seq", 0, 0, tiled=True)


def to_rows(whole):
    return lax.all_to_all(whole, "seq", 0, 0, tiled=True)


def rows_of(got, heads):
    count, width = got.shape[2], got.shape[3]
    return got.reshape(heads, MB, count, width).transpose(1, 2, 0, 3).reshape(MB * count, heads * width)


def norm_scale(values):
    return lax.rsqrt(jnp.mean(values * values, axis=-1, keepdims=True) + EPSILON)


def norm_backward(grad_in, values, row_scale, gain):
    normed = values * row_scale
    gain_grad = jnp.sum(grad_in * normed, axis=0)
    scaled = grad_in * gain
    inner = jnp.mean(scaled * normed, axis=-1, keepdims=True)
    return row_scale * (scaled - normed * inner), gain_grad


def nt(a, b):
    return jnp.einsum("re,de->rd", a, b, preferred_element_type=f32)


def shards(tokens, segment_ids, w_qkv, w_out, w_gate_up, w_down, gain_attn, gain_mlp, cotangent):
    rows = tokens.shape[2]
    seq = lax.axis_size("seq")
    gather = lambda w: lax.all_gather(w, ("dp", "seq"), axis=0, tiled=True)
    groups = 2 if H * MB % (2 * seq) == 0 else 1
    heads = H // groups
    pairs = heads * MB // seq
    width = heads * HD

    x = tokens.reshape(MB * rows, D).astype(f32)
    cot = cotangent.reshape(MB * rows, D)
    bounds, low = [], []
    for k in range(pairs):
        micro = lax.rem(lax.axis_index("seq") * pairs + k, MB)
        pair_low, pair_bounds = key_bounds(pick(segment_ids[:, 0], micro, 0))
        bounds.append(pair_bounds)
        low.append(pair_low)
    bounds, low = jnp.stack(bounds), jnp.stack(low)

    order_qkv = w_qkv.reshape(-1, 3, groups, heads, HD).transpose(0, 2, 3, 1, 4).reshape(w_qkv.shape)
    all_qkv = gather(order_qkv)
    full_qkv = [all_qkv[:, g * 3 * width : (g + 1) * 3 * width] for g in range(groups)]
    all_gains = gather_small(jnp.stack([gain_attn, gain_mlp]))
    gains = all_gains.astype(f32)
    gain_a, gain_m = gains[0], gains[1]
    scale_a = norm_scale(x)
    h_attn = (x * scale_a * gain_a).astype(bf16)
    soon = Gather([w_gate_up[:, :FF], w_out], False)
    later = Gather([w_gate_up[:, FF:], w_down.reshape(w_qkv.shape[0], -1)], True)
    far = len(soon.far)

    soon.wait(all_gains)
    soon.far_step(0)
    for n in range(1, far):
        later.wait(*soon.values())
        soon.far_step(n)
        later.far_step(n - 1)
    ready = soon.values() + later.values()
    h_attn = after(h_attn, *ready)
    soon.wait(*ready)
    soon.near_step(0)
    later.wait(*ready)
    later.far_step(far - 1)
    arrived = []
    step_in = h_attn
    for g in range(groups):
        qkv_rows = jnp.dot(step_in, full_qkv[g], preferred_element_type=f32).astype(bf16)
        arrived.append(to_heads(qkv_rows, heads))
        ready = soon.values() + later.values()
        step_in = after(h_attn, qkv_rows, *ready)
    later.wait(*ready)
    later.near_step(0)
    soon.wait(*ready)
    soon.near_step(1)
    saved, attended = [], []
    last = None
    for g in range(groups):
        qkv = arrived[g] if last is None else after(arrived[g], last)
        last, lse = attend(qkv, bounds, low)
        saved.append((qkv, last, lse))
        attended.append(rows_of(to_rows(last), heads))
        if g == 0:
            later.wait(last)
            later.near_step(1)
    soon.wait(last)
    soon.near_step(2)
    full_gate, full_out = soon.finish()
    attended = jnp.concatenate(attended, axis=1)

    mid = x + jnp.dot(attended, full_out, preferred_element_type=f32)
    scale_m = norm_scale(mid)
    h_mlp = (mid * scale_m * gain_m).astype(bf16)
    later.wait(h_mlp)
    later.near_step(2)
    gate = jnp.dot(h_mlp, full_gate, preferred_element_type=f32)
    full_up, full_down = later.finish()
    full_down = full_down.reshape(FF, D)
    up = jnp.dot(h_mlp, full_up, preferred_element_type=f32)
    sig = jax.nn.sigmoid(gate)
    act = (gate * sig * up).astype(bf16)

    down = Reduce(None, cot, False, product=tn(act, cot).astype(bf16))
    mark = (down.cross(),)
    grad_act = nt(after(cot, *mark), full_down)
    grad_gate = (grad_act * up * sig * (1.0 + gate * (1.0 - sig))).astype(bf16)
    grad_up = (grad_act * (gate * sig)).astype(bf16)
    mark = (down.send(grad_gate, grad_up),)
    gate_r = Reduce(pieces_of(h_mlp, False), grad_gate, False)
    up_r = Reduce(pieces_of(h_mlp, True), grad_up, True)
    mark = (up_r.cross(*mark),)
    mark = (gate_r.cross(*mark),)
    half_grad = nt(after(grad_gate, *mark), full_gate)
    mark = (up_r.send(half_grad),)
    grad_h_mlp = half_grad + nt(after(grad_up, *mark), full_up)
    grad_mid_norm, gain_m_grad = norm_backward(grad_h_mlp, mid, scale_m, gain_m)
    grad_mid = cot.astype(f32) + grad_mid_norm
    grad_branch = grad_mid.astype(bf16)
    grad_rows = [nt(grad_branch, full_out[g * width : (g + 1) * width]).astype(bf16) for g in range(groups)]
    grads = [to_heads(r, heads) for r in grad_rows]

    out_r = Reduce(pieces_of(attended, False), grad_branch, False)
    early = [down, up_r, gate_r, out_r]
    mark = (gate_r.send(*grad_rows),)
    mark = (out_r.cross(*mark),)
    mark = (down.keep(*mark),)
    down.second()
    grad_heads = []
    for g in range(groups):
        qkv, mixed, lse = saved[g]
        back = attend_back(after(qkv, *mark), grads[g], mixed, lse, bounds, low)
        grad_heads.append(back)
        mark = (back,)
        if g == 0:
            mark = (up_r.keep(*mark),)
            up_r.second()
            mark = (out_r.send(*mark),)
    arrived = [to_rows(back) for back in grad_heads]
    grad_qkv = []
    for r in (gate_r, out_r):
        mark = (r.keep(*mark),)
        r.second()
    layer_out = (mid + jnp.dot(after(act, *mark), full_down, preferred_element_type=f32)).astype(bf16)
    mark = (layer_out,)

    h_sides = [pieces_of(h_attn, False), pieces_of(h_attn, True)]
    half = 3 * width // 2
    late = []
    grad_h_attn = 0.0
    for g in range(groups):
        final = g == groups - 1
        if final:
            first = Finish(early, *mark)
            mark = mark + (first.step(0),)
        grad_qkv.append(rows_of(after(arrived[g], *mark), heads))
        pair = [Reduce(h_sides[0], grad_qkv[g][:, :half], False), Reduce(h_sides[1], grad_qkv[g][:, half:], True)]
        for r in pair:
            mark = (r.cross(*mark),)
        if final:
            for n in range(1, far):
                first.step(n)
        part = nt(after(grad_qkv[g], *mark), full_qkv[g])
        grad_h_attn = grad_h_attn + part
        mark = (part,)
        for r in pair:
            mark = (r.send(*mark),)
        if final:
            grad_tok_norm, gain_a_grad = norm_backward(after(grad_h_attn, *mark), x, scale_a, gain_a)
            grad_tokens = grad_mid + grad_tok_norm
            mark = (grad_tokens, first.total)
        for r in pair:
            mark = (r.keep(*mark),)
        for r in pair:
            r.second(*mark)
        late += pair
        if not final:
            mark = mark + tuple(r.total for r in early + pair)
    gain_grads = scatter_small(jnp.stack([gain_a_grad, gain_m_grad]))
    second = Finish(late)
    for n in range(far):
        second.step(n)
    down_grad, up_grad, gate_grad, out_grad = first.results()
    terms = second.results()
    qkv_grads = [
        jnp.concatenate(terms[2 * g : 2 * g + 2], axis=1).reshape(-1, 1, heads, 3, HD) for g in range(groups)
    ]
    qkv_grad = jnp.concatenate(qkv_grads, axis=1).transpose(0, 3, 1, 2, 4)

    return (
        layer_out.reshape(MB, 1, rows, D),
        grad_tokens.reshape(MB, 1, rows, D),
        qkv_grad.reshape(-1, 3 * D),
        out_grad,
        jnp.concatenate([gate_grad, up_grad], axis=1),
        down_grad,
        gain_grads[0],
        gain_grads[1],
    )


def solution(mesh):
    by_rows = P(("dp", "seq"), None)
    by_tokens = P(None, "dp", "seq", None)
    vector = P(("dp", "seq"))
    return jax.shard_map(
        shards,
        mesh=mesh,
        in_specs=(by_tokens, P(None, "dp", None), by_rows, by_rows, by_rows, by_rows, vector, vector, by_tokens),
        out_specs=(by_tokens, by_tokens, by_rows, by_rows, by_rows, by_rows, vector, vector),
        check_vma=False,
    )
```

```python
import functools
import math

import jax
import jax.numpy as jnp
from jax import lax
from jax.experimental import pallas as pl
from jax.experimental.pallas import tpu as pltpu
from jax.sharding import PartitionSpec as P

D = 2048
H = 16
HD = 128
FF = 5504
WINDOW = 2048
MB = 2
TILE = 512

EPSILON = 1e-05
MASKED = -1e30
LOG2E = 1.4426950408889634
SCALE = 1.0 / math.sqrt(HD)

bf16 = jnp.bfloat16
f32 = jnp.float32


def digits_of(axis):
    size = lax.axis_size(axis)
    return [(axis, 1 << bit) for bit in reversed(range(size.bit_length() - 1))]


def digit_index(digit):
    axis, stride = digit
    return lax.rem(lax.axis_index(axis) // stride, 2)


def swap(block, digit):
    axis, stride = digit
    return lax.ppermute(block, axis, [(i, i ^ stride) for i in range(lax.axis_size(axis))])


def pick(array, index, dim):
    return lax.dynamic_index_in_dim(array, index, dim, keepdims=False)


def scatter_digit(parts, digit, dim, out_type, hold=()):
    own = digit_index(digit)
    got = swap(pick(parts, 1 - own, dim), digit)
    if hold:
        got = lax.optimization_barrier((got,) + tuple(hold))[0]
    return (pick(parts, own, dim).astype(f32) + got.astype(f32)).astype(out_type)


def gather_small(block):
    for digit in reversed(digits_of("dp") + digits_of("seq")):
        got = swap(block, digit)
        low = digit_index(digit) == 0
        block = jnp.concatenate([jnp.where(low, block, got), jnp.where(low, got, block)], axis=-1)
    return block


def scatter_small(terms):
    k = terms.shape[0]
    for digit in digits_of("dp") + digits_of("seq"):
        terms = scatter_digit(terms.reshape(k, 2, -1), digit, 1, f32)
    return terms


SLOTS = 8


def place_kernel(count, rows, widths, target, *refs):
    sources, outs = refs[: -3 - len(widths)], refs[-3 - len(widths) : -3]
    held, in_sems, out_sems = refs[-3:]
    per = sources[0].shape[0] // rows

    def read(n):
        source = sources[n // per].at[pl.ds((n % per) * rows, rows), :]
        return pltpu.make_async_copy(source, held.at[n % SLOTS], in_sems.at[n % SLOTS])

    def writes(n):
        start, left = pl.multiple_of(target[n], 16), 0
        copies = []
        for k, width in enumerate(widths):
            source = held.at[n % SLOTS, :, pl.ds(left, width)]
            copies.append(pltpu.make_async_copy(source, outs[k].at[pl.ds(start, rows), :], out_sems.at[n % SLOTS, k]))
            left += width
        return copies

    lag = SLOTS // 2
    for n in range(min(lag, count)):
        read(n).start()
    for n in range(count):
        if n >= lag:
            for copy in writes(n - lag):
                copy.wait()
        if n + lag < count:
            read(n + lag).start()
        read(n).wait()
        for copy in writes(n):
            copy.start()
    for n in range(max(count - lag, 0), count):
        for copy in writes(n):
            copy.wait()


class Gather:
    def __init__(self, blocks, seq_first):
        self.rows, self.widths = blocks[0].shape[0], [b.shape[1] for b in blocks]
        fast, height = digits_of("seq")[-1:], digits_of("dp")[:-1]
        self.far = digits_of("seq")[:-1]
        self.near = (fast + height if seq_first else height + fast) + digits_of("dp")[-1:]
        self.buffers = [(jnp.concatenate(blocks, axis=1), ())]

    def values(self):
        return [b for b, _ in self.buffers]

    def wait(self, *others):
        self.buffers = [(after(b, *others), d) for b, d in self.buffers]

    def far_step(self, n):
        (block, digits), digit = self.buffers[0], self.far[n]
        self.buffers = [(jnp.concatenate([block, swap(block, digit)], axis=0), digits + (digit,))]

    def near_step(self, n):
        digit = self.near[n]
        self.buffers = self.buffers + [(swap(b, digit), d + (digit,)) for b, d in self.buffers]

    def finish(self):
        offsets = []
        rows = self.rows
        stride_of = lambda digit: digit[1] * (lax.axis_size("seq") if digit[0] == "dp" else 1)
        for _, digits in self.buffers:
            near = sum(stride_of(d) for d in digits if d not in self.far)
            for n in range(1 << len(self.far)):
                offsets.append(near + sum(stride_of(d) for bit, d in enumerate(self.far) if n >> bit & 1))
        mine = lax.axis_index("dp") * lax.axis_size("seq") + lax.axis_index("seq")
        targets = lax.bitwise_xor(jnp.asarray(offsets, jnp.int32), mine.astype(jnp.int32)) * rows
        count = len(offsets)
        return pl.pallas_call(
            functools.partial(place_kernel, count, rows, self.widths),
            grid_spec=pltpu.PrefetchScalarGridSpec(
                num_scalar_prefetch=1,
                in_specs=[pl.BlockSpec(memory_space=pl.ANY)] * len(self.buffers),
                out_specs=[pl.BlockSpec(memory_space=pl.ANY)] * len(self.widths),
                scratch_shapes=[
                    pltpu.VMEM((SLOTS, rows, sum(self.widths)), bf16),
                    pltpu.SemaphoreType.DMA((SLOTS,)),
                    pltpu.SemaphoreType.DMA((SLOTS, len(self.widths))),
                ],
            ),
            out_shape=[jax.ShapeDtypeStruct((count * rows, width), bf16) for width in self.widths],
            compiler_params=pltpu.CompilerParams(vmem_limit_bytes=16 * 1024 * 1024),
            cost_estimate=pl.CostEstimate(flops=0, bytes_accessed=4 * count * rows * sum(self.widths), transcendentals=0),
            name="place",
        )(targets, *self.values())


def tn(a, b):
    return lax.dot_general(a, b, (((0,), (0,)), ((), ())), preferred_element_type=f32)


def after(value, *others):
    return lax.optimization_barrier((value,) + others)[0]


def pieces_of(side, seq_first):
    dp, seq = lax.axis_size("dp"), lax.axis_size("seq")
    tokens, total = side.shape
    if seq_first:
        pieces = side.reshape(tokens, dp // 2, 2, seq // 2, 2, -1).transpose(2, 0, 4, 1, 3, 5)
    else:
        pieces = side.reshape(tokens, dp // 2, 2, -1).transpose(2, 0, 1, 3)
    return pieces.reshape(2, tokens, total // 2)


class Reduce:
    def __init__(self, pieces, cols_side, seq_first, product=None):
        self.pieces, self.cols_side, self.seq_first, self.product = pieces, cols_side, seq_first, product
        self.half = product.shape[0] // 4 if pieces is None else pieces.shape[2] // 2
        self.own = self.half * 4 // (lax.axis_size("dp") * lax.axis_size("seq"))
        self.core, self.height = digits_of("dp")[-1], digits_of("dp")[0]
        self.fast, self.far = digits_of("seq")[-1], digits_of("seq")[:-1]
        self.first = self.fast if seq_first else self.height
        self.c, self.mine = digit_index(self.core), digit_index(self.first)

    def term(self, core_index, index, others):
        if self.pieces is None:
            parts = pick(after(self.product, *others).reshape(2, 2, self.half, -1), core_index, 1)
            return (parts.reshape(2 * self.half, -1) if index is None else pick(parts, index, 0)).astype(f32)
        side = pick(after(self.pieces, *others), core_index, 0)
        if index is not None:
            side = lax.dynamic_slice_in_dim(side, index * self.half, self.half, 1)
        return tn(side, self.cols_side)

    def cross(self, *others):
        term = self.term(1 - self.c, None, others).astype(bf16)
        self.got = swap(term, self.core)
        return term

    def got_part(self, index):
        return lax.dynamic_slice_in_dim(self.got, index * self.half, self.half, 0).astype(f32)

    def send(self, *others):
        away = (self.term(self.c, 1 - self.mine, others) + self.got_part(1 - self.mine)).astype(bf16)
        self.away = swap(away, self.first)
        return away

    def keep(self, *others):
        total = self.term(self.c, self.mine, others) + self.got_part(self.mine) + self.away.astype(f32)
        self.total = total.astype(bf16)
        return self.total

    def second(self, *others):
        cols = self.cols_side.shape[1]
        total = after(self.total, *others)
        if self.seq_first:
            self.total = scatter_digit(total.reshape(2, -1, cols), self.height, 0, bf16)
        else:
            self.total = scatter_digit(total.reshape(-1, 2, self.own, cols), self.fast, 1, bf16)
        return self.total


class Finish:
    def __init__(self, reduces, *others):
        self.reduces, self.far = reduces, reduces[0].far
        self.count = 1 << len(self.far)
        self.unit = D // (lax.axis_size("dp") * lax.axis_size("seq"))
        totals = [after(r.total, *others).reshape(self.count, self.unit, -1) for r in reduces]
        self.widths = [t.shape[2] for t in totals]
        self.total = jnp.concatenate(totals, axis=2)

    def step(self, n, *others, hold=()):
        total = after(self.total, *others).reshape(-1, 2, self.unit, sum(self.widths))
        self.total = scatter_digit(total, self.far[-1 - n], 1, f32 if n == len(self.far) - 1 else bf16, hold)
        return self.total

    def results(self):
        left = 0
        results = []
        for r, width in zip(self.reduces, self.widths):
            results.append(self.total[0, :, left : left + width].reshape(r.own, -1))
            left += width
        return results


def dot_nt(a, b):
    return lax.dot_general(a, b, (((1,), (1,)), ((), ())), preferred_element_type=f32)


def dot_tn(a, b):
    return lax.dot_general(a, b, (((0,), (0,)), ((), ())), preferred_element_type=f32)


def dot_nn(a, b):
    return lax.dot_general(a, b, (((1,), (0,)), ((), ())), preferred_element_type=f32)


def tile_of(ref, index):
    per = TILE // ref.shape[1]
    return ref[pl.ds(index * per, per)].reshape(TILE, HD)


def mask_of(i, j, lo):
    key = j * TILE + lax.broadcasted_iota(jnp.int32, (TILE, TILE), 0)
    query = i * TILE + lax.broadcasted_iota(jnp.int32, (TILE, TILE), 1)
    return (key >= lo) & (key <= query)


def forward_kernel(bounds, q_ref, k_ref, v_ref, lo_ref, o_ref, lse_ref, acc):
    pair, i = pl.program_id(0), pl.program_id(1)
    q = q_ref[...].reshape(TILE, HD)
    lo = lo_ref[...]
    factor = SCALE * LOG2E

    def step(j, carry, masked):
        m, l = carry
        s = dot_nt(tile_of(k_ref, j), q) * factor
        if masked:
            s = jnp.where(mask_of(i, j, lo), s, MASKED)
        new = jnp.maximum(m, jnp.max(s, axis=0, keepdims=True))
        p = jnp.exp2(s - new)
        old = jnp.exp2(m - new)
        acc[...] = acc[...] * old + dot_tn(tile_of(v_ref, j), p.astype(bf16))
        return new, l * old + jnp.sum(p, axis=0, keepdims=True)

    acc[...] = jnp.zeros_like(acc)
    carry = (jnp.full((1, TILE), MASKED, f32), jnp.zeros((1, TILE), f32))
    start = bounds[pair, 0, i]
    middle = bounds[pair, 1, i]
    carry = lax.fori_loop(start, middle, lambda j, c: step(j, c, True), carry)
    carry = lax.fori_loop(middle, i, lambda j, c: step(j, c, False), carry)
    m, l = step(i, carry, True)
    o_ref[...] = (acc[...] / l).T.astype(bf16).reshape(o_ref.shape)
    lse_ref[...] = m + jnp.log2(l)


def attend(qkv, bounds, low):
    seq, pairs, rows, _ = qkv.shape
    length = seq * rows
    blocks, per = length // TILE, TILE // rows
    whole = lambda part: pl.BlockSpec((seq, None, rows, HD), lambda p, i, b: (0, p, 0, part))
    line = pl.BlockSpec((None, 1, TILE), lambda p, i, b: (p, 0, i))
    block = pl.BlockSpec((per, None, rows, HD), lambda p, i, b: (i, p, 0, 0))
    return pl.pallas_call(
        forward_kernel,
        grid_spec=pltpu.PrefetchScalarGridSpec(
            num_scalar_prefetch=1,
            grid=(pairs, blocks),
            in_specs=[block, whole(1), whole(2), line],
            out_specs=[block, line],
            scratch_shapes=[pltpu.VMEM((HD, TILE), f32)],
        ),
        out_shape=[
            jax.ShapeDtypeStruct((seq, pairs, rows, HD), bf16),
            jax.ShapeDtypeStruct((pairs, 1, length), f32),
        ],
        compiler_params=pltpu.CompilerParams(vmem_limit_bytes=32 * 1024 * 1024),
        cost_estimate=pl.CostEstimate(
            flops=8 * pairs * length * 1792 * HD,
            bytes_accessed=8 * pairs * length * HD,
            transcendentals=pairs * length * 1792,
        ),
        name="attend",
    )(bounds, qkv, qkv, qkv, low)


def backward_kernel(pair, bounds, q_ref, k_ref, v_ref, do_ref, o_ref, lse_ref, lo_ref, out_ref, dq, dk, dv, delta):
    j = pl.program_id(0)
    k = k_ref[...].reshape(TILE, HD)
    v = v_ref[...].reshape(TILE, HD)
    factor = SCALE * LOG2E

    def step(i, masked):
        rows = pl.ds(pl.multiple_of(i * TILE, TILE), TILE)
        q = tile_of(q_ref, i)
        do = tile_of(do_ref, i)
        s = dot_nt(k, q) * factor
        p = jnp.exp2(s - lse_ref[:, rows])
        if masked:
            p = jnp.where(mask_of(i, j, lo_ref[:, rows]), p, 0.0)
        dp = dot_nt(v, do)
        ds = (p * (dp - delta[:, rows])).astype(bf16)
        dv[...] += dot_nn(p.astype(bf16), do)
        dk[...] += dot_nn(ds, q)
        dq[rows, :] += dot_tn(ds, k)

    @pl.when(j == 0)
    def _():
        dq[...] = jnp.zeros_like(dq)

        @pl.loop(0, pl.num_programs(0))
        def _(i):
            rows = pl.ds(pl.multiple_of(i * TILE, TILE), TILE)
            product = tile_of(do_ref, i).astype(f32) * tile_of(o_ref, i).astype(f32)
            delta[:, rows] = jnp.sum(product.T, axis=0, keepdims=True)

    dk[...] = jnp.zeros_like(dk)
    dv[...] = jnp.zeros_like(dv)
    step(j, True)
    middle = bounds[pair, 2, j]
    end = bounds[pair, 3, j]

    @pl.loop(j + 1, middle)
    def _(i):
        step(i, False)

    @pl.loop(middle, end)
    def _(i):
        step(i, True)

    own = pl.ds(pl.multiple_of(j * TILE, TILE), TILE)
    shape = out_ref.shape[:-1] + (HD,)
    out_ref[:, :, :HD] = (dq[own, :] * SCALE).astype(bf16).reshape(shape)
    out_ref[:, :, HD : 2 * HD] = (dk[...] * SCALE).astype(bf16).reshape(shape)
    out_ref[:, :, 2 * HD :] = dv[...].astype(bf16).reshape(shape)


def attend_back(pair, qkv, grad, mixed, lse, bounds, low):
    seq, _, rows, _ = qkv.shape
    length = seq * rows
    blocks, per = length // TILE, TILE // rows
    whole = pl.BlockSpec((seq, None, rows, HD), lambda j, b: (0, pair, 0, 0))
    line = pl.BlockSpec((None, 1, length), lambda j, b: (pair, 0, 0))
    block = lambda part: pl.BlockSpec((per, None, rows, HD), lambda j, b: (j, pair, 0, part))
    return pl.pallas_call(
        functools.partial(backward_kernel, pair),
        grid_spec=pltpu.PrefetchScalarGridSpec(
            num_scalar_prefetch=1,
            grid=(blocks,),
            in_specs=[whole, block(1), block(2), whole, whole, line, line],
            out_specs=pl.BlockSpec((per, None, rows, 3 * HD), lambda j, b: (j, 0, 0, 0)),
            scratch_shapes=[
                pltpu.VMEM((length, HD), f32),
                pltpu.VMEM((TILE, HD), f32),
                pltpu.VMEM((TILE, HD), f32),
                pltpu.VMEM((1, length), f32),
            ],
        ),
        out_shape=jax.ShapeDtypeStruct((seq, 1, rows, 3 * HD), bf16),
        compiler_params=pltpu.CompilerParams(vmem_limit_bytes=40 * 1024 * 1024),
        cost_estimate=pl.CostEstimate(
            flops=20 * length * 1792 * HD,
            bytes_accessed=16 * length * HD,
            transcendentals=length * 1792,
        ),
        name="attend_back",
    )(bounds, qkv, qkv, qkv, grad, mixed, lse, low)


def key_bounds(segments):
    length = segments.shape[0]
    blocks = length // TILE
    place = jnp.arange(length, dtype=jnp.int32)
    start = jnp.zeros_like(place)
    for value in range(1, 4):
        earlier = jnp.sum(segments < value, dtype=jnp.int32)
        start = jnp.where(segments == value, earlier, start)
    low = jnp.maximum(start, place - (WINDOW - 1))
    index = jnp.arange(blocks, dtype=jnp.int32)
    first = low[::TILE]
    last = low[TILE - 1 :: TILE]
    begin = first // TILE
    middle = jnp.clip((last + TILE - 1) // TILE, begin, index)
    full = (last[None, :] <= index[:, None] * TILE) & (index[None, :] > index[:, None])
    some = (first[None, :] < (index[:, None] + 1) * TILE) & (index[None, :] > index[:, None])
    back_middle = index + 1 + jnp.sum(full, axis=1, dtype=jnp.int32)
    back_end = index + 1 + jnp.sum(some, axis=1, dtype=jnp.int32)
    return low[None], jnp.stack([begin, middle, back_middle, back_end])


def to_heads(rows, micros):
    seq = lax.axis_size("seq")
    count, width = rows.shape[0] // micros, rows.shape[1] // H
    split = rows.reshape(micros, count, H, width).transpose(2, 0, 1, 3)
    split = split.reshape(seq, H * micros // seq, count, width)
    return lax.all_to_all(split, "seq", 0, 0, tiled=True)


def to_rows(whole):
    return lax.all_to_all(whole, "seq", 0, 0, tiled=True)


def rows_of(got, micros):
    count, width = got.shape[2], got.shape[3]
    return got.reshape(H, micros, count, width).transpose(1, 2, 0, 3).reshape(micros * count, H * width)


def norm_scale(values):
    return lax.rsqrt(jnp.mean(values * values, axis=-1, keepdims=True) + EPSILON)


def norm_backward(grad_in, values, row_scale, gain):
    normed = values * row_scale
    gain_grad = jnp.sum(grad_in * normed, axis=0)
    scaled = grad_in * gain
    inner = jnp.mean(scaled * normed, axis=-1, keepdims=True)
    return row_scale * (scaled - normed * inner), gain_grad


def nt(a, b):
    return jnp.einsum("re,de->rd", a, b, preferred_element_type=f32)


def shards(tokens, segment_ids, w_qkv, w_out, w_gate_up, w_down, gain_attn, gain_mlp, cotangent):
    rows = tokens.shape[2]
    seq = lax.axis_size("seq")
    gather = lambda w: lax.all_gather(w, ("dp", "seq"), axis=0, tiled=True)
    groups = MB if H % seq == 0 else 1
    micros = MB // groups
    pairs = H * micros // seq
    size = micros * rows
    of = lambda array, g: array[g * size : (g + 1) * size]

    x = tokens.reshape(MB * rows, D).astype(f32)
    cot = cotangent.reshape(MB * rows, D)
    bounds, low = [], []
    for g in range(groups):
        made = []
        for k in range(pairs):
            micro = g if micros == 1 else lax.rem(lax.axis_index("seq") * pairs + k, micros)
            made.append(key_bounds(segment_ids[g, 0] if micros == 1 else pick(segment_ids[:, 0], micro, 0)))
        low.append(jnp.stack([m[0] for m in made]))
        bounds.append(jnp.stack([m[1] for m in made]))

    order_qkv = w_qkv.reshape(-1, 3, H, HD).transpose(0, 2, 1, 3).reshape(w_qkv.shape)
    full_qkv = gather(order_qkv)
    all_gains = gather_small(jnp.stack([gain_attn, gain_mlp]))
    gains = all_gains.astype(f32)
    gain_a, gain_m = gains[0], gains[1]
    scale_a = norm_scale(x)
    h_attn = (x * scale_a * gain_a).astype(bf16)
    soon = Gather([w_gate_up[:, :FF], w_out], False)
    later = Gather([w_gate_up[:, FF:], w_down.reshape(w_qkv.shape[0], -1)], True)
    far = len(soon.far)

    soon.wait(all_gains)
    soon.far_step(0)
    for n in range(1, far):
        later.wait(*soon.values())
        soon.far_step(n)
        later.far_step(n - 1)
    ready = soon.values() + later.values()
    soon.wait(*ready)
    soon.near_step(0)
    later.wait(*ready)
    later.far_step(far - 1)
    step_in = after(h_attn, *later.values())
    later.near_step(0)
    saved, attended, arrived = [], [], []
    for g in range(groups):
        qkv_rows = jnp.dot(of(step_in, g), full_qkv, preferred_element_type=f32).astype(bf16)
        qkv = to_heads(qkv_rows, micros)
        if g == 0:
            ready = soon.values() + later.values()
            qkv = after(qkv, *ready)
            soon.wait(*ready)
            soon.near_step(1)
            later.wait(*ready)
            later.near_step(1)
        else:
            qkv = after(qkv, gate_first)
        mixed, lse = attend(qkv, bounds[g], low[g])
        saved.append((qkv, mixed, lse))
        attended.append(rows_of(to_rows(mixed), micros))
        if g == 0:
            step_in = after(h_attn, attended[0])
            soon.near_step(2)
            full_gate, full_out = soon.finish()

            mid_first = of(x, 0) + jnp.dot(attended[0], full_out, preferred_element_type=f32)
            scale_first = norm_scale(mid_first)
            h_first = (mid_first * scale_first * gain_m).astype(bf16)
            gate_first = jnp.dot(h_first, full_gate, preferred_element_type=f32)
            later.near_step(2)
    later.wait(gate_first)
    full_up, full_down = later.finish()
    full_down = full_down.reshape(FF, D)

    parts = []
    grads = []
    rows_grad = []
    mark = (mixed,)

    def back_of(g, *others):
        qkv, mixed, lse = saved[g]
        pieces = []
        for k in range(pairs):
            back = attend_back(k, after(qkv, *others), grads[g], mixed, lse, bounds[g], low[g])
            others = (back,)
            pieces.append(to_rows(back))
        rows_grad.append(pieces)
        return back

    for g in range(groups):
        final = g == groups - 1
        if g == 0:
            mid, scale_m, h_mlp, gate = mid_first, scale_first, h_first, gate_first
        else:
            mid = of(x, g) + jnp.dot(after(attended[g], *mark), full_out, preferred_element_type=f32)
            scale_m = norm_scale(mid)
            h_mlp = (mid * scale_m * gain_m).astype(bf16)
            gate = jnp.dot(h_mlp, full_gate, preferred_element_type=f32)
        up = jnp.dot(after(h_mlp, *mark), full_up, preferred_element_type=f32)
        sig = jax.nn.sigmoid(gate)
        act = (gate * sig * up).astype(bf16)
        parts.append([mid, scale_m, h_mlp, act])
        mark = (act,)
        if g:
            mark = (back_of(g - 1, *mark),)
        if final:
            acts = jnp.concatenate([p[3] for p in parts], axis=0)
            sides = jnp.concatenate([p[2] for p in parts], axis=0)
            down = Reduce(None, cot, False, product=tn(after(acts, *mark), cot).astype(bf16))
            mark = (down.cross(),)
        if g:
            mark = mark + (rows_grad[-1][0],)
        cot_part = of(cot, g)
        grad_act = nt(after(cot_part, *mark), full_down)
        grad_gate = (grad_act * up * sig * (1.0 + gate * (1.0 - sig))).astype(bf16)
        grad_up = (grad_act * (gate * sig)).astype(bf16)
        parts[g] += [grad_gate, grad_up]
        mark = (grad_gate, grad_up)
        if final:
            mark = (down.send(*mark),)
            gate_r = Reduce(pieces_of(sides, False), jnp.concatenate([p[4] for p in parts], axis=0), False)
            up_r = Reduce(pieces_of(sides, True), jnp.concatenate([p[5] for p in parts], axis=0), True)
            mark = (up_r.cross(*mark),)
            mark = (gate_r.cross(*mark),)
        half_grad = nt(after(grad_gate, *mark), full_gate)
        mark = (half_grad,)
        if final:
            mark = (up_r.send(*mark),)
        grad_h_mlp = half_grad + nt(after(grad_up, *mark), full_up)
        grad_mid_norm, gain_part = norm_backward(grad_h_mlp, mid, scale_m, gain_m)
        grad_mid = cot_part.astype(f32) + grad_mid_norm
        grad_branch = grad_mid.astype(bf16)
        grad_rows = nt(after(grad_branch, *[r for pieces in rows_grad for r in pieces]), full_out).astype(bf16)
        grads.append(to_heads(grad_rows, micros))
        parts[g] += [grad_mid, grad_branch, gain_part]
        mark = (grad_rows,)

    attended_all = jnp.concatenate(attended, axis=0)
    out_r = Reduce(pieces_of(attended_all, False), jnp.concatenate([p[7] for p in parts], axis=0), False)
    early = [down, up_r, gate_r, out_r]
    mark = (gate_r.send(*mark),)
    mark = (out_r.cross(*mark),)
    mark = (down.keep(*mark),)
    down.second()
    mark = (back_of(groups - 1, *mark),)
    mark = (up_r.keep(*mark),)
    up_r.second()
    mark = (out_r.send(*mark), rows_grad[-1][0])
    for r in (gate_r, out_r):
        mark = (r.keep(*mark),)
        r.second()
    layer_outs, grad_qkv, grad_tokens, gain_a_parts = [], [], [], []

    def finish_tokens(g, *others):
        grad_h_attn = nt(after(grad_qkv[g], *others), full_qkv)
        grad_norm, gain_part = norm_backward(grad_h_attn, of(x, g), of(scale_a, g), gain_a)
        grad_tokens.append(parts[g][6] + grad_norm)
        gain_a_parts.append(gain_part)
        return grad_tokens[-1]

    for g in range(groups):
        act = after(parts[g][3], *mark)
        layer_outs.append((parts[g][0] + jnp.dot(act, full_down, preferred_element_type=f32)).astype(bf16))
        mark = (layer_outs[-1],)
    mark = mark + tuple(rows_grad[-1])
    first = Finish(early, *mark)
    first.step(0)
    h_sides = [pieces_of(h_attn, False), pieces_of(h_attn, True)]
    for g in range(groups - 1):
        grad_qkv.append(rows_of(jnp.concatenate(rows_grad[g], axis=1), micros))
    grad_qkv.append(rows_of(jnp.concatenate([after(r, *mark) for r in rows_grad[-1]], axis=1), micros))
    last_rows = grad_qkv[-1]
    all_qkv = jnp.concatenate(grad_qkv, axis=0)
    half = 3 * D // 2
    late = [Reduce(h_sides[0], all_qkv[:, :half], False), Reduce(h_sides[1], all_qkv[:, half:], True)]
    for r in late:
        mark = (r.cross(*mark),)
    for g in range(groups - 1):
        mark = (finish_tokens(g, *mark),)
    for r in late:
        mark = (r.send(*mark),)
    mark = mark + (first.total,)
    g = groups - 1
    grad_h_attn = nt(after(last_rows, *mark), full_qkv)
    grad_norm, gain_part = norm_backward(grad_h_attn, of(x, g), of(scale_a, g), gain_a)
    grad_tokens.append(parts[g][6] + grad_norm)
    gain_a_parts.append(gain_part)
    mark = (grad_tokens[-1],)
    for r in late:
        mark = (r.keep(*mark),)
    for r in late:
        r.second(*mark)
    gain_grads = scatter_small(jnp.stack([sum(gain_a_parts), sum(p[8] for p in parts)]))
    second = Finish(late)
    for n in range(far):
        if n:
            first.step(n, hold=mark)
        second.step(n)
    down_grad, up_grad, gate_grad, out_grad = first.results()
    qkv_grad = jnp.concatenate(second.results(), axis=1).reshape(-1, H, 3, HD).transpose(0, 2, 1, 3)
    join = lambda arrays: jnp.concatenate(arrays, axis=0).reshape(MB, 1, rows, D)

    return (
        join(layer_outs),
        join(grad_tokens),
        qkv_grad.reshape(-1, 3 * D),
        out_grad,
        jnp.concatenate([gate_grad, up_grad], axis=1),
        down_grad,
        gain_grads[0],
        gain_grads[1],
    )


def solution(mesh):
    by_rows = P(("dp", "seq"), None)
    by_tokens = P(None, "dp", "seq", None)
    vector = P(("dp", "seq"))
    return jax.shard_map(
        shards,
        mesh=mesh,
        in_specs=(by_tokens, P(None, "dp", None), by_rows, by_rows, by_rows, by_rows, vector, vector, by_tokens),
        out_specs=(by_tokens, by_tokens, by_rows, by_rows, by_rows, by_rows, vector, vector),
        check_vma=False,
    )
```

```python
import functools
import math

import jax
import jax.numpy as jnp
from jax import lax
from jax.experimental import pallas as pl
from jax.experimental.pallas import tpu as pltpu
from jax.sharding import PartitionSpec as P

D = 2048
H = 16
HD = 128
FF = 5504
WINDOW = 2048
MB = 2
TILE = 512

EPSILON = 1e-05
MASKED = -1e30
LOG2E = 1.4426950408889634
SCALE = 1.0 / math.sqrt(HD)

QUICK = pl.CostEstimate(flops=1024, bytes_accessed=1024, transcendentals=0)

bf16 = jnp.bfloat16
f32 = jnp.float32


def digits_of(axis):
    size = lax.axis_size(axis)
    return [(axis, 1 << bit) for bit in reversed(range(size.bit_length() - 1))]


def digit_index(digit):
    axis, stride = digit
    return lax.rem(lax.axis_index(axis) // stride, 2)


def swap(block, digit):
    axis, stride = digit
    return lax.ppermute(block, axis, [(i, i ^ stride) for i in range(lax.axis_size(axis))])


def pick(array, index, dim):
    return lax.dynamic_index_in_dim(array, index, dim, keepdims=False)


def scatter_digit(parts, digit, dim, out_type, hold=()):
    own = digit_index(digit)
    got = swap(pick(parts, 1 - own, dim), digit)
    if hold:
        got = lax.optimization_barrier((got,) + tuple(hold))[0]
    return (pick(parts, own, dim).astype(f32) + got.astype(f32)).astype(out_type)


def gather_small(block):
    for digit in reversed(digits_of("dp") + digits_of("seq")):
        got = swap(block, digit)
        low = digit_index(digit) == 0
        block = jnp.concatenate([jnp.where(low, block, got), jnp.where(low, got, block)], axis=-1)
    return block


class ScatterSmall:
    def __init__(self, terms):
        self.digits = digits_of("dp") + digits_of("seq")
        self.terms = terms.reshape((terms.shape[0],) + (2,) * len(self.digits) + (-1,))
        for digit in digits_of("dp")[::-1] + digits_of("seq")[-1:]:
            self.step(digit)

    def step(self, digit, *others):
        dim = 1 + self.digits.index(digit)
        self.digits = [d for d in self.digits if d != digit]
        self.terms = scatter_digit(after(self.terms, *others), digit, dim, f32)


SLOTS = 8


def place_kernel(count, rows, widths, target, *refs):
    sources, outs = refs[: -3 - len(widths)], refs[-3 - len(widths) : -3]
    held, in_sems, out_sems = refs[-3:]
    per = sources[0].shape[0] // rows

    def read(n):
        source = sources[n // per].at[pl.ds((n % per) * rows, rows), :]
        return pltpu.make_async_copy(source, held.at[n % SLOTS], in_sems.at[n % SLOTS])

    def writes(n):
        start, left = pl.multiple_of(target[n], 16), 0
        copies = []
        for k, width in enumerate(widths):
            source = held.at[n % SLOTS, :, pl.ds(left, width)]
            copies.append(pltpu.make_async_copy(source, outs[k].at[pl.ds(start, rows), :], out_sems.at[n % SLOTS, k]))
            left += width
        return copies

    lag = SLOTS // 2
    for n in range(min(lag, count)):
        read(n).start()
    for n in range(count):
        if n >= lag:
            for copy in writes(n - lag):
                copy.wait()
        if n + lag < count:
            read(n + lag).start()
        read(n).wait()
        for copy in writes(n):
            copy.start()
    for n in range(max(count - lag, 0), count):
        for copy in writes(n):
            copy.wait()


class Gather:
    def __init__(self, blocks, seq_first):
        self.rows, self.widths = blocks[0].shape[0], [b.shape[1] for b in blocks]
        fast, height = digits_of("seq")[-1:], digits_of("dp")[:-1]
        self.far = digits_of("seq")[:-1]
        self.near = (fast + height if seq_first else height + fast) + digits_of("dp")[-1:]
        self.buffers = [(jnp.concatenate(blocks, axis=1), ())]

    def values(self):
        return [b for b, _ in self.buffers]

    def wait(self, *others):
        self.buffers = [(after(b, *others), d) for b, d in self.buffers]

    def far_step(self, n):
        (block, digits), digit = self.buffers[0], self.far[n]
        self.buffers = [(jnp.concatenate([block, swap(block, digit)], axis=0), digits + (digit,))]

    def near_step(self, n):
        digit = self.near[n]
        self.buffers = self.buffers + [(swap(b, digit), d + (digit,)) for b, d in self.buffers]

    def finish(self):
        offsets = []
        rows = self.rows
        stride_of = lambda digit: digit[1] * (lax.axis_size("seq") if digit[0] == "dp" else 1)
        for _, digits in self.buffers:
            near = sum(stride_of(d) for d in digits if d not in self.far)
            for n in range(1 << len(self.far)):
                offsets.append(near + sum(stride_of(d) for bit, d in enumerate(self.far) if n >> bit & 1))
        mine = lax.axis_index("dp") * lax.axis_size("seq") + lax.axis_index("seq")
        targets = lax.bitwise_xor(jnp.asarray(offsets, jnp.int32), mine.astype(jnp.int32)) * rows
        count = len(offsets)
        return pl.pallas_call(
            functools.partial(place_kernel, count, rows, self.widths),
            grid_spec=pltpu.PrefetchScalarGridSpec(
                num_scalar_prefetch=1,
                in_specs=[pl.BlockSpec(memory_space=pl.ANY)] * len(self.buffers),
                out_specs=[pl.BlockSpec(memory_space=pl.ANY)] * len(self.widths),
                scratch_shapes=[
                    pltpu.VMEM((SLOTS, rows, sum(self.widths)), bf16),
                    pltpu.SemaphoreType.DMA((SLOTS,)),
                    pltpu.SemaphoreType.DMA((SLOTS, len(self.widths))),
                ],
            ),
            out_shape=[jax.ShapeDtypeStruct((count * rows, width), bf16) for width in self.widths],
            compiler_params=pltpu.CompilerParams(vmem_limit_bytes=16 * 1024 * 1024),
            cost_estimate=QUICK,
            name="place",
        )(targets, *self.values())


def tn(a, b):
    return lax.dot_general(a, b, (((0,), (0,)), ((), ())), preferred_element_type=f32)


def after(value, *others):
    return lax.optimization_barrier((value,) + others)[0]


def pieces_of(side, seq_first):
    dp, seq = lax.axis_size("dp"), lax.axis_size("seq")
    tokens, total = side.shape
    if seq_first:
        pieces = side.reshape(tokens, dp // 2, 2, seq // 2, 2, -1).transpose(2, 0, 4, 1, 3, 5)
    else:
        pieces = side.reshape(tokens, dp // 2, 2, -1).transpose(2, 0, 1, 3)
    return pieces.reshape(2, tokens, total // 2)


class Reduce:
    def __init__(self, pieces, cols_side, seq_first, product=None):
        self.pieces, self.cols_side, self.seq_first, self.product = pieces, cols_side, seq_first, product
        self.half = product.shape[0] // 4 if pieces is None else pieces.shape[2] // 2
        self.own = self.half * 4 // (lax.axis_size("dp") * lax.axis_size("seq"))
        self.core, self.height = digits_of("dp")[-1], digits_of("dp")[0]
        self.fast, self.far = digits_of("seq")[-1], digits_of("seq")[:-1]
        self.first = self.fast if seq_first else self.height
        self.c, self.mine = digit_index(self.core), digit_index(self.first)

    def term(self, core_index, index, others):
        if self.pieces is None:
            parts = pick(after(self.product, *others).reshape(2, 2, self.half, -1), core_index, 1)
            return (parts.reshape(2 * self.half, -1) if index is None else pick(parts, index, 0)).astype(f32)
        side = pick(after(self.pieces, *others), core_index, 0)
        if index is not None:
            side = lax.dynamic_slice_in_dim(side, index * self.half, self.half, 1)
        return tn(side, self.cols_side)

    def cross(self, *others):
        term = self.term(1 - self.c, None, others).astype(bf16)
        self.got = swap(term, self.core)
        return term

    def got_part(self, index):
        return lax.dynamic_slice_in_dim(self.got, index * self.half, self.half, 0).astype(f32)

    def send(self, *others):
        away = (self.term(self.c, 1 - self.mine, others) + self.got_part(1 - self.mine)).astype(bf16)
        self.away = swap(away, self.first)
        return away

    def keep(self, *others):
        total = self.term(self.c, self.mine, others) + self.got_part(self.mine) + self.away.astype(f32)
        self.total = total.astype(bf16)
        return self.total

    def second(self, *others):
        cols = self.cols_side.shape[1]
        total = after(self.total, *others)
        if self.seq_first:
            self.total = scatter_digit(total.reshape(2, -1, cols), self.height, 0, bf16)
        else:
            self.total = scatter_digit(total.reshape(-1, 2, self.own, cols), self.fast, 1, bf16)
        return self.total


class Finish:
    def __init__(self, reduces, *others):
        self.reduces, self.far = reduces, reduces[0].far
        self.count = 1 << len(self.far)
        self.unit = D // (lax.axis_size("dp") * lax.axis_size("seq"))
        totals = [after(r.total, *others).reshape(self.count, self.unit, -1) for r in reduces]
        self.widths = [t.shape[2] for t in totals]
        self.total = jnp.concatenate(totals, axis=2)

    def step(self, n, *others, hold=()):
        total = after(self.total, *others).reshape(-1, 2, self.unit, sum(self.widths))
        self.total = scatter_digit(total, self.far[-1 - n], 1, f32 if n == len(self.far) - 1 else bf16, hold)
        return self.total

    def results(self):
        left = 0
        results = []
        for r, width in zip(self.reduces, self.widths):
            results.append(self.total[0, :, left : left + width].reshape(r.own, -1))
            left += width
        return results


def dot_nt(a, b):
    return lax.dot_general(a, b, (((1,), (1,)), ((), ())), preferred_element_type=f32)


def dot_tn(a, b):
    return lax.dot_general(a, b, (((0,), (0,)), ((), ())), preferred_element_type=f32)


def dot_nn(a, b):
    return lax.dot_general(a, b, (((1,), (0,)), ((), ())), preferred_element_type=f32)


def tile_of(ref, index):
    per = TILE // ref.shape[1]
    return ref[pl.ds(index * per, per)].reshape(TILE, HD)


def mask_of(i, j, lo):
    key = j * TILE + lax.broadcasted_iota(jnp.int32, (TILE, TILE), 0)
    query = i * TILE + lax.broadcasted_iota(jnp.int32, (TILE, TILE), 1)
    return (key >= lo) & (key <= query)


def forward_kernel(bounds, q_ref, k_ref, v_ref, lo_ref, o_ref, lse_ref, acc):
    pair, i = pl.program_id(0), pl.program_id(1)
    q = q_ref[...].reshape(TILE, HD)
    lo = lo_ref[...]
    factor = SCALE * LOG2E

    def step(j, carry, masked):
        m, l = carry
        s = dot_nt(tile_of(k_ref, j), q) * factor
        if masked:
            s = jnp.where(mask_of(i, j, lo), s, MASKED)
        new = jnp.maximum(m, jnp.max(s, axis=0, keepdims=True))
        p = jnp.exp2(s - new)
        old = jnp.exp2(m - new)
        acc[...] = acc[...] * old + dot_tn(tile_of(v_ref, j), p.astype(bf16))
        return new, l * old + jnp.sum(p, axis=0, keepdims=True)

    acc[...] = jnp.zeros_like(acc)
    carry = (jnp.full((1, TILE), MASKED, f32), jnp.zeros((1, TILE), f32))
    start = bounds[pair, 0, i]
    middle = bounds[pair, 1, i]
    carry = lax.fori_loop(start, middle, lambda j, c: step(j, c, True), carry)
    carry = lax.fori_loop(middle, i, lambda j, c: step(j, c, False), carry)
    m, l = step(i, carry, True)
    o_ref[...] = (acc[...] / l).T.astype(bf16).reshape(o_ref.shape)
    lse_ref[...] = m + jnp.log2(l)


def attend(qkv, bounds, low):
    seq, pairs, rows, _ = qkv.shape
    length = seq * rows
    blocks, per = length // TILE, TILE // rows
    whole = lambda part: pl.BlockSpec((seq, None, rows, HD), lambda p, i, b: (0, p, 0, part))
    line = pl.BlockSpec((None, 1, TILE), lambda p, i, b: (p, 0, i))
    block = pl.BlockSpec((per, None, rows, HD), lambda p, i, b: (i, p, 0, 0))
    return pl.pallas_call(
        forward_kernel,
        grid_spec=pltpu.PrefetchScalarGridSpec(
            num_scalar_prefetch=1,
            grid=(pairs, blocks),
            in_specs=[block, whole(1), whole(2), line],
            out_specs=[block, line],
            scratch_shapes=[pltpu.VMEM((HD, TILE), f32)],
        ),
        out_shape=[
            jax.ShapeDtypeStruct((seq, pairs, rows, HD), bf16),
            jax.ShapeDtypeStruct((pairs, 1, length), f32),
        ],
        compiler_params=pltpu.CompilerParams(vmem_limit_bytes=32 * 1024 * 1024),
        cost_estimate=QUICK,
        name="attend",
    )(bounds, qkv, qkv, qkv, low)


def backward_kernel(pair, bounds, q_ref, k_ref, v_ref, do_ref, o_ref, lse_ref, lo_ref, out_ref, dq, dk, dv, delta):
    j = pl.program_id(0)
    k = k_ref[...].reshape(TILE, HD)
    v = v_ref[...].reshape(TILE, HD)
    factor = SCALE * LOG2E

    def step(i, masked):
        rows = pl.ds(pl.multiple_of(i * TILE, TILE), TILE)
        q = tile_of(q_ref, i)
        do = tile_of(do_ref, i)
        s = dot_nt(k, q) * factor
        p = jnp.exp2(s - lse_ref[:, rows])
        if masked:
            p = jnp.where(mask_of(i, j, lo_ref[:, rows]), p, 0.0)
        dp = dot_nt(v, do)
        ds = (p * (dp - delta[:, rows])).astype(bf16)
        dv[...] += dot_nn(p.astype(bf16), do)
        dk[...] += dot_nn(ds, q)
        dq[rows, :] += dot_tn(ds, k)

    @pl.when(j == 0)
    def _():
        dq[...] = jnp.zeros_like(dq)

        @pl.loop(0, pl.num_programs(0))
        def _(i):
            rows = pl.ds(pl.multiple_of(i * TILE, TILE), TILE)
            product = tile_of(do_ref, i).astype(f32) * tile_of(o_ref, i).astype(f32)
            delta[:, rows] = jnp.sum(product.T, axis=0, keepdims=True)

    dk[...] = jnp.zeros_like(dk)
    dv[...] = jnp.zeros_like(dv)
    step(j, True)
    middle = bounds[pair, 2, j]
    end = bounds[pair, 3, j]

    @pl.loop(j + 1, middle)
    def _(i):
        step(i, False)

    @pl.loop(middle, end)
    def _(i):
        step(i, True)

    own = pl.ds(pl.multiple_of(j * TILE, TILE), TILE)
    shape = out_ref.shape[:-1] + (HD,)
    out_ref[:, :, :HD] = (dq[own, :] * SCALE).astype(bf16).reshape(shape)
    out_ref[:, :, HD : 2 * HD] = (dk[...] * SCALE).astype(bf16).reshape(shape)
    out_ref[:, :, 2 * HD :] = dv[...].astype(bf16).reshape(shape)


def attend_back(pair, qkv, grad, mixed, lse, bounds, low):
    seq, _, rows, _ = qkv.shape
    length = seq * rows
    blocks, per = length // TILE, TILE // rows
    whole = pl.BlockSpec((seq, None, rows, HD), lambda j, b: (0, pair, 0, 0))
    line = pl.BlockSpec((None, 1, length), lambda j, b: (pair, 0, 0))
    block = lambda part: pl.BlockSpec((per, None, rows, HD), lambda j, b: (j, pair, 0, part))
    return pl.pallas_call(
        functools.partial(backward_kernel, pair),
        grid_spec=pltpu.PrefetchScalarGridSpec(
            num_scalar_prefetch=1,
            grid=(blocks,),
            in_specs=[whole, block(1), block(2), whole, whole, line, line],
            out_specs=pl.BlockSpec((per, None, rows, 3 * HD), lambda j, b: (j, 0, 0, 0)),
            scratch_shapes=[
                pltpu.VMEM((length, HD), f32),
                pltpu.VMEM((TILE, HD), f32),
                pltpu.VMEM((TILE, HD), f32),
                pltpu.VMEM((1, length), f32),
            ],
        ),
        out_shape=jax.ShapeDtypeStruct((seq, 1, rows, 3 * HD), bf16),
        compiler_params=pltpu.CompilerParams(vmem_limit_bytes=40 * 1024 * 1024),
        cost_estimate=QUICK,
        name="attend_back",
    )(bounds, qkv, qkv, qkv, grad, mixed, lse, low)


def key_bounds(segments):
    length = segments.shape[0]
    blocks = length // TILE
    place = jnp.arange(length, dtype=jnp.int32)
    start = jnp.zeros_like(place)
    for value in range(1, 4):
        earlier = jnp.sum(segments < value, dtype=jnp.int32)
        start = jnp.where(segments == value, earlier, start)
    low = jnp.maximum(start, place - (WINDOW - 1))
    index = jnp.arange(blocks, dtype=jnp.int32)
    first = low[::TILE]
    last = low[TILE - 1 :: TILE]
    begin = first // TILE
    middle = jnp.clip((last + TILE - 1) // TILE, begin, index)
    full = (last[None, :] <= index[:, None] * TILE) & (index[None, :] > index[:, None])
    some = (first[None, :] < (index[:, None] + 1) * TILE) & (index[None, :] > index[:, None])
    back_middle = index + 1 + jnp.sum(full, axis=1, dtype=jnp.int32)
    back_end = index + 1 + jnp.sum(some, axis=1, dtype=jnp.int32)
    return low[None], jnp.stack([begin, middle, back_middle, back_end])


def to_heads(rows, micros):
    seq = lax.axis_size("seq")
    count, width = rows.shape[0] // micros, rows.shape[1] // H
    split = rows.reshape(micros, count, H, width).transpose(2, 0, 1, 3)
    split = split.reshape(seq, H * micros // seq, count, width)
    return lax.all_to_all(split, "seq", 0, 0, tiled=True)


def to_rows(whole):
    return lax.all_to_all(whole, "seq", 0, 0, tiled=True)


def rows_of(got, micros):
    count, width = got.shape[2], got.shape[3]
    return got.reshape(H, micros, count, width).transpose(1, 2, 0, 3).reshape(micros * count, H * width)


def norm_scale(values):
    return lax.rsqrt(jnp.mean(values * values, axis=-1, keepdims=True) + EPSILON)


def norm_backward(grad_in, values, row_scale, gain):
    normed = values * row_scale
    gain_grad = jnp.sum(grad_in * normed, axis=0)
    scaled = grad_in * gain
    inner = jnp.mean(scaled * normed, axis=-1, keepdims=True)
    return row_scale * (scaled - normed * inner), gain_grad


def nt(a, b):
    return jnp.einsum("re,de->rd", a, b, preferred_element_type=f32)


def shards(tokens, segment_ids, w_qkv, w_out, w_gate_up, w_down, gain_attn, gain_mlp, cotangent):
    rows = tokens.shape[2]
    seq = lax.axis_size("seq")
    gather = lambda w: lax.all_gather(w, ("dp", "seq"), axis=0, tiled=True)
    groups = MB if H % seq == 0 else 1
    micros = MB // groups
    pairs = H * micros // seq
    size = micros * rows
    of = lambda array, g: array[g * size : (g + 1) * size]

    x = tokens.reshape(MB * rows, D).astype(f32)
    cot = cotangent.reshape(MB * rows, D)
    bounds, low = [], []
    for g in range(groups):
        made = []
        for k in range(pairs):
            micro = g if micros == 1 else lax.rem(lax.axis_index("seq") * pairs + k, micros)
            made.append(key_bounds(segment_ids[g, 0] if micros == 1 else pick(segment_ids[:, 0], micro, 0)))
        low.append(jnp.stack([m[0] for m in made]))
        bounds.append(jnp.stack([m[1] for m in made]))

    order_qkv = w_qkv.reshape(-1, 3, H, HD).transpose(0, 2, 1, 3).reshape(w_qkv.shape)
    full_qkv = gather(order_qkv)
    all_gains = gather_small(jnp.stack([gain_attn, gain_mlp]))
    gains = all_gains.astype(f32)
    gain_a, gain_m = gains[0], gains[1]
    scale_a = norm_scale(x)
    h_attn = (x * scale_a * gain_a).astype(bf16)
    soon = Gather([w_gate_up[:, :FF], w_out], False)
    later = Gather([w_gate_up[:, FF:], w_down.reshape(w_qkv.shape[0], -1)], True)
    far = len(soon.far)

    soon.wait(all_gains)
    soon.far_step(0)
    for n in range(1, far):
        later.wait(*soon.values())
        soon.far_step(n)
        later.far_step(n - 1)
    ready = soon.values() + later.values()
    soon.wait(*ready)
    soon.near_step(0)
    later.wait(*ready)
    later.far_step(far - 1)
    later.wait(*soon.values())
    later.near_step(0)
    h_kept = step_in = after(h_attn, *later.values())
    saved, attended, arrived = [], [], []
    for g in range(groups):
        qkv_rows = jnp.dot(of(step_in, g), full_qkv, preferred_element_type=f32).astype(bf16)
        qkv = to_heads(qkv_rows, micros)
        if g == 0:
            ready = soon.values() + later.values()
            for w in (soon, later):
                w.wait(*ready)
                w.near_step(1)
            qkv = after(qkv, *soon.values(), *later.values())
        else:
            qkv = after(qkv, gate_first)
        mixed, lse = attend(qkv, bounds[g], low[g])
        saved.append((qkv, mixed, lse))
        attended.append(rows_of(to_rows(mixed), micros))
        if g == 0:
            soon.near_step(2)
            later.near_step(2)
            step_in = after(h_kept, attended[0], *soon.values(), *later.values())
            full_gate, full_out = soon.finish()

            mid_first = of(x, 0) + jnp.dot(attended[0], full_out, preferred_element_type=f32)
            scale_first = norm_scale(mid_first)
            h_first = (mid_first * scale_first * gain_m).astype(bf16)
            gate_first = jnp.dot(h_first, full_gate, preferred_element_type=f32)
    full_up, full_down = later.finish()
    full_down = full_down.reshape(FF, D)

    parts = []
    grads = []
    rows_grad = []
    mark = (mixed,)

    def back_of(g, *others):
        qkv, mixed, lse = saved[g]
        pieces = []
        for k in range(pairs):
            back = attend_back(k, after(qkv, *others), grads[g], mixed, lse, bounds[g], low[g])
            others = (back,)
            pieces.append(to_rows(back))
        rows_grad.append(pieces)
        return back

    for g in range(groups):
        final = g == groups - 1
        if g == 0:
            mid, scale_m, h_mlp, gate = mid_first, scale_first, h_first, gate_first
        else:
            mid = of(x, g) + jnp.dot(after(attended[g], *mark), full_out, preferred_element_type=f32)
            scale_m = norm_scale(mid)
            h_mlp = (mid * scale_m * gain_m).astype(bf16)
            gate = jnp.dot(h_mlp, full_gate, preferred_element_type=f32)
        up = jnp.dot(after(h_mlp, *mark), full_up, preferred_element_type=f32)
        sig = jax.nn.sigmoid(gate)
        act = (gate * sig * up).astype(bf16)
        parts.append([mid, scale_m, h_mlp, act])
        mark = (act,)
        if final:
            acts = jnp.concatenate([p[3] for p in parts], axis=0)
            sides = jnp.concatenate([p[2] for p in parts], axis=0)
            down = Reduce(None, cot, False, product=tn(after(acts, *mark, *grads), cot).astype(bf16))
            mark = (down.cross(),)
        if g:
            mark = (back_of(g - 1, *mark),)
        if final:
            mark = (down.send(*mark),)
        if g:
            mark = mark + (rows_grad[-1][0],)
        cot_part = of(cot, g)
        grad_act = nt(after(cot_part, *mark), full_down)
        grad_gate = (grad_act * up * sig * (1.0 + gate * (1.0 - sig))).astype(bf16)
        grad_up = (grad_act * (gate * sig)).astype(bf16)
        parts[g] += [grad_gate, grad_up]
        mark = (grad_gate, grad_up)
        if final:
            gate_r = Reduce(pieces_of(sides, False), jnp.concatenate([p[4] for p in parts], axis=0), False)
            up_r = Reduce(pieces_of(sides, True), jnp.concatenate([p[5] for p in parts], axis=0), True)
            mark = (up_r.cross(*mark),)
            mark = (gate_r.cross(*mark),)
        if final:
            mark = mark + (down.away,) + tuple(r for pieces in rows_grad for r in pieces)
        half_grad = nt(after(grad_gate, *mark), full_gate)
        mark = (half_grad,)
        if final:
            mark = (down.keep(*mark),)
            down.second()
            mark = (up_r.send(*mark),)
        grad_h_mlp = half_grad + nt(after(grad_up, *mark), full_up)
        grad_mid_norm, gain_part = norm_backward(grad_h_mlp, mid, scale_m, gain_m)
        grad_mid = cot_part.astype(f32) + grad_mid_norm
        grad_branch = grad_mid.astype(bf16)
        grad_rows = nt(grad_branch, full_out).astype(bf16)
        grads.append(to_heads(grad_rows, micros))
        parts[g] += [grad_mid, grad_branch, gain_part]
        mark = (grad_rows,)

    attended_all = jnp.concatenate(attended, axis=0)
    out_r = Reduce(pieces_of(attended_all, False), jnp.concatenate([p[7] for p in parts], axis=0), False)
    early = [down, up_r, gate_r, out_r]
    mark = (gate_r.send(*mark),)
    mark = (out_r.cross(*mark),)
    mark = (back_of(groups - 1, *mark),)
    mark = (up_r.keep(*mark),)
    up_r.second()
    mark = (out_r.send(*mark), rows_grad[-1][0])
    for r in (gate_r, out_r):
        mark = (r.keep(*mark),)
        r.second()
    layer_outs, grad_qkv, grad_tokens, gain_a_parts = [], [], [], []

    def finish_tokens(g, *others):
        grad_h_attn = nt(after(grad_qkv[g], *others), full_qkv)
        grad_norm, gain_part = norm_backward(grad_h_attn, of(x, g), of(scale_a, g), gain_a)
        grad_tokens.append(parts[g][6] + grad_norm)
        gain_a_parts.append(gain_part)
        return grad_tokens[-1]

    for g in range(groups):
        act = after(parts[g][3], *mark)
        layer_outs.append((parts[g][0] + jnp.dot(act, full_down, preferred_element_type=f32)).astype(bf16))
        mark = (layer_outs[-1],)
    mark = mark + tuple(rows_grad[-1])
    first = Finish(early, *mark)
    first.step(0)
    h_sides = [pieces_of(h_kept, False), pieces_of(h_kept, True)]
    for g in range(groups - 1):
        grad_qkv.append(rows_of(jnp.concatenate(rows_grad[g], axis=1), micros))
    grad_qkv.append(rows_of(jnp.concatenate([after(r, *mark) for r in rows_grad[-1]], axis=1), micros))
    last_rows = grad_qkv[-1]
    all_qkv = jnp.concatenate(grad_qkv, axis=0)
    half = 3 * D // 2
    late = [Reduce(h_sides[0], all_qkv[:, :half], False), Reduce(h_sides[1], all_qkv[:, half:], True)]
    for r in late:
        mark = (r.cross(*mark),)
    for g in range(groups - 1):
        mark = (finish_tokens(g, *mark),)
    for r in late:
        mark = (r.send(*mark),)
    mark = mark + (first.total,)
    g = groups - 1
    grad_h_attn = nt(after(last_rows, *mark), full_qkv)
    grad_norm, gain_part = norm_backward(grad_h_attn, of(x, g), of(scale_a, g), gain_a)
    grad_tokens.append(parts[g][6] + grad_norm)
    gain_a_parts.append(gain_part)
    mark = (grad_tokens[-1],)
    for r in late:
        mark = (r.keep(*mark),)
    for r in late:
        r.second(*mark)
    gain_sums = ScatterSmall(jnp.stack([sum(gain_a_parts), sum(p[8] for p in parts)]))
    second = Finish(late)
    for n in range(far):
        if n:
            first.step(n, hold=mark)
        gain_sums.step(digits_of("seq")[-2 - n], second.total)
        second.step(n)
    gain_grads = gain_sums.terms
    down_grad, up_grad, gate_grad, out_grad = first.results()
    qkv_grad = jnp.concatenate(second.results(), axis=1).reshape(-1, H, 3, HD).transpose(0, 2, 1, 3)
    join = lambda arrays: jnp.concatenate(arrays, axis=0).reshape(MB, 1, rows, D)

    return (
        join(layer_outs),
        join(grad_tokens),
        qkv_grad.reshape(-1, 3 * D),
        out_grad,
        jnp.concatenate([gate_grad, up_grad], axis=1),
        down_grad,
        gain_grads[0],
        gain_grads[1],
    )


def solution(mesh):
    by_rows = P(("dp", "seq"), None)
    by_tokens = P(None, "dp", "seq", None)
    vector = P(("dp", "seq"))
    return jax.shard_map(
        shards,
        mesh=mesh,
        in_specs=(by_tokens, P(None, "dp", None), by_rows, by_rows, by_rows, by_rows, vector, vector, by_tokens),
        out_specs=(by_tokens, by_tokens, by_rows, by_rows, by_rows, by_rows, vector, vector),
        check_vma=False,
    )
```

```python
import functools
import math

import jax
import jax.numpy as jnp
from jax import lax
from jax.experimental import pallas as pl
from jax.experimental.pallas import tpu as pltpu
from jax.sharding import PartitionSpec as P

D = 2048
H = 16
HD = 128
FF = 5504
WINDOW = 2048
MB = 2
TILE = 512

EPSILON = 1e-05
MASKED = -1e30
LOG2E = 1.4426950408889634
SCALE = 1.0 / math.sqrt(HD)

QUICK = pl.CostEstimate(flops=1024, bytes_accessed=1024, transcendentals=0)

bf16 = jnp.bfloat16
f32 = jnp.float32


def digits_of(axis):
    size = lax.axis_size(axis)
    return [(axis, 1 << bit) for bit in reversed(range(size.bit_length() - 1))]


def digit_index(digit):
    axis, stride = digit
    return lax.rem(lax.axis_index(axis) // stride, 2)


def swap(block, digit):
    axis, stride = digit
    return lax.ppermute(block, axis, [(i, i ^ stride) for i in range(lax.axis_size(axis))])


def pick(array, index, dim):
    return lax.dynamic_index_in_dim(array, index, dim, keepdims=False)


def scatter_digit(parts, digit, dim, out_type, hold=()):
    own = digit_index(digit)
    got = swap(pick(parts, 1 - own, dim), digit)
    if hold:
        got = lax.optimization_barrier((got,) + tuple(hold))[0]
    return (pick(parts, own, dim).astype(f32) + got.astype(f32)).astype(out_type)


def gather_small(block):
    for digit in reversed(digits_of("dp") + digits_of("seq")):
        got = swap(block, digit)
        low = digit_index(digit) == 0
        block = jnp.concatenate([jnp.where(low, block, got), jnp.where(low, got, block)], axis=-1)
    return block


class ScatterSmall:
    def __init__(self, terms):
        self.digits = digits_of("dp") + digits_of("seq")
        self.terms = terms.reshape((terms.shape[0],) + (2,) * len(self.digits) + (-1,))
        for digit in digits_of("dp")[::-1] + digits_of("seq")[-1:]:
            self.step(digit)

    def step(self, digit, *others):
        dim = 1 + self.digits.index(digit)
        self.digits = [d for d in self.digits if d != digit]
        self.terms = scatter_digit(after(self.terms, *others), digit, dim, f32)


SLOTS = 8


def place_kernel(count, rows, widths, target, *refs):
    sources, outs = refs[: -3 - len(widths)], refs[-3 - len(widths) : -3]
    held, in_sems, out_sems = refs[-3:]
    per = sources[0].shape[0] // rows

    def read(n):
        source = sources[n // per].at[pl.ds((n % per) * rows, rows), :]
        return pltpu.make_async_copy(source, held.at[n % SLOTS], in_sems.at[n % SLOTS])

    def writes(n):
        start, left = pl.multiple_of(target[n], 16), 0
        copies = []
        for k, width in enumerate(widths):
            source = held.at[n % SLOTS, :, pl.ds(left, width)]
            copies.append(pltpu.make_async_copy(source, outs[k].at[pl.ds(start, rows), :], out_sems.at[n % SLOTS, k]))
            left += width
        return copies

    lag = SLOTS // 2
    for n in range(min(lag, count)):
        read(n).start()
    for n in range(count):
        if n >= lag:
            for copy in writes(n - lag):
                copy.wait()
        if n + lag < count:
            read(n + lag).start()
        read(n).wait()
        for copy in writes(n):
            copy.start()
    for n in range(max(count - lag, 0), count):
        for copy in writes(n):
            copy.wait()


class Gather:
    def __init__(self, blocks, seq_first):
        self.rows, self.widths = blocks[0].shape[0], [b.shape[1] for b in blocks]
        fast, height = digits_of("seq")[-1:], digits_of("dp")[:-1]
        self.far = digits_of("seq")[:-1]
        self.near = (fast + height if seq_first else height + fast) + digits_of("dp")[-1:]
        self.buffers = [(jnp.concatenate(blocks, axis=1), ())]

    def values(self):
        return [b for b, _ in self.buffers]

    def wait(self, *others):
        self.buffers = [(after(b, *others), d) for b, d in self.buffers]

    def far_step(self, n):
        (block, digits), digit = self.buffers[0], self.far[n]
        self.buffers = [(jnp.concatenate([block, swap(block, digit)], axis=0), digits + (digit,))]

    def near_step(self, n):
        digit = self.near[n]
        self.buffers = self.buffers + [(swap(b, digit), d + (digit,)) for b, d in self.buffers]

    def finish(self):
        offsets = []
        rows = self.rows
        stride_of = lambda digit: digit[1] * (lax.axis_size("seq") if digit[0] == "dp" else 1)
        for _, digits in self.buffers:
            near = sum(stride_of(d) for d in digits if d not in self.far)
            for n in range(1 << len(self.far)):
                offsets.append(near + sum(stride_of(d) for bit, d in enumerate(self.far) if n >> bit & 1))
        mine = lax.axis_index("dp") * lax.axis_size("seq") + lax.axis_index("seq")
        targets = lax.bitwise_xor(jnp.asarray(offsets, jnp.int32), mine.astype(jnp.int32)) * rows
        count = len(offsets)
        return pl.pallas_call(
            functools.partial(place_kernel, count, rows, self.widths),
            grid_spec=pltpu.PrefetchScalarGridSpec(
                num_scalar_prefetch=1,
                in_specs=[pl.BlockSpec(memory_space=pl.ANY)] * len(self.buffers),
                out_specs=[pl.BlockSpec(memory_space=pl.ANY)] * len(self.widths),
                scratch_shapes=[
                    pltpu.VMEM((SLOTS, rows, sum(self.widths)), bf16),
                    pltpu.SemaphoreType.DMA((SLOTS,)),
                    pltpu.SemaphoreType.DMA((SLOTS, len(self.widths))),
                ],
            ),
            out_shape=[jax.ShapeDtypeStruct((count * rows, width), bf16) for width in self.widths],
            compiler_params=pltpu.CompilerParams(vmem_limit_bytes=16 * 1024 * 1024),
            cost_estimate=QUICK,
            name="place",
        )(targets, *self.values())


def tn(a, b):
    return lax.dot_general(a, b, (((0,), (0,)), ((), ())), preferred_element_type=f32)


def after(value, *others):
    return lax.optimization_barrier((value,) + others)[0]


def pieces_of(side, seq_first):
    dp, seq = lax.axis_size("dp"), lax.axis_size("seq")
    tokens, total = side.shape
    if seq_first:
        pieces = side.reshape(tokens, dp // 2, 2, seq // 2, 2, -1).transpose(2, 0, 4, 1, 3, 5)
    else:
        pieces = side.reshape(tokens, dp // 2, 2, -1).transpose(2, 0, 1, 3)
    return pieces.reshape(2, tokens, total // 2)


class Reduce:
    def __init__(self, pieces, cols_side, seq_first, product=None):
        self.pieces, self.cols_side, self.seq_first, self.product = pieces, cols_side, seq_first, product
        self.half = product.shape[0] // 4 if pieces is None else pieces.shape[2] // 2
        self.own = self.half * 4 // (lax.axis_size("dp") * lax.axis_size("seq"))
        self.core, self.height = digits_of("dp")[-1], digits_of("dp")[0]
        self.fast, self.far = digits_of("seq")[-1], digits_of("seq")[:-1]
        self.first = self.fast if seq_first else self.height
        self.c, self.mine = digit_index(self.core), digit_index(self.first)

    def term(self, core_index, index, others):
        if self.pieces is None:
            parts = pick(after(self.product, *others).reshape(2, 2, self.half, -1), core_index, 1)
            return (parts.reshape(2 * self.half, -1) if index is None else pick(parts, index, 0)).astype(f32)
        side = pick(after(self.pieces, *others), core_index, 0)
        if index is not None:
            side = lax.dynamic_slice_in_dim(side, index * self.half, self.half, 1)
        return tn(side, self.cols_side)

    def cross(self, *others):
        term = self.term(1 - self.c, None, others).astype(bf16)
        self.got = swap(term, self.core)
        return term

    def got_part(self, index):
        return lax.dynamic_slice_in_dim(self.got, index * self.half, self.half, 0).astype(f32)

    def send(self, *others):
        away = (self.term(self.c, 1 - self.mine, others) + self.got_part(1 - self.mine)).astype(bf16)
        self.away = swap(away, self.first)
        return away

    def keep(self, *others):
        total = self.term(self.c, self.mine, others) + self.got_part(self.mine) + self.away.astype(f32)
        self.total = total.astype(bf16)
        return self.total

    def second(self, *others):
        cols = self.cols_side.shape[1]
        total = after(self.total, *others)
        if self.seq_first:
            self.total = scatter_digit(total.reshape(2, -1, cols), self.height, 0, bf16)
        else:
            self.total = scatter_digit(total.reshape(-1, 2, self.own, cols), self.fast, 1, bf16)
        return self.total


class Finish:
    def __init__(self, reduces, *others):
        self.reduces, self.far = reduces, reduces[0].far
        self.count = 1 << len(self.far)
        self.unit = D // (lax.axis_size("dp") * lax.axis_size("seq"))
        totals = [after(r.total, *others).reshape(self.count, self.unit, -1) for r in reduces]
        self.widths = [t.shape[2] for t in totals]
        self.total = jnp.concatenate(totals, axis=2)

    def step(self, n, *others, hold=()):
        total = after(self.total, *others).reshape(-1, 2, self.unit, sum(self.widths))
        self.total = scatter_digit(total, self.far[-1 - n], 1, f32 if n == len(self.far) - 1 else bf16, hold)
        return self.total

    def results(self):
        left = 0
        results = []
        for r, width in zip(self.reduces, self.widths):
            results.append(self.total[0, :, left : left + width].reshape(r.own, -1))
            left += width
        return results


def dot_nt(a, b):
    return lax.dot_general(a, b, (((1,), (1,)), ((), ())), preferred_element_type=f32)


def dot_tn(a, b):
    return lax.dot_general(a, b, (((0,), (0,)), ((), ())), preferred_element_type=f32)


def dot_nn(a, b):
    return lax.dot_general(a, b, (((1,), (0,)), ((), ())), preferred_element_type=f32)


def tile_of(ref, index):
    per = TILE // ref.shape[1]
    return ref[pl.ds(index * per, per)].reshape(TILE, HD)


def mask_of(i, j, lo):
    key = j * TILE + lax.broadcasted_iota(jnp.int32, (TILE, TILE), 0)
    query = i * TILE + lax.broadcasted_iota(jnp.int32, (TILE, TILE), 1)
    return (key >= lo) & (key <= query)


def forward_kernel(bounds, q_ref, k_ref, v_ref, lo_ref, o_ref, lse_ref, acc):
    pair, i = pl.program_id(0), pl.program_id(1)
    q = q_ref[...].reshape(TILE, HD)
    lo = lo_ref[...]
    factor = SCALE * LOG2E

    def step(j, carry, masked):
        m, l = carry
        s = dot_nt(tile_of(k_ref, j), q) * factor
        if masked:
            s = jnp.where(mask_of(i, j, lo), s, MASKED)
        new = jnp.maximum(m, jnp.max(s, axis=0, keepdims=True))
        p = jnp.exp2(s - new)
        old = jnp.exp2(m - new)
        acc[...] = acc[...] * old + dot_tn(tile_of(v_ref, j), p.astype(bf16))
        return new, l * old + jnp.sum(p, axis=0, keepdims=True)

    acc[...] = jnp.zeros_like(acc)
    carry = (jnp.full((1, TILE), MASKED, f32), jnp.zeros((1, TILE), f32))
    start = bounds[pair, 0, i]
    middle = bounds[pair, 1, i]
    carry = lax.fori_loop(start, middle, lambda j, c: step(j, c, True), carry)
    carry = lax.fori_loop(middle, i, lambda j, c: step(j, c, False), carry)
    m, l = step(i, carry, True)
    o_ref[...] = (acc[...] / l).T.astype(bf16).reshape(o_ref.shape)
    lse_ref[...] = m + jnp.log2(l)


def attend(qkv, bounds, low):
    seq, pairs, rows, _ = qkv.shape
    length = seq * rows
    blocks, per = length // TILE, TILE // rows
    whole = lambda part: pl.BlockSpec((seq, None, rows, HD), lambda p, i, b: (0, p, 0, part))
    line = pl.BlockSpec((None, 1, TILE), lambda p, i, b: (p, 0, i))
    block = pl.BlockSpec((per, None, rows, HD), lambda p, i, b: (i, p, 0, 0))
    return pl.pallas_call(
        forward_kernel,
        grid_spec=pltpu.PrefetchScalarGridSpec(
            num_scalar_prefetch=1,
            grid=(pairs, blocks),
            in_specs=[block, whole(1), whole(2), line],
            out_specs=[block, line],
            scratch_shapes=[pltpu.VMEM((HD, TILE), f32)],
        ),
        out_shape=[
            jax.ShapeDtypeStruct((seq, pairs, rows, HD), bf16),
            jax.ShapeDtypeStruct((pairs, 1, length), f32),
        ],
        compiler_params=pltpu.CompilerParams(vmem_limit_bytes=32 * 1024 * 1024),
        cost_estimate=QUICK,
        name="attend",
    )(bounds, qkv, qkv, qkv, low)


def backward_kernel(pair, bounds, q_ref, k_ref, v_ref, do_ref, o_ref, lse_ref, lo_ref, out_ref, dq, dk, dv, delta):
    j = pl.program_id(0)
    k = k_ref[...].reshape(TILE, HD)
    v = v_ref[...].reshape(TILE, HD)
    factor = SCALE * LOG2E

    def step(i, masked):
        rows = pl.ds(pl.multiple_of(i * TILE, TILE), TILE)
        q = tile_of(q_ref, i)
        do = tile_of(do_ref, i)
        s = dot_nt(k, q) * factor
        p = jnp.exp2(s - lse_ref[:, rows])
        if masked:
            p = jnp.where(mask_of(i, j, lo_ref[:, rows]), p, 0.0)
        dp = dot_nt(v, do)
        ds = (p * (dp - delta[:, rows])).astype(bf16)
        dv[...] += dot_nn(p.astype(bf16), do)
        dk[...] += dot_nn(ds, q)
        dq[rows, :] += dot_tn(ds, k)

    @pl.when(j == 0)
    def _():
        dq[...] = jnp.zeros_like(dq)

        @pl.loop(0, pl.num_programs(0))
        def _(i):
            rows = pl.ds(pl.multiple_of(i * TILE, TILE), TILE)
            product = tile_of(do_ref, i).astype(f32) * tile_of(o_ref, i).astype(f32)
            delta[:, rows] = jnp.sum(product.T, axis=0, keepdims=True)

    dk[...] = jnp.zeros_like(dk)
    dv[...] = jnp.zeros_like(dv)
    step(j, True)
    middle = bounds[pair, 2, j]
    end = bounds[pair, 3, j]

    @pl.loop(j + 1, middle)
    def _(i):
        step(i, False)

    @pl.loop(middle, end)
    def _(i):
        step(i, True)

    own = pl.ds(pl.multiple_of(j * TILE, TILE), TILE)
    shape = out_ref.shape[:-1] + (HD,)
    out_ref[:, :, :HD] = (dq[own, :] * SCALE).astype(bf16).reshape(shape)
    out_ref[:, :, HD : 2 * HD] = (dk[...] * SCALE).astype(bf16).reshape(shape)
    out_ref[:, :, 2 * HD :] = dv[...].astype(bf16).reshape(shape)


def attend_back(pair, qkv, grad, mixed, lse, bounds, low):
    seq, _, rows, _ = qkv.shape
    length = seq * rows
    blocks, per = length // TILE, TILE // rows
    whole = pl.BlockSpec((seq, None, rows, HD), lambda j, b: (0, pair, 0, 0))
    line = pl.BlockSpec((None, 1, length), lambda j, b: (pair, 0, 0))
    block = lambda part: pl.BlockSpec((per, None, rows, HD), lambda j, b: (j, pair, 0, part))
    return pl.pallas_call(
        functools.partial(backward_kernel, pair),
        grid_spec=pltpu.PrefetchScalarGridSpec(
            num_scalar_prefetch=1,
            grid=(blocks,),
            in_specs=[whole, block(1), block(2), whole, whole, line, line],
            out_specs=pl.BlockSpec((per, None, rows, 3 * HD), lambda j, b: (j, 0, 0, 0)),
            scratch_shapes=[
                pltpu.VMEM((length, HD), f32),
                pltpu.VMEM((TILE, HD), f32),
                pltpu.VMEM((TILE, HD), f32),
                pltpu.VMEM((1, length), f32),
            ],
        ),
        out_shape=jax.ShapeDtypeStruct((seq, 1, rows, 3 * HD), bf16),
        compiler_params=pltpu.CompilerParams(vmem_limit_bytes=40 * 1024 * 1024),
        cost_estimate=QUICK,
        name="attend_back",
    )(bounds, qkv, qkv, qkv, grad, mixed, lse, low)


def key_bounds(segments):
    length = segments.shape[0]
    blocks = length // TILE
    place = jnp.arange(length, dtype=jnp.int32)
    start = jnp.zeros_like(place)
    for value in range(1, 4):
        earlier = jnp.sum(segments < value, dtype=jnp.int32)
        start = jnp.where(segments == value, earlier, start)
    low = jnp.maximum(start, place - (WINDOW - 1))
    index = jnp.arange(blocks, dtype=jnp.int32)
    first = low[::TILE]
    last = low[TILE - 1 :: TILE]
    begin = first // TILE
    middle = jnp.clip((last + TILE - 1) // TILE, begin, index)
    full = (last[None, :] <= index[:, None] * TILE) & (index[None, :] > index[:, None])
    some = (first[None, :] < (index[:, None] + 1) * TILE) & (index[None, :] > index[:, None])
    back_middle = index + 1 + jnp.sum(full, axis=1, dtype=jnp.int32)
    back_end = index + 1 + jnp.sum(some, axis=1, dtype=jnp.int32)
    return low[None], jnp.stack([begin, middle, back_middle, back_end])


def to_heads(rows, micros):
    seq = lax.axis_size("seq")
    count, width = rows.shape[0] // micros, rows.shape[1] // H
    split = rows.reshape(micros, count, H, width).transpose(2, 0, 1, 3)
    split = split.reshape(seq, H * micros // seq, count, width)
    return lax.all_to_all(split, "seq", 0, 0, tiled=True)


def to_rows(whole):
    return lax.all_to_all(whole, "seq", 0, 0, tiled=True)


def rows_of(got, micros):
    count, width = got.shape[2], got.shape[3]
    return got.reshape(H, micros, count, width).transpose(1, 2, 0, 3).reshape(micros * count, H * width)


def norm_scale(values):
    return lax.rsqrt(jnp.mean(values * values, axis=-1, keepdims=True) + EPSILON)


def norm_backward(grad_in, values, row_scale, gain):
    normed = values * row_scale
    gain_grad = jnp.sum(grad_in * normed, axis=0)
    scaled = grad_in * gain
    inner = jnp.mean(scaled * normed, axis=-1, keepdims=True)
    return row_scale * (scaled - normed * inner), gain_grad


def nt(a, b):
    return jnp.einsum("re,de->rd", a, b, preferred_element_type=f32)


def shards(tokens, segment_ids, w_qkv, w_out, w_gate_up, w_down, gain_attn, gain_mlp, cotangent):
    rows = tokens.shape[2]
    seq = lax.axis_size("seq")
    gather = lambda w: lax.all_gather(w, ("dp", "seq"), axis=0, tiled=True)
    groups = MB if H % seq == 0 else 1
    micros = MB // groups
    pairs = H * micros // seq
    size = micros * rows
    of = lambda array, g: array[g * size : (g + 1) * size]

    x = tokens.reshape(MB * rows, D).astype(f32)
    cot = cotangent.reshape(MB * rows, D)
    bounds, low = [], []
    for g in range(groups):
        made = []
        for k in range(pairs):
            micro = g if micros == 1 else lax.rem(lax.axis_index("seq") * pairs + k, micros)
            made.append(key_bounds(segment_ids[g, 0] if micros == 1 else pick(segment_ids[:, 0], micro, 0)))
        low.append(jnp.stack([m[0] for m in made]))
        bounds.append(jnp.stack([m[1] for m in made]))

    order_qkv = w_qkv.reshape(-1, 3, H, HD).transpose(0, 2, 1, 3).reshape(w_qkv.shape)
    full_qkv = gather(order_qkv)
    all_gains = gather_small(jnp.stack([gain_attn, gain_mlp]))
    gains = all_gains.astype(f32)
    gain_a, gain_m = gains[0], gains[1]
    scale_a = norm_scale(x)
    h_attn = (x * scale_a * gain_a).astype(bf16)
    soon = Gather([w_gate_up[:, :FF], w_out], False)
    later = Gather([w_gate_up[:, FF:], w_down.reshape(w_qkv.shape[0], -1)], True)
    far = len(soon.far)

    soon.wait(all_gains, h_attn)
    soon.far_step(0)
    for n in range(1, far):
        later.wait(*soon.values())
        soon.far_step(n)
        later.far_step(n - 1)
    ready = soon.values() + later.values()
    soon.wait(*ready)
    soon.near_step(0)
    later.wait(*ready)
    later.far_step(far - 1)
    later.wait(*soon.values())
    later.near_step(0)
    h_kept = step_in = after(h_attn, *later.values())
    saved, attended, arrived = [], [], []

    def project(g, *others):
        qkv_rows = jnp.dot(of(after(h_kept, *others), g), full_qkv, preferred_element_type=f32).astype(bf16)
        arrived.append(to_heads(qkv_rows, micros))

    def attention(g, others):
        qkv = after(arrived[g], *others)
        mixed, lse = attend(qkv, bounds[g], low[g])
        saved.append((qkv, mixed, lse))
        return to_rows(mixed)

    project(0)
    ready = soon.values() + later.values()
    for w in (soon, later):
        w.wait(*ready)
        w.near_step(1)
    back_rows = attention(0, soon.values() + later.values())
    soon.near_step(2)
    later.near_step(2)
    full_gate, full_out = soon.finish()
    full_up, full_down = later.finish()
    full_down = full_down.reshape(FF, D)
    attended.append(rows_of(after(back_rows, full_gate, full_out, full_up, full_down), micros))
    if groups > 1:
        project(1, attended[0])

    parts = []
    grads = []
    rows_grad = []
    mark = ()

    def back_of(g, *others):
        qkv, mixed, lse = saved[g]
        pieces = []
        for k in range(pairs):
            back = attend_back(k, after(qkv, *others), grads[g], mixed, lse, bounds[g], low[g])
            others = (back,)
            pieces.append(to_rows(back))
        rows_grad.append(pieces)
        return back

    for g in range(groups):
        final = g == groups - 1
        mid = of(x, g) + jnp.dot(after(attended[g], *mark), full_out, preferred_element_type=f32)
        scale_m = norm_scale(mid)
        h_mlp = (mid * scale_m * gain_m).astype(bf16)
        gate = jnp.dot(h_mlp, full_gate, preferred_element_type=f32)
        up = jnp.dot(after(h_mlp, *mark), full_up, preferred_element_type=f32)
        sig = jax.nn.sigmoid(gate)
        act = (gate * sig * up).astype(bf16)
        parts.append([mid, scale_m, h_mlp, act])
        mark = (act,)
        if final:
            acts = jnp.concatenate([p[3] for p in parts], axis=0)
            sides = jnp.concatenate([p[2] for p in parts], axis=0)
            down = Reduce(None, cot, False, product=tn(after(acts, *mark, *grads), cot).astype(bf16))
            mark = (down.cross(),)
        if g:
            mark = (back_of(g - 1, *mark),)
        if final:
            mark = (down.send(*mark),)
        if g:
            mark = mark + (rows_grad[-1][0],)
        cot_part = of(cot, g)
        grad_act = nt(after(cot_part, *mark), full_down)
        grad_gate = (grad_act * up * sig * (1.0 + gate * (1.0 - sig))).astype(bf16)
        grad_up = (grad_act * (gate * sig)).astype(bf16)
        parts[g] += [grad_gate, grad_up]
        mark = (grad_gate, grad_up)
        if not final:
            back_rows = attention(g + 1, mark)
            mark = (saved[-1][1],)
        if final:
            gate_r = Reduce(pieces_of(sides, False), jnp.concatenate([p[4] for p in parts], axis=0), False)
            up_r = Reduce(pieces_of(sides, True), jnp.concatenate([p[5] for p in parts], axis=0), True)
            mark = (up_r.cross(*mark),)
            mark = (gate_r.cross(*mark),)
        if final:
            mark = (up_r.send(*mark),)
        half_grad = nt(after(grad_gate, *mark), full_gate)
        mark = (half_grad,)
        grad_h_mlp = half_grad + nt(after(grad_up, *mark), full_up)
        grad_mid_norm, gain_part = norm_backward(grad_h_mlp, mid, scale_m, gain_m)
        grad_mid = cot_part.astype(f32) + grad_mid_norm
        grad_branch = grad_mid.astype(bf16)
        arrivals = [r for pieces in rows_grad for r in pieces]
        grad_rows = nt(after(grad_branch, *arrivals), full_out).astype(bf16)
        if not final:
            attended.append(rows_of(after(back_rows, grad_rows), micros))
        grads.append(to_heads(grad_rows, micros))
        parts[g] += [grad_mid, grad_branch, gain_part]
        mark = (grad_rows,)

    attended_all = jnp.concatenate(attended, axis=0)
    out_r = Reduce(pieces_of(attended_all, False), jnp.concatenate([p[7] for p in parts], axis=0), False)
    early = [down, up_r, gate_r, out_r]
    mark = (gate_r.send(*mark),)
    mark = (out_r.cross(*mark),)
    mark = (down.keep(*mark),)
    down.second(grads[-1])
    mark = (back_of(groups - 1, *mark),)
    mark = (up_r.keep(*mark),)
    up_r.second()
    mark = (out_r.send(*mark), rows_grad[-1][0])
    for r in (gate_r, out_r):
        mark = (r.keep(*mark),)
        r.second()
    layer_outs, grad_qkv, grad_tokens, gain_a_parts = [], [], [], []

    def finish_tokens(g, *others):
        grad_h_attn = nt(after(grad_qkv[g], *others), full_qkv)
        grad_norm, gain_part = norm_backward(grad_h_attn, of(x, g), of(scale_a, g), gain_a)
        grad_tokens.append(parts[g][6] + grad_norm)
        gain_a_parts.append(gain_part)
        return grad_tokens[-1]

    for g in range(groups):
        act = after(parts[g][3], *mark)
        layer_outs.append((parts[g][0] + jnp.dot(act, full_down, preferred_element_type=f32)).astype(bf16))
        mark = (layer_outs[-1],)
    mark = mark + tuple(rows_grad[-1])
    first = Finish(early, *mark)
    first.step(0)
    h_sides = [pieces_of(h_kept, False), pieces_of(h_kept, True)]
    for g in range(groups - 1):
        grad_qkv.append(rows_of(jnp.concatenate(rows_grad[g], axis=1), micros))
    grad_qkv.append(rows_of(jnp.concatenate([after(r, *mark) for r in rows_grad[-1]], axis=1), micros))
    last_rows = grad_qkv[-1]
    all_qkv = jnp.concatenate(grad_qkv, axis=0)
    half = 3 * D // 2
    late = [Reduce(h_sides[0], all_qkv[:, :half], False), Reduce(h_sides[1], all_qkv[:, half:], True)]
    for r in late:
        mark = (r.cross(*mark),)
    for g in range(groups - 1):
        mark = (finish_tokens(g, *mark),)
    for r in late:
        mark = (r.send(*mark),)
    g = groups - 1
    grad_h_attn = nt(after(last_rows, *mark), full_qkv)
    grad_norm, gain_part = norm_backward(grad_h_attn, of(x, g), of(scale_a, g), gain_a)
    grad_tokens.append(parts[g][6] + grad_norm)
    gain_a_parts.append(gain_part)
    mark = (grad_tokens[-1], first.total)
    for r in late:
        mark = (r.keep(*mark),)
    for r in late:
        r.second(*mark)
    gain_sums = ScatterSmall(jnp.stack([sum(gain_a_parts), sum(p[8] for p in parts)]))
    second = Finish(late)
    for n in range(far):
        if n:
            first.step(n, hold=mark)
        gain_sums.step(digits_of("seq")[-2 - n], second.total)
        second.step(n)
    gain_grads = gain_sums.terms
    down_grad, up_grad, gate_grad, out_grad = first.results()
    qkv_grad = jnp.concatenate(second.results(), axis=1).reshape(-1, H, 3, HD).transpose(0, 2, 1, 3)
    join = lambda arrays: jnp.concatenate(arrays, axis=0).reshape(MB, 1, rows, D)

    return (
        join(layer_outs),
        join(grad_tokens),
        qkv_grad.reshape(-1, 3 * D),
        out_grad,
        jnp.concatenate([gate_grad, up_grad], axis=1),
        down_grad,
        gain_grads[0],
        gain_grads[1],
    )


def solution(mesh):
    by_rows = P(("dp", "seq"), None)
    by_tokens = P(None, "dp", "seq", None)
    vector = P(("dp", "seq"))
    return jax.shard_map(
        shards,
        mesh=mesh,
        in_specs=(by_tokens, P(None, "dp", None), by_rows, by_rows, by_rows, by_rows, vector, vector, by_tokens),
        out_specs=(by_tokens, by_tokens, by_rows, by_rows, by_rows, by_rows, vector, vector),
        check_vma=False,
    )
```

```python
import functools
import math

import jax
import jax.numpy as jnp
from jax import lax
from jax.experimental import pallas as pl
from jax.experimental.pallas import tpu as pltpu
from jax.sharding import PartitionSpec as P

D = 2048
H = 16
HD = 128
FF = 5504
WINDOW = 2048
MB = 2
TILE = 512

EPSILON = 1e-05
MASKED = -1e30
LOG2E = 1.4426950408889634
SCALE = 1.0 / math.sqrt(HD)

QUICK = pl.CostEstimate(flops=1024, bytes_accessed=1024, transcendentals=0)

bf16 = jnp.bfloat16
f32 = jnp.float32


def digits_of(axis):
    size = lax.axis_size(axis)
    return [(axis, 1 << bit) for bit in reversed(range(size.bit_length() - 1))]


def digit_index(digit):
    axis, stride = digit
    return lax.rem(lax.axis_index(axis) // stride, 2)


def swap(block, digit):
    axis, stride = digit
    return lax.ppermute(block, axis, [(i, i ^ stride) for i in range(lax.axis_size(axis))])


def pick(array, index, dim):
    return lax.dynamic_index_in_dim(array, index, dim, keepdims=False)


def scatter_digit(parts, digit, dim, out_type, hold=()):
    own = digit_index(digit)
    got = swap(pick(parts, 1 - own, dim), digit)
    if hold:
        got = lax.optimization_barrier((got,) + tuple(hold))[0]
    return (pick(parts, own, dim).astype(f32) + got.astype(f32)).astype(out_type)


def gather_small(block):
    for digit in reversed(digits_of("dp") + digits_of("seq")):
        got = swap(block, digit)
        low = digit_index(digit) == 0
        block = jnp.concatenate([jnp.where(low, block, got), jnp.where(low, got, block)], axis=-1)
    return block


class ScatterSmall:
    def __init__(self, terms):
        self.digits = digits_of("dp") + digits_of("seq")
        self.terms = terms.reshape((terms.shape[0],) + (2,) * len(self.digits) + (-1,))
        for digit in digits_of("dp")[::-1] + digits_of("seq")[-1:]:
            self.step(digit)

    def step(self, digit, *others):
        dim = 1 + self.digits.index(digit)
        self.digits = [d for d in self.digits if d != digit]
        self.terms = scatter_digit(after(self.terms, *others), digit, dim, f32)


SLOTS = 8


def place_kernel(count, rows, widths, target, *refs):
    sources, outs = refs[: -3 - len(widths)], refs[-3 - len(widths) : -3]
    held, in_sems, out_sems = refs[-3:]
    per = sources[0].shape[0] // rows

    def read(n):
        source = sources[n // per].at[pl.ds((n % per) * rows, rows), :]
        return pltpu.make_async_copy(source, held.at[n % SLOTS], in_sems.at[n % SLOTS])

    def writes(n):
        start, left = pl.multiple_of(target[n], 16), 0
        copies = []
        for k, width in enumerate(widths):
            source = held.at[n % SLOTS, :, pl.ds(left, width)]
            copies.append(pltpu.make_async_copy(source, outs[k].at[pl.ds(start, rows), :], out_sems.at[n % SLOTS, k]))
            left += width
        return copies

    lag = SLOTS // 2
    for n in range(min(lag, count)):
        read(n).start()
    for n in range(count):
        if n >= lag:
            for copy in writes(n - lag):
                copy.wait()
        if n + lag < count:
            read(n + lag).start()
        read(n).wait()
        for copy in writes(n):
            copy.start()
    for n in range(max(count - lag, 0), count):
        for copy in writes(n):
            copy.wait()


class Gather:
    def __init__(self, blocks, seq_first):
        self.rows, self.widths = blocks[0].shape[0], [b.shape[1] for b in blocks]
        fast, height = digits_of("seq")[-1:], digits_of("dp")[:-1]
        self.far = digits_of("seq")[:-1]
        self.near = (fast + height if seq_first else height + fast) + digits_of("dp")[-1:]
        self.buffers = [(jnp.concatenate(blocks, axis=1), ())]

    def values(self):
        return [b for b, _ in self.buffers]

    def wait(self, *others):
        self.buffers = [(after(b, *others), d) for b, d in self.buffers]

    def far_step(self, n):
        (block, digits), digit = self.buffers[0], self.far[n]
        self.buffers = [(jnp.concatenate([block, swap(block, digit)], axis=0), digits + (digit,))]

    def near_step(self, n):
        digit = self.near[n]
        self.buffers = self.buffers + [(swap(b, digit), d + (digit,)) for b, d in self.buffers]

    def finish(self):
        offsets = []
        rows = self.rows
        stride_of = lambda digit: digit[1] * (lax.axis_size("seq") if digit[0] == "dp" else 1)
        for _, digits in self.buffers:
            near = sum(stride_of(d) for d in digits if d not in self.far)
            for n in range(1 << len(self.far)):
                offsets.append(near + sum(stride_of(d) for bit, d in enumerate(self.far) if n >> bit & 1))
        mine = lax.axis_index("dp") * lax.axis_size("seq") + lax.axis_index("seq")
        targets = lax.bitwise_xor(jnp.asarray(offsets, jnp.int32), mine.astype(jnp.int32)) * rows
        count = len(offsets)
        return pl.pallas_call(
            functools.partial(place_kernel, count, rows, self.widths),
            grid_spec=pltpu.PrefetchScalarGridSpec(
                num_scalar_prefetch=1,
                in_specs=[pl.BlockSpec(memory_space=pl.ANY)] * len(self.buffers),
                out_specs=[pl.BlockSpec(memory_space=pl.ANY)] * len(self.widths),
                scratch_shapes=[
                    pltpu.VMEM((SLOTS, rows, sum(self.widths)), bf16),
                    pltpu.SemaphoreType.DMA((SLOTS,)),
                    pltpu.SemaphoreType.DMA((SLOTS, len(self.widths))),
                ],
            ),
            out_shape=[jax.ShapeDtypeStruct((count * rows, width), bf16) for width in self.widths],
            compiler_params=pltpu.CompilerParams(vmem_limit_bytes=16 * 1024 * 1024),
            cost_estimate=QUICK,
            name="place",
        )(targets, *self.values())


def tn(a, b):
    return lax.dot_general(a, b, (((0,), (0,)), ((), ())), preferred_element_type=f32)


def after(value, *others):
    return lax.optimization_barrier((value,) + others)[0]


def pieces_of(side, seq_first):
    dp, seq = lax.axis_size("dp"), lax.axis_size("seq")
    tokens, total = side.shape
    if seq_first:
        pieces = side.reshape(tokens, dp // 2, 2, seq // 2, 2, -1).transpose(2, 0, 4, 1, 3, 5)
    else:
        pieces = side.reshape(tokens, dp // 2, 2, -1).transpose(2, 0, 1, 3)
    return pieces.reshape(2, tokens, total // 2)


class Reduce:
    def __init__(self, pieces, cols_side, seq_first, product=None):
        self.pieces, self.cols_side, self.seq_first, self.product = pieces, cols_side, seq_first, product
        self.half = product.shape[0] // 4 if pieces is None else pieces.shape[2] // 2
        self.own = self.half * 4 // (lax.axis_size("dp") * lax.axis_size("seq"))
        self.core, self.height = digits_of("dp")[-1], digits_of("dp")[0]
        self.fast, self.far = digits_of("seq")[-1], digits_of("seq")[:-1]
        self.first = self.fast if seq_first else self.height
        self.c, self.mine = digit_index(self.core), digit_index(self.first)

    def term(self, core_index, index, others):
        if self.pieces is None:
            parts = pick(after(self.product, *others).reshape(2, 2, self.half, -1), core_index, 1)
            return (parts.reshape(2 * self.half, -1) if index is None else pick(parts, index, 0)).astype(f32)
        side = pick(after(self.pieces, *others), core_index, 0)
        if index is not None:
            side = lax.dynamic_slice_in_dim(side, index * self.half, self.half, 1)
        return tn(side, self.cols_side)

    def cross(self, *others):
        term = self.term(1 - self.c, None, others).astype(bf16)
        self.got = swap(term, self.core)
        return term

    def got_part(self, index):
        return lax.dynamic_slice_in_dim(self.got, index * self.half, self.half, 0).astype(f32)

    def send(self, *others):
        away = (self.term(self.c, 1 - self.mine, others) + self.got_part(1 - self.mine)).astype(bf16)
        self.away = swap(away, self.first)
        return away

    def keep(self, *others):
        total = self.term(self.c, self.mine, others) + self.got_part(self.mine) + self.away.astype(f32)
        self.total = total.astype(bf16)
        return self.total

    def second(self, *others):
        cols = self.cols_side.shape[1]
        total = after(self.total, *others)
        if self.seq_first:
            self.total = scatter_digit(total.reshape(2, -1, cols), self.height, 0, bf16)
        else:
            self.total = scatter_digit(total.reshape(-1, 2, self.own, cols), self.fast, 1, bf16)
        return self.total


class Finish:
    def __init__(self, reduces, *others):
        self.reduces, self.far = reduces, reduces[0].far
        self.count = 1 << len(self.far)
        self.unit = D // (lax.axis_size("dp") * lax.axis_size("seq"))
        totals = [after(r.total, *others).reshape(self.count, self.unit, -1) for r in reduces]
        self.widths = [t.shape[2] for t in totals]
        self.total = jnp.concatenate(totals, axis=2)

    def step(self, n, *others, hold=()):
        total = after(self.total, *others).reshape(-1, 2, self.unit, sum(self.widths))
        self.total = scatter_digit(total, self.far[-1 - n], 1, f32 if n == len(self.far) - 1 else bf16, hold)
        return self.total

    def results(self):
        left = 0
        results = []
        for r, width in zip(self.reduces, self.widths):
            results.append(self.total[0, :, left : left + width].reshape(r.own, -1))
            left += width
        return results


def dot_nt(a, b):
    return lax.dot_general(a, b, (((1,), (1,)), ((), ())), preferred_element_type=f32)


def dot_tn(a, b):
    return lax.dot_general(a, b, (((0,), (0,)), ((), ())), preferred_element_type=f32)


def dot_nn(a, b):
    return lax.dot_general(a, b, (((1,), (0,)), ((), ())), preferred_element_type=f32)


def tile_of(ref, index):
    per = TILE // ref.shape[1]
    return ref[pl.ds(index * per, per)].reshape(TILE, HD)


def mask_of(i, j, lo):
    key = j * TILE + lax.broadcasted_iota(jnp.int32, (TILE, TILE), 0)
    query = i * TILE + lax.broadcasted_iota(jnp.int32, (TILE, TILE), 1)
    return (key >= lo) & (key <= query)


def forward_kernel(bounds, q_ref, k_ref, v_ref, lo_ref, o_ref, lse_ref, acc):
    pair, i = pl.program_id(0), pl.program_id(1)
    q = q_ref[...].reshape(TILE, HD)
    lo = lo_ref[...]
    factor = SCALE * LOG2E

    def step(j, carry, masked):
        m, l = carry
        s = dot_nt(tile_of(k_ref, j), q) * factor
        if masked:
            s = jnp.where(mask_of(i, j, lo), s, MASKED)
        new = jnp.maximum(m, jnp.max(s, axis=0, keepdims=True))
        p = jnp.exp2(s - new)
        old = jnp.exp2(m - new)
        acc[...] = acc[...] * old + dot_tn(tile_of(v_ref, j), p.astype(bf16))
        return new, l * old + jnp.sum(p, axis=0, keepdims=True)

    acc[...] = jnp.zeros_like(acc)
    carry = (jnp.full((1, TILE), MASKED, f32), jnp.zeros((1, TILE), f32))
    start = bounds[pair, 0, i]
    middle = bounds[pair, 1, i]
    carry = lax.fori_loop(start, middle, lambda j, c: step(j, c, True), carry)
    carry = lax.fori_loop(middle, i, lambda j, c: step(j, c, False), carry)
    m, l = step(i, carry, True)
    o_ref[...] = (acc[...] / l).T.astype(bf16).reshape(o_ref.shape)
    lse_ref[...] = m + jnp.log2(l)


def attend(qkv, bounds, low):
    seq, pairs, rows, _ = qkv.shape
    length = seq * rows
    blocks, per = length // TILE, TILE // rows
    whole = lambda part: pl.BlockSpec((seq, None, rows, HD), lambda p, i, b: (0, p, 0, part))
    line = pl.BlockSpec((None, 1, TILE), lambda p, i, b: (p, 0, i))
    block = pl.BlockSpec((per, None, rows, HD), lambda p, i, b: (i, p, 0, 0))
    return pl.pallas_call(
        forward_kernel,
        grid_spec=pltpu.PrefetchScalarGridSpec(
            num_scalar_prefetch=1,
            grid=(pairs, blocks),
            in_specs=[block, whole(1), whole(2), line],
            out_specs=[block, line],
            scratch_shapes=[pltpu.VMEM((HD, TILE), f32)],
        ),
        out_shape=[
            jax.ShapeDtypeStruct((seq, pairs, rows, HD), bf16),
            jax.ShapeDtypeStruct((pairs, 1, length), f32),
        ],
        compiler_params=pltpu.CompilerParams(vmem_limit_bytes=32 * 1024 * 1024),
        cost_estimate=QUICK,
        name="attend",
    )(bounds, qkv, qkv, qkv, low)


def backward_kernel(pair, bounds, q_ref, k_ref, v_ref, do_ref, o_ref, lse_ref, lo_ref, out_ref, dq, dk, dv, delta):
    j = pl.program_id(0)
    k = k_ref[...].reshape(TILE, HD)
    v = v_ref[...].reshape(TILE, HD)
    factor = SCALE * LOG2E

    def step(i, masked):
        rows = pl.ds(pl.multiple_of(i * TILE, TILE), TILE)
        q = tile_of(q_ref, i)
        do = tile_of(do_ref, i)
        s = dot_nt(k, q) * factor
        p = jnp.exp2(s - lse_ref[:, rows])
        if masked:
            p = jnp.where(mask_of(i, j, lo_ref[:, rows]), p, 0.0)
        dp = dot_nt(v, do)
        ds = (p * (dp - delta[:, rows])).astype(bf16)
        dv[...] += dot_nn(p.astype(bf16), do)
        dk[...] += dot_nn(ds, q)
        dq[rows, :] += dot_tn(ds, k)

    @pl.when(j == 0)
    def _():
        dq[...] = jnp.zeros_like(dq)

        @pl.loop(0, pl.num_programs(0))
        def _(i):
            rows = pl.ds(pl.multiple_of(i * TILE, TILE), TILE)
            product = tile_of(do_ref, i).astype(f32) * tile_of(o_ref, i).astype(f32)
            delta[:, rows] = jnp.sum(product.T, axis=0, keepdims=True)

    dk[...] = jnp.zeros_like(dk)
    dv[...] = jnp.zeros_like(dv)
    step(j, True)
    middle = bounds[pair, 2, j]
    end = bounds[pair, 3, j]

    @pl.loop(j + 1, middle)
    def _(i):
        step(i, False)

    @pl.loop(middle, end)
    def _(i):
        step(i, True)

    own = pl.ds(pl.multiple_of(j * TILE, TILE), TILE)
    shape = out_ref.shape[:-1] + (HD,)
    out_ref[:, :, :HD] = (dq[own, :] * SCALE).astype(bf16).reshape(shape)
    out_ref[:, :, HD : 2 * HD] = (dk[...] * SCALE).astype(bf16).reshape(shape)
    out_ref[:, :, 2 * HD :] = dv[...].astype(bf16).reshape(shape)


def attend_back(pair, qkv, grad, mixed, lse, bounds, low):
    seq, _, rows, _ = qkv.shape
    length = seq * rows
    blocks, per = length // TILE, TILE // rows
    whole = pl.BlockSpec((seq, None, rows, HD), lambda j, b: (0, pair, 0, 0))
    line = pl.BlockSpec((None, 1, length), lambda j, b: (pair, 0, 0))
    block = lambda part: pl.BlockSpec((per, None, rows, HD), lambda j, b: (j, pair, 0, part))
    return pl.pallas_call(
        functools.partial(backward_kernel, pair),
        grid_spec=pltpu.PrefetchScalarGridSpec(
            num_scalar_prefetch=1,
            grid=(blocks,),
            in_specs=[whole, block(1), block(2), whole, whole, line, line],
            out_specs=pl.BlockSpec((per, None, rows, 3 * HD), lambda j, b: (j, 0, 0, 0)),
            scratch_shapes=[
                pltpu.VMEM((length, HD), f32),
                pltpu.VMEM((TILE, HD), f32),
                pltpu.VMEM((TILE, HD), f32),
                pltpu.VMEM((1, length), f32),
            ],
        ),
        out_shape=jax.ShapeDtypeStruct((seq, 1, rows, 3 * HD), bf16),
        compiler_params=pltpu.CompilerParams(vmem_limit_bytes=40 * 1024 * 1024),
        cost_estimate=QUICK,
        name="attend_back",
    )(bounds, qkv, qkv, qkv, grad, mixed, lse, low)


def key_bounds(segments):
    length = segments.shape[0]
    blocks = length // TILE
    place = jnp.arange(length, dtype=jnp.int32)
    start = jnp.zeros_like(place)
    for value in range(1, 4):
        earlier = jnp.sum(segments < value, dtype=jnp.int32)
        start = jnp.where(segments == value, earlier, start)
    low = jnp.maximum(start, place - (WINDOW - 1))
    index = jnp.arange(blocks, dtype=jnp.int32)
    first = low[::TILE]
    last = low[TILE - 1 :: TILE]
    begin = first // TILE
    middle = jnp.clip((last + TILE - 1) // TILE, begin, index)
    full = (last[None, :] <= index[:, None] * TILE) & (index[None, :] > index[:, None])
    some = (first[None, :] < (index[:, None] + 1) * TILE) & (index[None, :] > index[:, None])
    back_middle = index + 1 + jnp.sum(full, axis=1, dtype=jnp.int32)
    back_end = index + 1 + jnp.sum(some, axis=1, dtype=jnp.int32)
    return low[None], jnp.stack([begin, middle, back_middle, back_end])


def to_heads(rows, micros):
    seq = lax.axis_size("seq")
    count, width = rows.shape[0] // micros, rows.shape[1] // H
    split = rows.reshape(micros, count, H, width).transpose(2, 0, 1, 3)
    split = split.reshape(seq, H * micros // seq, count, width)
    return lax.all_to_all(split, "seq", 0, 0, tiled=True)


def to_rows(whole):
    return lax.all_to_all(whole, "seq", 0, 0, tiled=True)


def rows_of(got, micros):
    count, width = got.shape[2], got.shape[3]
    return got.reshape(H, micros, count, width).transpose(1, 2, 0, 3).reshape(micros * count, H * width)


def norm_scale(values):
    return lax.rsqrt(jnp.mean(values * values, axis=-1, keepdims=True) + EPSILON)


def norm_backward(grad_in, values, row_scale, gain):
    normed = values * row_scale
    gain_grad = jnp.sum(grad_in * normed, axis=0)
    scaled = grad_in * gain
    inner = jnp.mean(scaled * normed, axis=-1, keepdims=True)
    return row_scale * (scaled - normed * inner), gain_grad


def nt(a, b):
    return jnp.einsum("re,de->rd", a, b, preferred_element_type=f32)


def shards(tokens, segment_ids, w_qkv, w_out, w_gate_up, w_down, gain_attn, gain_mlp, cotangent):
    rows = tokens.shape[2]
    seq = lax.axis_size("seq")
    gather = lambda w: lax.all_gather(w, ("dp", "seq"), axis=0, tiled=True)
    groups = MB if H % seq == 0 else 1
    micros = MB // groups
    pairs = H * micros // seq
    size = micros * rows
    of = lambda array, g: array[g * size : (g + 1) * size]

    x = tokens.reshape(MB * rows, D).astype(f32)
    cot = cotangent.reshape(MB * rows, D)
    bounds, low = [], []
    for g in range(groups):
        made = []
        for k in range(pairs):
            micro = g if micros == 1 else lax.rem(lax.axis_index("seq") * pairs + k, micros)
            made.append(key_bounds(segment_ids[g, 0] if micros == 1 else pick(segment_ids[:, 0], micro, 0)))
        low.append(jnp.stack([m[0] for m in made]))
        bounds.append(jnp.stack([m[1] for m in made]))

    order_qkv = w_qkv.reshape(-1, 3, H, HD).transpose(0, 2, 1, 3).reshape(w_qkv.shape)
    full_qkv = gather(order_qkv)
    all_gains = gather_small(jnp.stack([gain_attn, gain_mlp]))
    gains = all_gains.astype(f32)
    gain_a, gain_m = gains[0], gains[1]
    scale_a = norm_scale(x)
    h_attn = (x * scale_a * gain_a).astype(bf16)
    soon = Gather([w_gate_up[:, :FF], w_out], False)
    later = Gather([w_gate_up[:, FF:], w_down.reshape(w_qkv.shape[0], -1)], True)
    far = len(soon.far)

    soon.wait(all_gains, h_attn)
    soon.far_step(0)
    for n in range(1, far):
        later.wait(*soon.values())
        soon.far_step(n)
        later.far_step(n - 1)
    ready = soon.values() + later.values()
    soon.wait(*ready)
    soon.near_step(0)
    later.wait(*ready)
    later.far_step(far - 1)
    later.near_step(0)
    h_kept = after(h_attn, *later.values(), *soon.values())
    saved, attended, arrived = [], [], []

    def project(g, *others):
        qkv_rows = jnp.dot(of(after(h_kept, *others), g), full_qkv, preferred_element_type=f32).astype(bf16)
        arrived.append(to_heads(qkv_rows, micros))

    def attention(g, others):
        qkv = after(arrived[g], *others)
        mixed, lse = attend(qkv, bounds[g], low[g])
        saved.append((qkv, mixed, lse))
        return to_rows(mixed)

    project(0)
    ready = soon.values() + later.values()
    for w in (soon, later):
        w.wait(*ready)
        w.near_step(1)
    back_rows = attention(0, soon.values() + later.values())
    soon.near_step(2)
    later.near_step(2)
    full_gate, full_out = soon.finish()
    full_up, flat_down = later.finish()
    attended.append(rows_of(after(back_rows, full_gate, full_out, full_up, flat_down), micros))
    if groups > 1:
        project(1, attended[0])

    parts = []
    grads = []
    rows_grad = []
    mark = ()

    def back_of(g, *others):
        qkv, mixed, lse = saved[g]
        pieces = []
        for k in range(pairs):
            back = attend_back(k, after(qkv, *others), grads[g], mixed, lse, bounds[g], low[g])
            others = (back,)
            pieces.append(to_rows(back))
        rows_grad.append(pieces)
        return back

    for g in range(groups):
        final = g == groups - 1
        mid = of(x, g) + jnp.dot(after(attended[g], *mark), full_out, preferred_element_type=f32)
        scale_m = norm_scale(mid)
        h_mlp = (mid * scale_m * gain_m).astype(bf16)
        gate = jnp.dot(h_mlp, full_gate, preferred_element_type=f32)
        up = jnp.dot(after(h_mlp, *mark), full_up, preferred_element_type=f32)
        sig = jax.nn.sigmoid(gate)
        act = (gate * sig * up).astype(bf16)
        parts.append([mid, scale_m, h_mlp, act])
        mark = (act,)
        if g == 0:
            full_down = after(flat_down, act).reshape(FF, D)
        if final:
            acts = jnp.concatenate([p[3] for p in parts], axis=0)
            sides = jnp.concatenate([p[2] for p in parts], axis=0)
            down = Reduce(None, cot, False, product=tn(after(acts, *mark, *grads), cot).astype(bf16))
            mark = (down.cross(),)
        if g:
            mark = (back_of(g - 1, *mark),)
        if final:
            mark = (down.send(*mark),)
        if g:
            mark = mark + (rows_grad[-1][0],)
        cot_part = of(cot, g)
        grad_act = nt(after(cot_part, *mark), full_down)
        grad_gate = (grad_act * up * sig * (1.0 + gate * (1.0 - sig))).astype(bf16)
        grad_up = (grad_act * (gate * sig)).astype(bf16)
        parts[g] += [grad_gate, grad_up]
        mark = (grad_gate, grad_up)
        if not final:
            back_rows = attention(g + 1, mark)
            mark = (saved[-1][1],)
        if final:
            gate_r = Reduce(pieces_of(sides, False), jnp.concatenate([p[4] for p in parts], axis=0), False)
            up_r = Reduce(pieces_of(sides, True), jnp.concatenate([p[5] for p in parts], axis=0), True)
            mark = (up_r.cross(*mark),)
            mark = (gate_r.cross(*mark),)
        if final:
            mark = (up_r.send(*mark, *[r for pieces in rows_grad for r in pieces]),)
        half_grad = nt(after(grad_gate, *mark), full_gate)
        mark = (half_grad,)
        grad_h_mlp = half_grad + nt(after(grad_up, *mark), full_up)
        grad_mid_norm, gain_part = norm_backward(grad_h_mlp, mid, scale_m, gain_m)
        grad_mid = cot_part.astype(f32) + grad_mid_norm
        grad_branch = grad_mid.astype(bf16)
        arrivals = [r for pieces in rows_grad for r in pieces]
        grad_rows = nt(after(grad_branch, *arrivals), full_out).astype(bf16)
        if not final:
            attended.append(rows_of(after(back_rows, grad_rows), micros))
        grads.append(to_heads(grad_rows, micros))
        parts[g] += [grad_mid, grad_branch, gain_part]
        mark = (grad_rows,)

    attended_all = jnp.concatenate(attended, axis=0)
    out_r = Reduce(pieces_of(attended_all, False), jnp.concatenate([p[7] for p in parts], axis=0), False)
    early = [down, up_r, gate_r, out_r]
    mark = (gate_r.send(*mark),)
    mark = (out_r.cross(*mark),)
    mark = (down.keep(*mark),)
    down.second(grads[-1])
    mark = (back_of(groups - 1, *mark),)
    mark = (up_r.keep(*mark),)
    up_r.second()
    mark = (out_r.send(*mark), rows_grad[-1][0])
    for r in (gate_r, out_r):
        mark = (r.keep(*mark),)
        r.second()
    layer_outs, grad_qkv, grad_tokens, gain_a_parts = [], [], [], []

    def finish_tokens(g, *others):
        grad_h_attn = nt(after(grad_qkv[g], *others), full_qkv)
        grad_norm, gain_part = norm_backward(grad_h_attn, of(x, g), of(scale_a, g), gain_a)
        grad_tokens.append(parts[g][6] + grad_norm)
        gain_a_parts.append(gain_part)
        return grad_tokens[-1]

    for g in range(groups):
        act = after(parts[g][3], *mark)
        layer_outs.append((parts[g][0] + jnp.dot(act, full_down, preferred_element_type=f32)).astype(bf16))
        mark = (layer_outs[-1],)
    mark = mark + tuple(rows_grad[-1]) + tuple(r.total for r in early)
    first = Finish(early, *mark)
    h_sides = [pieces_of(h_kept, False), pieces_of(h_kept, True)]
    for g in range(groups - 1):
        grad_qkv.append(rows_of(jnp.concatenate(rows_grad[g], axis=1), micros))
    grad_qkv.append(rows_of(jnp.concatenate([after(r, *mark) for r in rows_grad[-1]], axis=1), micros))
    last_rows = grad_qkv[-1]
    all_qkv = jnp.concatenate(grad_qkv, axis=0)
    half = 3 * D // 2
    late = [Reduce(h_sides[0], all_qkv[:, :half], False), Reduce(h_sides[1], all_qkv[:, half:], True)]
    for r in late:
        mark = (r.cross(*mark),)
    for g in range(groups - 1):
        mark = (finish_tokens(g, *mark),)
    for r in late:
        mark = (r.send(*mark),)
    first.step(0, hold=mark)
    g = groups - 1
    grad_h_attn = nt(after(last_rows, *mark), full_qkv)
    grad_norm, gain_part = norm_backward(grad_h_attn, of(x, g), of(scale_a, g), gain_a)
    grad_tokens.append(parts[g][6] + grad_norm)
    gain_a_parts.append(gain_part)
    mark = (grad_tokens[-1], first.total)
    for r in late:
        mark = (r.keep(*mark),)
    for r in late:
        r.second(*mark)
    gain_sums = ScatterSmall(jnp.stack([sum(gain_a_parts), sum(p[8] for p in parts)]))
    second = Finish(late)
    for n in range(far):
        if n:
            first.step(n, hold=mark)
        gain_sums.step(digits_of("seq")[-2 - n], second.total)
        second.step(n)
    gain_grads = gain_sums.terms
    down_grad, up_grad, gate_grad, out_grad = first.results()
    qkv_grad = jnp.concatenate(second.results(), axis=1).reshape(-1, H, 3, HD).transpose(0, 2, 1, 3)
    join = lambda arrays: jnp.concatenate(arrays, axis=0).reshape(MB, 1, rows, D)

    return (
        join(layer_outs),
        join(grad_tokens),
        qkv_grad.reshape(-1, 3 * D),
        out_grad,
        jnp.concatenate([gate_grad, up_grad], axis=1),
        down_grad,
        gain_grads[0],
        gain_grads[1],
    )


def solution(mesh):
    by_rows = P(("dp", "seq"), None)
    by_tokens = P(None, "dp", "seq", None)
    vector = P(("dp", "seq"))
    return jax.shard_map(
        shards,
        mesh=mesh,
        in_specs=(by_tokens, P(None, "dp", None), by_rows, by_rows, by_rows, by_rows, vector, vector, by_tokens),
        out_specs=(by_tokens, by_tokens, by_rows, by_rows, by_rows, by_rows, vector, vector),
        check_vma=False,
    )
```

```python
import functools
import math

import jax
import jax.numpy as jnp
from jax import lax
from jax.experimental import pallas as pl
from jax.experimental.pallas import tpu as pltpu
from jax.sharding import PartitionSpec as P

D = 2048
H = 16
HD = 128
FF = 5504
WINDOW = 2048
MB = 2
TILE = 512

EPSILON = 1e-05
MASKED = -1e30
LOG2E = 1.4426950408889634
SCALE = 1.0 / math.sqrt(HD)

QUICK = pl.CostEstimate(flops=1024, bytes_accessed=1024, transcendentals=0)

bf16 = jnp.bfloat16
f32 = jnp.float32


def digits_of(axis):
    size = lax.axis_size(axis)
    return [(axis, 1 << bit) for bit in reversed(range(size.bit_length() - 1))]


def digit_index(digit):
    axis, stride = digit
    return lax.rem(lax.axis_index(axis) // stride, 2)


def swap(block, digit):
    axis, stride = digit
    return lax.ppermute(block, axis, [(i, i ^ stride) for i in range(lax.axis_size(axis))])


def pick(array, index, dim):
    return lax.dynamic_index_in_dim(array, index, dim, keepdims=False)


def scatter_digit(parts, digit, dim, out_type, hold=()):
    own = digit_index(digit)
    got = swap(pick(parts, 1 - own, dim), digit)
    if hold:
        got = lax.optimization_barrier((got,) + tuple(hold))[0]
    return (pick(parts, own, dim).astype(f32) + got.astype(f32)).astype(out_type)


def gather_small(block):
    for digit in reversed(digits_of("dp") + digits_of("seq")):
        got = swap(block, digit)
        low = digit_index(digit) == 0
        block = jnp.concatenate([jnp.where(low, block, got), jnp.where(low, got, block)], axis=-1)
    return block


class ScatterSmall:
    def __init__(self, terms):
        self.digits = digits_of("dp") + digits_of("seq")
        self.terms = terms.reshape((terms.shape[0],) + (2,) * len(self.digits) + (-1,))
        for digit in digits_of("dp")[::-1] + digits_of("seq")[-1:]:
            self.step(digit)

    def step(self, digit, *others):
        dim = 1 + self.digits.index(digit)
        self.digits = [d for d in self.digits if d != digit]
        self.terms = scatter_digit(after(self.terms, *others), digit, dim, f32)


SLOTS = 8


def place_kernel(count, rows, widths, target, *refs):
    sources, outs = refs[: -3 - len(widths)], refs[-3 - len(widths) : -3]
    held, in_sems, out_sems = refs[-3:]
    per = sources[0].shape[0] // rows

    def read(n):
        source = sources[n // per].at[pl.ds((n % per) * rows, rows), :]
        return pltpu.make_async_copy(source, held.at[n % SLOTS], in_sems.at[n % SLOTS])

    def writes(n):
        start, left = pl.multiple_of(target[n], 16), 0
        copies = []
        for k, width in enumerate(widths):
            source = held.at[n % SLOTS, :, pl.ds(left, width)]
            copies.append(pltpu.make_async_copy(source, outs[k].at[pl.ds(start, rows), :], out_sems.at[n % SLOTS, k]))
            left += width
        return copies

    lag = SLOTS // 2
    for n in range(min(lag, count)):
        read(n).start()
    for n in range(count):
        if n >= lag:
            for copy in writes(n - lag):
                copy.wait()
        if n + lag < count:
            read(n + lag).start()
        read(n).wait()
        for copy in writes(n):
            copy.start()
    for n in range(max(count - lag, 0), count):
        for copy in writes(n):
            copy.wait()


class Gather:
    def __init__(self, blocks, seq_first):
        self.rows, self.widths = blocks[0].shape[0], [b.shape[1] for b in blocks]
        fast, height = digits_of("seq")[-1:], digits_of("dp")[:-1]
        self.far = digits_of("seq")[:-1]
        self.near = (fast + height if seq_first else height + fast) + digits_of("dp")[-1:]
        self.buffers = [(jnp.concatenate(blocks, axis=1), ())]

    def values(self):
        return [b for b, _ in self.buffers]

    def wait(self, *others):
        self.buffers = [(after(b, *others), d) for b, d in self.buffers]

    def far_step(self, n):
        (block, digits), digit = self.buffers[0], self.far[n]
        self.buffers = [(jnp.concatenate([block, swap(block, digit)], axis=0), digits + (digit,))]

    def near_step(self, n):
        digit = self.near[n]
        self.buffers = self.buffers + [(swap(b, digit), d + (digit,)) for b, d in self.buffers]

    def finish(self):
        offsets = []
        rows = self.rows
        stride_of = lambda digit: digit[1] * (lax.axis_size("seq") if digit[0] == "dp" else 1)
        for _, digits in self.buffers:
            near = sum(stride_of(d) for d in digits if d not in self.far)
            for n in range(1 << len(self.far)):
                offsets.append(near + sum(stride_of(d) for bit, d in enumerate(self.far) if n >> bit & 1))
        mine = lax.axis_index("dp") * lax.axis_size("seq") + lax.axis_index("seq")
        targets = lax.bitwise_xor(jnp.asarray(offsets, jnp.int32), mine.astype(jnp.int32)) * rows
        count = len(offsets)
        return pl.pallas_call(
            functools.partial(place_kernel, count, rows, self.widths),
            grid_spec=pltpu.PrefetchScalarGridSpec(
                num_scalar_prefetch=1,
                in_specs=[pl.BlockSpec(memory_space=pl.ANY)] * len(self.buffers),
                out_specs=[pl.BlockSpec(memory_space=pl.ANY)] * len(self.widths),
                scratch_shapes=[
                    pltpu.VMEM((SLOTS, rows, sum(self.widths)), bf16),
                    pltpu.SemaphoreType.DMA((SLOTS,)),
                    pltpu.SemaphoreType.DMA((SLOTS, len(self.widths))),
                ],
            ),
            out_shape=[jax.ShapeDtypeStruct((count * rows, width), bf16) for width in self.widths],
            compiler_params=pltpu.CompilerParams(vmem_limit_bytes=16 * 1024 * 1024),
            cost_estimate=QUICK,
            name="place",
        )(targets, *self.values())


def tn(a, b):
    return lax.dot_general(a, b, (((0,), (0,)), ((), ())), preferred_element_type=f32)


def after(value, *others):
    return lax.optimization_barrier((value,) + others)[0]


def pieces_of(side, seq_first):
    dp, seq = lax.axis_size("dp"), lax.axis_size("seq")
    tokens, total = side.shape
    if seq_first:
        pieces = side.reshape(tokens, dp // 2, 2, seq // 2, 2, -1).transpose(2, 0, 4, 1, 3, 5)
    else:
        pieces = side.reshape(tokens, dp // 2, 2, -1).transpose(2, 0, 1, 3)
    return pieces.reshape(2, tokens, total // 2)


class Reduce:
    def __init__(self, pieces, cols_side, seq_first, product=None):
        self.pieces, self.cols_side, self.seq_first, self.product = pieces, cols_side, seq_first, product
        self.half = product.shape[0] // 4 if pieces is None else pieces.shape[2] // 2
        self.own = self.half * 4 // (lax.axis_size("dp") * lax.axis_size("seq"))
        self.core, self.height = digits_of("dp")[-1], digits_of("dp")[0]
        self.fast, self.far = digits_of("seq")[-1], digits_of("seq")[:-1]
        self.first = self.fast if seq_first else self.height
        self.c, self.mine = digit_index(self.core), digit_index(self.first)

    def term(self, core_index, index, others):
        if self.pieces is None:
            parts = pick(after(self.product, *others).reshape(2, 2, self.half, -1), core_index, 1)
            return (parts.reshape(2 * self.half, -1) if index is None else pick(parts, index, 0)).astype(f32)
        side = pick(after(self.pieces, *others), core_index, 0)
        if index is not None:
            side = lax.dynamic_slice_in_dim(side, index * self.half, self.half, 1)
        return tn(side, self.cols_side)

    def cross(self, *others):
        term = self.term(1 - self.c, None, others).astype(bf16)
        self.got = swap(term, self.core)
        return term

    def got_part(self, index):
        return lax.dynamic_slice_in_dim(self.got, index * self.half, self.half, 0).astype(f32)

    def send(self, *others):
        away = (self.term(self.c, 1 - self.mine, others) + self.got_part(1 - self.mine)).astype(bf16)
        self.away = swap(away, self.first)
        return away

    def keep(self, *others):
        total = self.term(self.c, self.mine, others) + self.got_part(self.mine) + self.away.astype(f32)
        self.total = total.astype(bf16)
        return self.total

    def second(self, *others):
        cols = self.cols_side.shape[1]
        total = after(self.total, *others)
        if self.seq_first:
            self.total = scatter_digit(total.reshape(2, -1, cols), self.height, 0, bf16)
        else:
            self.total = scatter_digit(total.reshape(-1, 2, self.own, cols), self.fast, 1, bf16)
        return self.total


class Finish:
    def __init__(self, reduces, *others):
        self.reduces, self.far = reduces, reduces[0].far
        self.count = 1 << len(self.far)
        self.unit = D // (lax.axis_size("dp") * lax.axis_size("seq"))
        totals = [after(r.total, *others).reshape(self.count, self.unit, -1) for r in reduces]
        self.widths = [t.shape[2] for t in totals]
        self.total = jnp.concatenate(totals, axis=2)

    def step(self, n, *others, hold=()):
        total = after(self.total, *others).reshape(-1, 2, self.unit, sum(self.widths))
        self.total = scatter_digit(total, self.far[-1 - n], 1, f32 if n == len(self.far) - 1 else bf16, hold)
        return self.total

    def results(self):
        left = 0
        results = []
        for r, width in zip(self.reduces, self.widths):
            results.append(self.total[0, :, left : left + width].reshape(r.own, -1))
            left += width
        return results


def dot_nt(a, b):
    return lax.dot_general(a, b, (((1,), (1,)), ((), ())), preferred_element_type=f32)


def dot_tn(a, b):
    return lax.dot_general(a, b, (((0,), (0,)), ((), ())), preferred_element_type=f32)


def dot_nn(a, b):
    return lax.dot_general(a, b, (((1,), (0,)), ((), ())), preferred_element_type=f32)


def tile_of(ref, index):
    per = TILE // ref.shape[1]
    return ref[pl.ds(index * per, per)].reshape(TILE, HD)


def mask_of(i, j, lo):
    key = j * TILE + lax.broadcasted_iota(jnp.int32, (TILE, TILE), 0)
    query = i * TILE + lax.broadcasted_iota(jnp.int32, (TILE, TILE), 1)
    return (key >= lo) & (key <= query)


def forward_kernel(bounds, q_ref, k_ref, v_ref, lo_ref, o_ref, lse_ref, acc):
    pair, i = pl.program_id(0), pl.program_id(1)
    q = q_ref[...].reshape(TILE, HD)
    lo = lo_ref[...]
    factor = SCALE * LOG2E

    def step(j, carry, masked):
        m, l = carry
        s = dot_nt(tile_of(k_ref, j), q) * factor
        if masked:
            s = jnp.where(mask_of(i, j, lo), s, MASKED)
        new = jnp.maximum(m, jnp.max(s, axis=0, keepdims=True))
        p = jnp.exp2(s - new)
        old = jnp.exp2(m - new)
        acc[...] = acc[...] * old + dot_tn(tile_of(v_ref, j), p.astype(bf16))
        return new, l * old + jnp.sum(p, axis=0, keepdims=True)

    acc[...] = jnp.zeros_like(acc)
    carry = (jnp.full((1, TILE), MASKED, f32), jnp.zeros((1, TILE), f32))
    start = bounds[pair, 0, i]
    middle = bounds[pair, 1, i]
    carry = lax.fori_loop(start, middle, lambda j, c: step(j, c, True), carry)
    carry = lax.fori_loop(middle, i, lambda j, c: step(j, c, False), carry)
    m, l = step(i, carry, True)
    o_ref[...] = (acc[...] / l).T.astype(bf16).reshape(o_ref.shape)
    lse_ref[...] = m + jnp.log2(l)


def attend(qkv, bounds, low):
    seq, pairs, rows, _ = qkv.shape
    length = seq * rows
    blocks, per = length // TILE, TILE // rows
    whole = lambda part: pl.BlockSpec((seq, None, rows, HD), lambda p, i, b: (0, p, 0, part))
    line = pl.BlockSpec((None, 1, TILE), lambda p, i, b: (p, 0, i))
    block = pl.BlockSpec((per, None, rows, HD), lambda p, i, b: (i, p, 0, 0))
    return pl.pallas_call(
        forward_kernel,
        grid_spec=pltpu.PrefetchScalarGridSpec(
            num_scalar_prefetch=1,
            grid=(pairs, blocks),
            in_specs=[block, whole(1), whole(2), line],
            out_specs=[block, line],
            scratch_shapes=[pltpu.VMEM((HD, TILE), f32)],
        ),
        out_shape=[
            jax.ShapeDtypeStruct((seq, pairs, rows, HD), bf16),
            jax.ShapeDtypeStruct((pairs, 1, length), f32),
        ],
        compiler_params=pltpu.CompilerParams(vmem_limit_bytes=32 * 1024 * 1024),
        cost_estimate=QUICK,
        name="attend",
    )(bounds, qkv, qkv, qkv, low)


def backward_kernel(pair, bounds, q_ref, k_ref, v_ref, do_ref, o_ref, lse_ref, lo_ref, out_ref, dq, dk, dv, delta):
    j = pl.program_id(0)
    k = k_ref[...].reshape(TILE, HD)
    v = v_ref[...].reshape(TILE, HD)
    factor = SCALE * LOG2E

    def step(i, masked):
        rows = pl.ds(pl.multiple_of(i * TILE, TILE), TILE)
        q = tile_of(q_ref, i)
        do = tile_of(do_ref, i)
        s = dot_nt(k, q) * factor
        p = jnp.exp2(s - lse_ref[:, rows])
        if masked:
            p = jnp.where(mask_of(i, j, lo_ref[:, rows]), p, 0.0)
        dp = dot_nt(v, do)
        ds = (p * (dp - delta[:, rows])).astype(bf16)
        dv[...] += dot_nn(p.astype(bf16), do)
        dk[...] += dot_nn(ds, q)
        dq[rows, :] += dot_tn(ds, k)

    @pl.when(j == 0)
    def _():
        dq[...] = jnp.zeros_like(dq)

        @pl.loop(0, pl.num_programs(0))
        def _(i):
            rows = pl.ds(pl.multiple_of(i * TILE, TILE), TILE)
            product = tile_of(do_ref, i).astype(f32) * tile_of(o_ref, i).astype(f32)
            delta[:, rows] = jnp.sum(product.T, axis=0, keepdims=True)

    dk[...] = jnp.zeros_like(dk)
    dv[...] = jnp.zeros_like(dv)
    step(j, True)
    middle = bounds[pair, 2, j]
    end = bounds[pair, 3, j]

    @pl.loop(j + 1, middle)
    def _(i):
        step(i, False)

    @pl.loop(middle, end)
    def _(i):
        step(i, True)

    own = pl.ds(pl.multiple_of(j * TILE, TILE), TILE)
    shape = out_ref.shape[:-1] + (HD,)
    out_ref[:, :, :HD] = (dq[own, :] * SCALE).astype(bf16).reshape(shape)
    out_ref[:, :, HD : 2 * HD] = (dk[...] * SCALE).astype(bf16).reshape(shape)
    out_ref[:, :, 2 * HD :] = dv[...].astype(bf16).reshape(shape)


def attend_back(pair, qkv, grad, mixed, lse, bounds, low):
    seq, _, rows, _ = qkv.shape
    length = seq * rows
    blocks, per = length // TILE, TILE // rows
    whole = pl.BlockSpec((seq, None, rows, HD), lambda j, b: (0, pair, 0, 0))
    line = pl.BlockSpec((None, 1, length), lambda j, b: (pair, 0, 0))
    block = lambda part: pl.BlockSpec((per, None, rows, HD), lambda j, b: (j, pair, 0, part))
    return pl.pallas_call(
        functools.partial(backward_kernel, pair),
        grid_spec=pltpu.PrefetchScalarGridSpec(
            num_scalar_prefetch=1,
            grid=(blocks,),
            in_specs=[whole, block(1), block(2), whole, whole, line, line],
            out_specs=pl.BlockSpec((per, None, rows, 3 * HD), lambda j, b: (j, 0, 0, 0)),
            scratch_shapes=[
                pltpu.VMEM((length, HD), f32),
                pltpu.VMEM((TILE, HD), f32),
                pltpu.VMEM((TILE, HD), f32),
                pltpu.VMEM((1, length), f32),
            ],
        ),
        out_shape=jax.ShapeDtypeStruct((seq, 1, rows, 3 * HD), bf16),
        compiler_params=pltpu.CompilerParams(vmem_limit_bytes=40 * 1024 * 1024),
        cost_estimate=QUICK,
        name="attend_back",
    )(bounds, qkv, qkv, qkv, grad, mixed, lse, low)


def key_bounds(segments):
    length = segments.shape[0]
    blocks = length // TILE
    place = jnp.arange(length, dtype=jnp.int32)
    start = jnp.zeros_like(place)
    for value in range(1, 4):
        earlier = jnp.sum(segments < value, dtype=jnp.int32)
        start = jnp.where(segments == value, earlier, start)
    low = jnp.maximum(start, place - (WINDOW - 1))
    index = jnp.arange(blocks, dtype=jnp.int32)
    first = low[::TILE]
    last = low[TILE - 1 :: TILE]
    begin = first // TILE
    middle = jnp.clip((last + TILE - 1) // TILE, begin, index)
    full = (last[None, :] <= index[:, None] * TILE) & (index[None, :] > index[:, None])
    some = (first[None, :] < (index[:, None] + 1) * TILE) & (index[None, :] > index[:, None])
    back_middle = index + 1 + jnp.sum(full, axis=1, dtype=jnp.int32)
    back_end = index + 1 + jnp.sum(some, axis=1, dtype=jnp.int32)
    return low[None], jnp.stack([begin, middle, back_middle, back_end])


def to_heads(rows, micros):
    seq = lax.axis_size("seq")
    count, width = rows.shape[0] // micros, rows.shape[1] // H
    split = rows.reshape(micros, count, H, width).transpose(2, 0, 1, 3)
    split = split.reshape(seq, H * micros // seq, count, width)
    return lax.all_to_all(split, "seq", 0, 0, tiled=True)


def to_rows(whole):
    return lax.all_to_all(whole, "seq", 0, 0, tiled=True)


def rows_of(got, micros):
    count, width = got.shape[2], got.shape[3]
    return got.reshape(H, micros, count, width).transpose(1, 2, 0, 3).reshape(micros * count, H * width)


def norm_scale(values):
    return lax.rsqrt(jnp.mean(values * values, axis=-1, keepdims=True) + EPSILON)


def norm_backward(grad_in, values, row_scale, gain):
    normed = values * row_scale
    gain_grad = jnp.sum(grad_in * normed, axis=0)
    scaled = grad_in * gain
    inner = jnp.mean(scaled * normed, axis=-1, keepdims=True)
    return row_scale * (scaled - normed * inner), gain_grad


def nt(a, b):
    return jnp.einsum("re,de->rd", a, b, preferred_element_type=f32)


def shards(tokens, segment_ids, w_qkv, w_out, w_gate_up, w_down, gain_attn, gain_mlp, cotangent):
    rows = tokens.shape[2]
    seq = lax.axis_size("seq")
    gather = lambda w: lax.all_gather(w, ("dp", "seq"), axis=0, tiled=True)
    groups = MB if H % seq == 0 else 1
    micros = MB // groups
    pairs = H * micros // seq
    size = micros * rows
    of = lambda array, g: array[g * size : (g + 1) * size]

    x = tokens.reshape(MB * rows, D).astype(f32)
    cot = cotangent.reshape(MB * rows, D)
    bounds, low = [], []
    for g in range(groups):
        made = []
        for k in range(pairs):
            micro = g if micros == 1 else lax.rem(lax.axis_index("seq") * pairs + k, micros)
            made.append(key_bounds(segment_ids[g, 0] if micros == 1 else pick(segment_ids[:, 0], micro, 0)))
        low.append(jnp.stack([m[0] for m in made]))
        bounds.append(jnp.stack([m[1] for m in made]))

    order_qkv = w_qkv.reshape(-1, 3, H, HD).transpose(0, 2, 1, 3).reshape(w_qkv.shape)
    full_qkv = gather(order_qkv)
    all_gains = gather_small(jnp.stack([gain_attn, gain_mlp]))
    gains = all_gains.astype(f32)
    gain_a, gain_m = gains[0], gains[1]
    scale_a = norm_scale(x)
    h_attn = (x * scale_a * gain_a).astype(bf16)
    soon = Gather([w_gate_up[:, :FF], w_out], False)
    later = Gather([w_gate_up[:, FF:], w_down.reshape(w_qkv.shape[0], -1)], True)
    far = len(soon.far)

    soon.wait(all_gains, h_attn)
    soon.far_step(0)
    for n in range(1, far):
        later.wait(*soon.values())
        soon.far_step(n)
        later.far_step(n - 1)
    ready = soon.values() + later.values()
    soon.wait(*ready)
    soon.near_step(0)
    later.wait(*ready)
    later.far_step(far - 1)
    later.near_step(0)
    h_kept = after(h_attn, *later.values(), *soon.values())
    saved, attended, arrived = [], [], []

    def project(g, *others):
        qkv_rows = jnp.dot(of(after(h_kept, *others), g), full_qkv, preferred_element_type=f32).astype(bf16)
        arrived.append(to_heads(qkv_rows, micros))

    def attention(g, others):
        qkv = after(arrived[g], *others)
        mixed, lse = attend(qkv, bounds[g], low[g])
        saved.append((qkv, mixed, lse))
        return to_rows(mixed)

    project(0)
    ready = soon.values() + later.values()
    for w in (soon, later):
        w.wait(*ready)
        w.near_step(1)
    back_rows = attention(0, soon.values() + later.values())
    soon.near_step(2)
    later.near_step(2)
    full_gate, full_out = soon.finish()
    full_up, flat_down = later.finish()
    attended.append(rows_of(after(back_rows, full_gate, full_out, full_up, flat_down), micros))
    if groups > 1:
        project(1, attended[0])

    parts = []
    grads = []
    rows_grad = []
    mark = ()

    def back_of(g, *others):
        qkv, mixed, lse = saved[g]
        pieces = []
        for k in range(pairs):
            back = attend_back(k, after(qkv, *others), grads[g], mixed, lse, bounds[g], low[g])
            others = (back,)
            pieces.append(to_rows(back))
        rows_grad.append(pieces)
        return back

    for g in range(groups):
        final = g == groups - 1
        mid = of(x, g) + jnp.dot(after(attended[g], *mark), full_out, preferred_element_type=f32)
        scale_m = norm_scale(mid)
        h_mlp = (mid * scale_m * gain_m).astype(bf16)
        gate = jnp.dot(h_mlp, full_gate, preferred_element_type=f32)
        up = jnp.dot(after(h_mlp, *mark), full_up, preferred_element_type=f32)
        sig = jax.nn.sigmoid(gate)
        act = (gate * sig * up).astype(bf16)
        parts.append([mid, scale_m, h_mlp, act])
        mark = (act,)
        if g == 0:
            full_down = after(flat_down, act).reshape(FF, D)
        if final:
            acts = jnp.concatenate([p[3] for p in parts], axis=0)
            sides = jnp.concatenate([p[2] for p in parts], axis=0)
            down = Reduce(None, cot, False, product=tn(after(acts, *mark, *grads), cot).astype(bf16))
            mark = (down.cross(),)
        if g:
            mark = (back_of(g - 1, *mark),)
        if final:
            mark = (down.send(*mark),)
        if g:
            mark = mark + (rows_grad[-1][0],)
        cot_part = of(cot, g)
        grad_act = nt(after(cot_part, *mark), full_down)
        grad_gate = (grad_act * up * sig * (1.0 + gate * (1.0 - sig))).astype(bf16)
        grad_up = (grad_act * (gate * sig)).astype(bf16)
        parts[g] += [grad_gate, grad_up]
        mark = (grad_gate, grad_up)
        if not final:
            back_rows = attention(g + 1, mark)
            mark = (saved[-1][1],)
        if final:
            gate_r = Reduce(pieces_of(sides, False), jnp.concatenate([p[4] for p in parts], axis=0), False)
            up_r = Reduce(pieces_of(sides, True), jnp.concatenate([p[5] for p in parts], axis=0), True)
            mark = (up_r.cross(*mark),)
            mark = (gate_r.cross(*mark),)
        if final:
            mark = (up_r.send(*mark, *[r for pieces in rows_grad for r in pieces]),)
        half_grad = nt(after(grad_gate, *mark), full_gate)
        mark = (half_grad,)
        grad_h_mlp = half_grad + nt(after(grad_up, *mark), full_up)
        grad_mid_norm, gain_part = norm_backward(grad_h_mlp, mid, scale_m, gain_m)
        grad_mid = cot_part.astype(f32) + grad_mid_norm
        grad_branch = grad_mid.astype(bf16)
        arrivals = [r for pieces in rows_grad for r in pieces]
        grad_rows = nt(after(grad_branch, *arrivals), full_out).astype(bf16)
        if not final:
            attended.append(rows_of(after(back_rows, grad_rows), micros))
        grads.append(to_heads(grad_rows, micros))
        parts[g] += [grad_mid, grad_branch, gain_part]
        mark = (grad_rows,)

    attended_all = jnp.concatenate(attended, axis=0)
    out_r = Reduce(pieces_of(attended_all, False), jnp.concatenate([p[7] for p in parts], axis=0), False)
    early = [down, up_r, gate_r, out_r]
    mark = (gate_r.send(*mark),)
    mark = (out_r.cross(*mark),)
    mark = (down.keep(*mark),)
    down.second(grads[-1])
    mark = (back_of(groups - 1, *mark),)
    mark = (up_r.keep(*mark),)
    up_r.second()
    mark = (out_r.send(*mark), rows_grad[-1][0])
    for r in (gate_r, out_r):
        mark = (r.keep(*mark),)
        r.second()
    layer_outs, grad_qkv, grad_tokens, gain_a_parts = [], [], [], []

    def finish_tokens(g, *others):
        grad_h_attn = nt(after(grad_qkv[g], *others), full_qkv)
        grad_norm, gain_part = norm_backward(grad_h_attn, of(x, g), of(scale_a, g), gain_a)
        grad_tokens.append(parts[g][6] + grad_norm)
        gain_a_parts.append(gain_part)
        return grad_tokens[-1]

    for g in range(groups):
        act = after(parts[g][3], *mark)
        layer_outs.append((parts[g][0] + jnp.dot(act, full_down, preferred_element_type=f32)).astype(bf16))
        mark = (layer_outs[-1],)
    mark = mark + tuple(rows_grad[-1]) + tuple(r.total for r in early)
    first = Finish(early, *mark)
    mark = mark + (first.total,)
    h_sides = [pieces_of(h_kept, False), pieces_of(h_kept, True)]
    for g in range(groups - 1):
        grad_qkv.append(rows_of(jnp.concatenate(rows_grad[g], axis=1), micros))
    grad_qkv.append(rows_of(jnp.concatenate([after(r, *mark) for r in rows_grad[-1]], axis=1), micros))
    last_rows = grad_qkv[-1]
    all_qkv = jnp.concatenate(grad_qkv, axis=0)
    half = 3 * D // 2
    late = [Reduce(h_sides[0], all_qkv[:, :half], False), Reduce(h_sides[1], all_qkv[:, half:], True)]
    for r in late:
        mark = (r.cross(*mark),)
    for r in late:
        mark = (r.send(*mark),)
    first.step(0, hold=mark)
    mark = mark + (first.total,)
    for g in range(groups - 1):
        mark = (finish_tokens(g, *mark),)
    g = groups - 1
    grad_h_attn = nt(after(last_rows, *mark), full_qkv)
    grad_norm, gain_part = norm_backward(grad_h_attn, of(x, g), of(scale_a, g), gain_a)
    grad_tokens.append(parts[g][6] + grad_norm)
    gain_a_parts.append(gain_part)
    mark = (grad_tokens[-1], first.total)
    for r in late:
        mark = (r.keep(*mark),)
    for r in late:
        r.second(*mark)
    gain_sums = ScatterSmall(jnp.stack([sum(gain_a_parts), sum(p[8] for p in parts)]))
    second = Finish(late)
    for n in range(far):
        if n:
            first.step(n, hold=mark)
        gain_sums.step(digits_of("seq")[-2 - n], second.total)
        second.step(n)
    gain_grads = gain_sums.terms
    down_grad, up_grad, gate_grad, out_grad = first.results()
    qkv_grad = jnp.concatenate(second.results(), axis=1).reshape(-1, H, 3, HD).transpose(0, 2, 1, 3)
    join = lambda arrays: jnp.concatenate(arrays, axis=0).reshape(MB, 1, rows, D)

    return (
        join(layer_outs),
        join(grad_tokens),
        qkv_grad.reshape(-1, 3 * D),
        out_grad,
        jnp.concatenate([gate_grad, up_grad], axis=1),
        down_grad,
        gain_grads[0],
        gain_grads[1],
    )


def solution(mesh):
    by_rows = P(("dp", "seq"), None)
    by_tokens = P(None, "dp", "seq", None)
    vector = P(("dp", "seq"))
    return jax.shard_map(
        shards,
        mesh=mesh,
        in_specs=(by_tokens, P(None, "dp", None), by_rows, by_rows, by_rows, by_rows, vector, vector, by_tokens),
        out_specs=(by_tokens, by_tokens, by_rows, by_rows, by_rows, by_rows, vector, vector),
        check_vma=False,
    )
```

```python
import functools
import math

import jax
import jax.numpy as jnp
from jax import lax
from jax.experimental import pallas as pl
from jax.experimental.pallas import tpu as pltpu
from jax.sharding import PartitionSpec as P

D = 2048
H = 16
HD = 128
FF = 5504
WINDOW = 2048
MB = 2
TILE = 512

EPSILON = 1e-05
MASKED = -1e30
LOG2E = 1.4426950408889634
SCALE = 1.0 / math.sqrt(HD)

QUICK = pl.CostEstimate(flops=1024, bytes_accessed=1024, transcendentals=0)

bf16 = jnp.bfloat16
f32 = jnp.float32


def digits_of(axis):
    size = lax.axis_size(axis)
    return [(axis, 1 << bit) for bit in reversed(range(size.bit_length() - 1))]


def digit_index(digit):
    axis, stride = digit
    return lax.rem(lax.axis_index(axis) // stride, 2)


def swap(block, digit):
    axis, stride = digit
    return lax.ppermute(block, axis, [(i, i ^ stride) for i in range(lax.axis_size(axis))])


def pick(array, index, dim):
    return lax.dynamic_index_in_dim(array, index, dim, keepdims=False)


def scatter_digit(parts, digit, dim, out_type, hold=()):
    own = digit_index(digit)
    got = swap(pick(parts, 1 - own, dim), digit)
    if hold:
        got = lax.optimization_barrier((got,) + tuple(hold))[0]
    return (pick(parts, own, dim).astype(f32) + got.astype(f32)).astype(out_type)


def gather_small(block):
    for digit in reversed(digits_of("dp") + digits_of("seq")):
        got = swap(block, digit)
        low = digit_index(digit) == 0
        block = jnp.concatenate([jnp.where(low, block, got), jnp.where(low, got, block)], axis=-1)
    return block


class ScatterSmall:
    def __init__(self, terms):
        self.digits = digits_of("dp") + digits_of("seq")
        self.terms = terms.reshape((terms.shape[0],) + (2,) * len(self.digits) + (-1,))
        for digit in digits_of("dp")[::-1] + digits_of("seq")[-1:]:
            self.step(digit)

    def step(self, digit, *others):
        dim = 1 + self.digits.index(digit)
        self.digits = [d for d in self.digits if d != digit]
        self.terms = scatter_digit(after(self.terms, *others), digit, dim, f32)


SLOTS = 8


def place_kernel(count, rows, widths, target, *refs):
    sources, outs = refs[: -3 - len(widths)], refs[-3 - len(widths) : -3]
    held, in_sems, out_sems = refs[-3:]
    per = sources[0].shape[0] // rows

    def read(n):
        source = sources[n // per].at[pl.ds((n % per) * rows, rows), :]
        return pltpu.make_async_copy(source, held.at[n % SLOTS], in_sems.at[n % SLOTS])

    def writes(n):
        start, left = pl.multiple_of(target[n], 16), 0
        copies = []
        for k, width in enumerate(widths):
            source = held.at[n % SLOTS, :, pl.ds(left, width)]
            copies.append(pltpu.make_async_copy(source, outs[k].at[pl.ds(start, rows), :], out_sems.at[n % SLOTS, k]))
            left += width
        return copies

    lag = SLOTS // 2
    for n in range(min(lag, count)):
        read(n).start()
    for n in range(count):
        if n >= lag:
            for copy in writes(n - lag):
                copy.wait()
        if n + lag < count:
            read(n + lag).start()
        read(n).wait()
        for copy in writes(n):
            copy.start()
    for n in range(max(count - lag, 0), count):
        for copy in writes(n):
            copy.wait()


class Gather:
    def __init__(self, blocks, seq_first):
        self.rows, self.widths = blocks[0].shape[0], [b.shape[1] for b in blocks]
        fast, height = digits_of("seq")[-1:], digits_of("dp")[:-1]
        self.far = digits_of("seq")[:-1]
        self.near = (fast + height if seq_first else height + fast) + digits_of("dp")[-1:]
        self.buffers = [(jnp.concatenate(blocks, axis=1), ())]

    def values(self):
        return [b for b, _ in self.buffers]

    def wait(self, *others):
        self.buffers = [(after(b, *others), d) for b, d in self.buffers]

    def far_step(self, n):
        (block, digits), digit = self.buffers[0], self.far[n]
        self.buffers = [(jnp.concatenate([block, swap(block, digit)], axis=0), digits + (digit,))]

    def near_step(self, n):
        digit = self.near[n]
        self.buffers = self.buffers + [(swap(b, digit), d + (digit,)) for b, d in self.buffers]

    def finish(self):
        offsets = []
        rows = self.rows
        stride_of = lambda digit: digit[1] * (lax.axis_size("seq") if digit[0] == "dp" else 1)
        for _, digits in self.buffers:
            near = sum(stride_of(d) for d in digits if d not in self.far)
            for n in range(1 << len(self.far)):
                offsets.append(near + sum(stride_of(d) for bit, d in enumerate(self.far) if n >> bit & 1))
        mine = lax.axis_index("dp") * lax.axis_size("seq") + lax.axis_index("seq")
        targets = lax.bitwise_xor(jnp.asarray(offsets, jnp.int32), mine.astype(jnp.int32)) * rows
        count = len(offsets)
        return pl.pallas_call(
            functools.partial(place_kernel, count, rows, self.widths),
            grid_spec=pltpu.PrefetchScalarGridSpec(
                num_scalar_prefetch=1,
                in_specs=[pl.BlockSpec(memory_space=pl.ANY)] * len(self.buffers),
                out_specs=[pl.BlockSpec(memory_space=pl.ANY)] * len(self.widths),
                scratch_shapes=[
                    pltpu.VMEM((SLOTS, rows, sum(self.widths)), bf16),
                    pltpu.SemaphoreType.DMA((SLOTS,)),
                    pltpu.SemaphoreType.DMA((SLOTS, len(self.widths))),
                ],
            ),
            out_shape=[jax.ShapeDtypeStruct((count * rows, width), bf16) for width in self.widths],
            compiler_params=pltpu.CompilerParams(vmem_limit_bytes=16 * 1024 * 1024),
            cost_estimate=QUICK,
            name="place",
        )(targets, *self.values())


def tn(a, b):
    return lax.dot_general(a, b, (((0,), (0,)), ((), ())), preferred_element_type=f32)


def after(value, *others):
    return lax.optimization_barrier((value,) + others)[0]


def pieces_of(side, seq_first):
    dp, seq = lax.axis_size("dp"), lax.axis_size("seq")
    tokens, total = side.shape
    if seq_first:
        pieces = side.reshape(tokens, dp // 2, 2, seq // 2, 2, -1).transpose(2, 0, 4, 1, 3, 5)
    else:
        pieces = side.reshape(tokens, dp // 2, 2, -1).transpose(2, 0, 1, 3)
    return pieces.reshape(2, tokens, total // 2)


class Reduce:
    def __init__(self, pieces, cols_side, seq_first, product=None):
        self.pieces, self.cols_side, self.seq_first, self.product = pieces, cols_side, seq_first, product
        self.half = product.shape[0] // 4 if pieces is None else pieces.shape[2] // 2
        self.own = self.half * 4 // (lax.axis_size("dp") * lax.axis_size("seq"))
        self.core, self.height = digits_of("dp")[-1], digits_of("dp")[0]
        self.fast, self.far = digits_of("seq")[-1], digits_of("seq")[:-1]
        self.first = self.fast if seq_first else self.height
        self.c, self.mine = digit_index(self.core), digit_index(self.first)

    def term(self, core_index, index, others):
        if self.pieces is None:
            parts = pick(after(self.product, *others).reshape(2, 2, self.half, -1), core_index, 1)
            return (parts.reshape(2 * self.half, -1) if index is None else pick(parts, index, 0)).astype(f32)
        side = pick(after(self.pieces, *others), core_index, 0)
        if index is not None:
            side = lax.dynamic_slice_in_dim(side, index * self.half, self.half, 1)
        return tn(side, self.cols_side)

    def cross(self, *others):
        term = self.term(1 - self.c, None, others).astype(bf16)
        self.got = swap(term, self.core)
        return term

    def got_part(self, index):
        return lax.dynamic_slice_in_dim(self.got, index * self.half, self.half, 0).astype(f32)

    def send(self, *others):
        away = (self.term(self.c, 1 - self.mine, others) + self.got_part(1 - self.mine)).astype(bf16)
        self.away = swap(away, self.first)
        return away

    def keep(self, *others):
        total = self.term(self.c, self.mine, others) + self.got_part(self.mine) + self.away.astype(f32)
        self.total = total.astype(bf16)
        return self.total

    def second(self, *others):
        cols = self.cols_side.shape[1]
        total = after(self.total, *others)
        if self.seq_first:
            self.total = scatter_digit(total.reshape(2, -1, cols), self.height, 0, bf16)
        else:
            self.total = scatter_digit(total.reshape(-1, 2, self.own, cols), self.fast, 1, bf16)
        return self.total


class Finish:
    def __init__(self, reduces, *others):
        self.reduces, self.far = reduces, reduces[0].far
        self.count = 1 << len(self.far)
        self.unit = D // (lax.axis_size("dp") * lax.axis_size("seq"))
        totals = [after(r.total, *others).reshape(self.count, self.unit, -1) for r in reduces]
        self.widths = [t.shape[2] for t in totals]
        self.total = jnp.concatenate(totals, axis=2)

    def step(self, n, *others, hold=()):
        total = after(self.total, *others).reshape(-1, 2, self.unit, sum(self.widths))
        self.total = scatter_digit(total, self.far[-1 - n], 1, f32 if n == len(self.far) - 1 else bf16, hold)
        return self.total

    def results(self):
        left = 0
        results = []
        for r, width in zip(self.reduces, self.widths):
            results.append(self.total[0, :, left : left + width].reshape(r.own, -1))
            left += width
        return results


def dot_nt(a, b):
    return lax.dot_general(a, b, (((1,), (1,)), ((), ())), preferred_element_type=f32)


def dot_tn(a, b):
    return lax.dot_general(a, b, (((0,), (0,)), ((), ())), preferred_element_type=f32)


def dot_nn(a, b):
    return lax.dot_general(a, b, (((1,), (0,)), ((), ())), preferred_element_type=f32)


def tile_of(ref, index):
    per = TILE // ref.shape[1]
    return ref[pl.ds(index * per, per)].reshape(TILE, HD)


def mask_of(i, j, lo):
    key = j * TILE + lax.broadcasted_iota(jnp.int32, (TILE, TILE), 0)
    query = i * TILE + lax.broadcasted_iota(jnp.int32, (TILE, TILE), 1)
    return (key >= lo) & (key <= query)


def forward_kernel(bounds, q_ref, k_ref, v_ref, lo_ref, o_ref, lse_ref, acc):
    pair, i = pl.program_id(0), pl.program_id(1)
    q = q_ref[...].reshape(TILE, HD)
    lo = lo_ref[...]
    factor = SCALE * LOG2E

    def step(j, carry, masked):
        m, l = carry
        s = dot_nt(tile_of(k_ref, j), q) * factor
        if masked:
            s = jnp.where(mask_of(i, j, lo), s, MASKED)
        new = jnp.maximum(m, jnp.max(s, axis=0, keepdims=True))
        p = jnp.exp2(s - new)
        old = jnp.exp2(m - new)
        acc[...] = acc[...] * old + dot_tn(tile_of(v_ref, j), p.astype(bf16))
        return new, l * old + jnp.sum(p, axis=0, keepdims=True)

    acc[...] = jnp.zeros_like(acc)
    carry = (jnp.full((1, TILE), MASKED, f32), jnp.zeros((1, TILE), f32))
    start = bounds[pair, 0, i]
    middle = bounds[pair, 1, i]
    carry = lax.fori_loop(start, middle, lambda j, c: step(j, c, True), carry)
    carry = lax.fori_loop(middle, i, lambda j, c: step(j, c, False), carry)
    m, l = step(i, carry, True)
    o_ref[...] = (acc[...] / l).T.astype(bf16).reshape(o_ref.shape)
    lse_ref[...] = m + jnp.log2(l)


def attend(qkv, bounds, low):
    seq, pairs, rows, _ = qkv.shape
    length = seq * rows
    blocks, per = length // TILE, TILE // rows
    whole = lambda part: pl.BlockSpec((seq, None, rows, HD), lambda p, i, b: (0, p, 0, part))
    line = pl.BlockSpec((None, 1, TILE), lambda p, i, b: (p, 0, i))
    block = pl.BlockSpec((per, None, rows, HD), lambda p, i, b: (i, p, 0, 0))
    return pl.pallas_call(
        forward_kernel,
        grid_spec=pltpu.PrefetchScalarGridSpec(
            num_scalar_prefetch=1,
            grid=(pairs, blocks),
            in_specs=[block, whole(1), whole(2), line],
            out_specs=[block, line],
            scratch_shapes=[pltpu.VMEM((HD, TILE), f32)],
        ),
        out_shape=[
            jax.ShapeDtypeStruct((seq, pairs, rows, HD), bf16),
            jax.ShapeDtypeStruct((pairs, 1, length), f32),
        ],
        compiler_params=pltpu.CompilerParams(vmem_limit_bytes=32 * 1024 * 1024),
        cost_estimate=QUICK,
        name="attend",
    )(bounds, qkv, qkv, qkv, low)


def backward_kernel(pair, bounds, q_ref, k_ref, v_ref, do_ref, o_ref, lse_ref, lo_ref, out_ref, dq, dk, dv, delta):
    j = pl.program_id(0)
    k = k_ref[...].reshape(TILE, HD)
    v = v_ref[...].reshape(TILE, HD)
    factor = SCALE * LOG2E

    def step(i, masked):
        rows = pl.ds(pl.multiple_of(i * TILE, TILE), TILE)
        q = tile_of(q_ref, i)
        do = tile_of(do_ref, i)
        s = dot_nt(k, q) * factor
        p = jnp.exp2(s - lse_ref[:, rows])
        if masked:
            p = jnp.where(mask_of(i, j, lo_ref[:, rows]), p, 0.0)
        dp = dot_nt(v, do)
        ds = (p * (dp - delta[:, rows])).astype(bf16)
        dv[...] += dot_nn(p.astype(bf16), do)
        dk[...] += dot_nn(ds, q)
        dq[rows, :] += dot_tn(ds, k)

    @pl.when(j == 0)
    def _():
        dq[...] = jnp.zeros_like(dq)

        @pl.loop(0, pl.num_programs(0))
        def _(i):
            rows = pl.ds(pl.multiple_of(i * TILE, TILE), TILE)
            product = tile_of(do_ref, i).astype(f32) * tile_of(o_ref, i).astype(f32)
            delta[:, rows] = jnp.sum(product.T, axis=0, keepdims=True)

    dk[...] = jnp.zeros_like(dk)
    dv[...] = jnp.zeros_like(dv)
    step(j, True)
    middle = bounds[pair, 2, j]
    end = bounds[pair, 3, j]

    @pl.loop(j + 1, middle)
    def _(i):
        step(i, False)

    @pl.loop(middle, end)
    def _(i):
        step(i, True)

    own = pl.ds(pl.multiple_of(j * TILE, TILE), TILE)
    shape = out_ref.shape[:-1] + (HD,)
    out_ref[:, :, :HD] = (dq[own, :] * SCALE).astype(bf16).reshape(shape)
    out_ref[:, :, HD : 2 * HD] = (dk[...] * SCALE).astype(bf16).reshape(shape)
    out_ref[:, :, 2 * HD :] = dv[...].astype(bf16).reshape(shape)


def attend_back(pair, qkv, grad, mixed, lse, bounds, low):
    seq, _, rows, _ = qkv.shape
    length = seq * rows
    blocks, per = length // TILE, TILE // rows
    whole = pl.BlockSpec((seq, None, rows, HD), lambda j, b: (0, pair, 0, 0))
    line = pl.BlockSpec((None, 1, length), lambda j, b: (pair, 0, 0))
    block = lambda part: pl.BlockSpec((per, None, rows, HD), lambda j, b: (j, pair, 0, part))
    return pl.pallas_call(
        functools.partial(backward_kernel, pair),
        grid_spec=pltpu.PrefetchScalarGridSpec(
            num_scalar_prefetch=1,
            grid=(blocks,),
            in_specs=[whole, block(1), block(2), whole, whole, line, line],
            out_specs=pl.BlockSpec((per, None, rows, 3 * HD), lambda j, b: (j, 0, 0, 0)),
            scratch_shapes=[
                pltpu.VMEM((length, HD), f32),
                pltpu.VMEM((TILE, HD), f32),
                pltpu.VMEM((TILE, HD), f32),
                pltpu.VMEM((1, length), f32),
            ],
        ),
        out_shape=jax.ShapeDtypeStruct((seq, 1, rows, 3 * HD), bf16),
        compiler_params=pltpu.CompilerParams(vmem_limit_bytes=40 * 1024 * 1024),
        cost_estimate=QUICK,
        name="attend_back",
    )(bounds, qkv, qkv, qkv, grad, mixed, lse, low)


def key_bounds(segments):
    length = segments.shape[0]
    blocks = length // TILE
    place = jnp.arange(length, dtype=jnp.int32)
    start = jnp.zeros_like(place)
    for value in range(1, 4):
        earlier = jnp.sum(segments < value, dtype=jnp.int32)
        start = jnp.where(segments == value, earlier, start)
    low = jnp.maximum(start, place - (WINDOW - 1))
    index = jnp.arange(blocks, dtype=jnp.int32)
    first = low[::TILE]
    last = low[TILE - 1 :: TILE]
    begin = first // TILE
    middle = jnp.clip((last + TILE - 1) // TILE, begin, index)
    full = (last[None, :] <= index[:, None] * TILE) & (index[None, :] > index[:, None])
    some = (first[None, :] < (index[:, None] + 1) * TILE) & (index[None, :] > index[:, None])
    back_middle = index + 1 + jnp.sum(full, axis=1, dtype=jnp.int32)
    back_end = index + 1 + jnp.sum(some, axis=1, dtype=jnp.int32)
    return low[None], jnp.stack([begin, middle, back_middle, back_end])


def to_heads(rows, micros):
    seq = lax.axis_size("seq")
    count, width = rows.shape[0] // micros, rows.shape[1] // H
    split = rows.reshape(micros, count, H, width).transpose(2, 0, 1, 3)
    split = split.reshape(seq, H * micros // seq, count, width)
    return lax.all_to_all(split, "seq", 0, 0, tiled=True)


def to_rows(whole):
    return lax.all_to_all(whole, "seq", 0, 0, tiled=True)


def rows_of(got, micros):
    count, width = got.shape[2], got.shape[3]
    return got.reshape(H, micros, count, width).transpose(1, 2, 0, 3).reshape(micros * count, H * width)


def norm_scale(values):
    return lax.rsqrt(jnp.mean(values * values, axis=-1, keepdims=True) + EPSILON)


def norm_backward(grad_in, values, row_scale, gain):
    normed = values * row_scale
    gain_grad = jnp.sum(grad_in * normed, axis=0)
    scaled = grad_in * gain
    inner = jnp.mean(scaled * normed, axis=-1, keepdims=True)
    return row_scale * (scaled - normed * inner), gain_grad


def nt(a, b):
    return jnp.einsum("re,de->rd", a, b, preferred_element_type=f32)


def shards(tokens, segment_ids, w_qkv, w_out, w_gate_up, w_down, gain_attn, gain_mlp, cotangent):
    rows = tokens.shape[2]
    seq = lax.axis_size("seq")
    gather = lambda w: lax.all_gather(w, ("dp", "seq"), axis=0, tiled=True)
    groups = MB if H % seq == 0 else 1
    micros = MB // groups
    pairs = H * micros // seq
    size = micros * rows
    of = lambda array, g: array[g * size : (g + 1) * size]

    x = tokens.reshape(MB * rows, D).astype(f32)
    cot = cotangent.reshape(MB * rows, D)
    bounds, low = [], []
    for g in range(groups):
        made = []
        for k in range(pairs):
            micro = g if micros == 1 else lax.rem(lax.axis_index("seq") * pairs + k, micros)
            made.append(key_bounds(segment_ids[g, 0] if micros == 1 else pick(segment_ids[:, 0], micro, 0)))
        low.append(jnp.stack([m[0] for m in made]))
        bounds.append(jnp.stack([m[1] for m in made]))

    order_qkv = w_qkv.reshape(-1, 3, H, HD).transpose(0, 2, 1, 3).reshape(w_qkv.shape)
    full_qkv = gather(order_qkv)
    all_gains = gather_small(jnp.stack([gain_attn, gain_mlp]))
    gains = all_gains.astype(f32)
    gain_a, gain_m = gains[0], gains[1]
    scale_a = norm_scale(x)
    h_attn = (x * scale_a * gain_a).astype(bf16)
    soon = Gather([w_gate_up[:, :FF], w_out], False)
    later = Gather([w_gate_up[:, FF:], w_down.reshape(w_qkv.shape[0], -1)], True)
    far = len(soon.far)

    soon.wait(all_gains, h_attn)
    soon.far_step(0)
    for n in range(1, far):
        later.wait(*soon.values())
        soon.far_step(n)
        later.far_step(n - 1)
    ready = soon.values() + later.values()
    soon.wait(*ready)
    soon.near_step(0)
    later.wait(*ready)
    later.far_step(far - 1)
    later.near_step(0)
    h_kept = after(h_attn, *later.values(), *soon.values())
    saved, attended, arrived = [], [], []

    def project(g, *others):
        qkv_rows = jnp.dot(of(after(h_kept, *others), g), full_qkv, preferred_element_type=f32).astype(bf16)
        arrived.append(to_heads(qkv_rows, micros))

    def attention(g, others):
        qkv = after(arrived[g], *others)
        mixed, lse = attend(qkv, bounds[g], low[g])
        saved.append((qkv, mixed, lse))
        return to_rows(mixed)

    project(0)
    ready = soon.values() + later.values()
    for w in (soon, later):
        w.wait(*ready)
        w.near_step(1)
    back_rows = attention(0, soon.values() + later.values())
    soon.near_step(2)
    later.near_step(2)
    full_gate, full_out = soon.finish()
    full_up, flat_down = later.finish()
    attended.append(rows_of(after(back_rows, full_gate, full_out, full_up, flat_down), micros))
    if groups > 1:
        project(1, attended[0])

    parts = []
    grads = []
    rows_grad = []
    mark = ()

    def back_of(g, *others):
        qkv, mixed, lse = saved[g]
        pieces = []
        for k in range(pairs):
            back = attend_back(k, after(qkv, *others), grads[g], mixed, lse, bounds[g], low[g])
            others = (back,)
            pieces.append(to_rows(back))
        rows_grad.append(pieces)
        return back

    for g in range(groups):
        final = g == groups - 1
        mid = of(x, g) + jnp.dot(after(attended[g], *mark), full_out, preferred_element_type=f32)
        scale_m = norm_scale(mid)
        h_mlp = (mid * scale_m * gain_m).astype(bf16)
        gate = jnp.dot(h_mlp, full_gate, preferred_element_type=f32)
        up = jnp.dot(after(h_mlp, *mark), full_up, preferred_element_type=f32)
        sig = jax.nn.sigmoid(gate)
        act = (gate * sig * up).astype(bf16)
        parts.append([mid, scale_m, h_mlp, act])
        mark = (act,)
        if g == 0:
            full_down = after(flat_down, act).reshape(FF, D)
        if final:
            acts = jnp.concatenate([p[3] for p in parts], axis=0)
            sides = jnp.concatenate([p[2] for p in parts], axis=0)
            down = Reduce(None, cot, False, product=tn(after(acts, *mark, *grads), cot).astype(bf16))
            mark = (down.cross(),)
        if g:
            mark = (back_of(g - 1, *mark),)
        if final:
            mark = (down.send(*mark),)
        if g:
            mark = mark + (rows_grad[-1][0],)
        cot_part = of(cot, g)
        grad_act = nt(after(cot_part, *mark), full_down)
        grad_gate = (grad_act * up * sig * (1.0 + gate * (1.0 - sig))).astype(bf16)
        grad_up = (grad_act * (gate * sig)).astype(bf16)
        parts[g] += [grad_gate, grad_up]
        mark = (grad_gate, grad_up)
        if not final:
            back_rows = attention(g + 1, mark)
            mark = (saved[-1][1],)
        if final:
            gate_r = Reduce(pieces_of(sides, False), jnp.concatenate([p[4] for p in parts], axis=0), False)
            up_r = Reduce(pieces_of(sides, True), jnp.concatenate([p[5] for p in parts], axis=0), True)
            mark = (up_r.cross(*mark),)
            mark = (gate_r.cross(*mark),)
        if final:
            mark = (up_r.send(*mark, *[r for pieces in rows_grad for r in pieces]),)
        half_grad = nt(after(grad_gate, *mark), full_gate)
        mark = (half_grad,)
        grad_h_mlp = half_grad + nt(after(grad_up, *mark), full_up)
        grad_mid_norm, gain_part = norm_backward(grad_h_mlp, mid, scale_m, gain_m)
        grad_mid = cot_part.astype(f32) + grad_mid_norm
        grad_branch = grad_mid.astype(bf16)
        arrivals = [r for pieces in rows_grad for r in pieces]
        grad_rows = nt(after(grad_branch, *arrivals), full_out).astype(bf16)
        if not final:
            attended.append(rows_of(after(back_rows, grad_rows), micros))
        grads.append(to_heads(grad_rows, micros))
        parts[g] += [grad_mid, grad_branch, gain_part]
        mark = (grad_rows,)

    attended_all = jnp.concatenate(attended, axis=0)
    out_r = Reduce(pieces_of(attended_all, False), jnp.concatenate([p[7] for p in parts], axis=0), False)
    early = [down, up_r, gate_r, out_r]
    mark = (gate_r.send(*mark),)
    mark = (out_r.cross(*mark),)
    mark = (down.keep(*mark),)
    down.second(grads[-1])
    mark = (back_of(groups - 1, *mark),)
    mark = (up_r.keep(*mark),)
    up_r.second()
    mark = (out_r.send(*mark), rows_grad[-1][0])
    for r in (gate_r, out_r):
        mark = (r.keep(*mark),)
        r.second()
    layer_outs, grad_qkv, grad_tokens, gain_a_parts = [], [], [], []

    def finish_tokens(g, *others):
        grad_h_attn = nt(after(grad_qkv[g], *others), full_qkv)
        grad_norm, gain_part = norm_backward(grad_h_attn, of(x, g), of(scale_a, g), gain_a)
        grad_tokens.append(parts[g][6] + grad_norm)
        gain_a_parts.append(gain_part)
        return grad_tokens[-1]

    for g in range(groups):
        act = after(parts[g][3], *mark)
        layer_outs.append((parts[g][0] + jnp.dot(act, full_down, preferred_element_type=f32)).astype(bf16))
        mark = (layer_outs[-1],)
    mark = mark + tuple(rows_grad[-1]) + tuple(r.total for r in early)
    first = Finish(early, *mark)
    mark = mark + (first.total,)
    h_sides = [pieces_of(h_kept, False), pieces_of(h_kept, True)]
    for g in range(groups - 1):
        grad_qkv.append(rows_of(jnp.concatenate(rows_grad[g], axis=1), micros))
    grad_qkv.append(rows_of(jnp.concatenate([after(r, *mark) for r in rows_grad[-1]], axis=1), micros))
    last_rows = grad_qkv[-1]
    all_qkv = jnp.concatenate(grad_qkv, axis=0)
    half = 3 * D // 2
    late = [Reduce(h_sides[0], all_qkv[:, :half], False), Reduce(h_sides[1], all_qkv[:, half:], True)]
    for r in late:
        mark = (r.cross(*mark),)
    for r in late:
        mark = (r.send(*mark),)
    first.step(0, hold=mark)
    for g in range(groups - 1):
        mark = (finish_tokens(g, *mark),)
    mark = mark + (first.total,)
    g = groups - 1
    grad_h_attn = nt(after(last_rows, *mark), full_qkv)
    grad_norm, gain_part = norm_backward(grad_h_attn, of(x, g), of(scale_a, g), gain_a)
    grad_tokens.append(parts[g][6] + grad_norm)
    gain_a_parts.append(gain_part)
    mark = (grad_tokens[-1], first.total)
    for r in late:
        mark = (r.keep(*mark),)
    for r in late:
        r.second(*mark)
    gain_sums = ScatterSmall(jnp.stack([sum(gain_a_parts), sum(p[8] for p in parts)]))
    second = Finish(late)
    for n in range(far):
        if n:
            first.step(n, hold=mark)
        gain_sums.step(digits_of("seq")[-2 - n], second.total)
        second.step(n)
    gain_grads = gain_sums.terms
    down_grad, up_grad, gate_grad, out_grad = first.results()
    qkv_grad = jnp.concatenate(second.results(), axis=1).reshape(-1, H, 3, HD).transpose(0, 2, 1, 3)
    join = lambda arrays: jnp.concatenate(arrays, axis=0).reshape(MB, 1, rows, D)

    return (
        join(layer_outs),
        join(grad_tokens),
        qkv_grad.reshape(-1, 3 * D),
        out_grad,
        jnp.concatenate([gate_grad, up_grad], axis=1),
        down_grad,
        gain_grads[0],
        gain_grads[1],
    )


def solution(mesh):
    by_rows = P(("dp", "seq"), None)
    by_tokens = P(None, "dp", "seq", None)
    vector = P(("dp", "seq"))
    return jax.shard_map(
        shards,
        mesh=mesh,
        in_specs=(by_tokens, P(None, "dp", None), by_rows, by_rows, by_rows, by_rows, vector, vector, by_tokens),
        out_specs=(by_tokens, by_tokens, by_rows, by_rows, by_rows, by_rows, vector, vector),
        check_vma=False,
    )
```
